128 devices in a mesh: dp: 2 (over z_hi), expert: 64 (over y, z_lo, x, core).
Axes of the slice: x: 4, y: 4, z: 4 (z_hi: 2, z_lo: 2; z = z_hi * 2 + z_lo), core: 2. Of those that a mesh axis runs over, the one named last changes fastest.
Arguments:
- latent: bfloat16 [16384, 1024], P(('dp', 'expert')), may hold values from -6 to 6
- routes: int32 [16384, 8], P(('dp', 'expert')), may hold values from 0 to 63, all different within a row; in each aligned block of 128 rows (0 to 127, 128 to 255, ...) at most 20 rows name the same one
- gates: float32 [16384, 8], P(('dp', 'expert')), may hold values from 0.05 to 0.5
- grad_out: bfloat16 [16384, 4096], P(('dp', 'expert')), may hold values from -6 to 6
- w_out_t: bfloat16 [4096, 1024], P('expert'), may hold values from -0.1875 to 0.1875
- expert_up: bfloat16 [64, 1024, 2048], P('expert'), may hold values from -0.1875 to 0.1875
- expert_down: bfloat16 [64, 2048, 1024], P('expert'), may hold values from -0.125 to 0.125
Outputs:
- mixed: bfloat16 [16384, 4096], P(('dp', 'expert'))
- grad_latent: bfloat16 [16384, 1024], P(('dp', 'expert'))
- grad_w_out: float32 [4096, 1024], P('expert')
The draws below stay inside these ranges and needn't reach their ends.
Inputs may be any that keep to these rules, and one draw needn't show every extreme that they name: `routes`: within the 128 rows of one device each row names 8 different experts, and no expert is named by more than 20 of those rows; some expert is named by exactly 20 rows of some device.
All inputs are finite; a program needn't handle non-finite values.
Results may differ from the reference program's by a relative error of at most 0.02.
Values may be sent and summed in bfloat16 or wider, within the bound.
A program may use at most 128 MiB of HBM per device.

```python
import math
import jax
import jax.numpy as jnp
import numpy as np
from jax import lax

D = 4096
L = 1024
H = 2048
K = 8
TOK_DEV = 128
EXPERTS = 64
TOKENS = 16384
CAP = 20
N_DP = 2
N_EXPERT = 64


def block_levels(stream_key, shape, shards, least, high):
    loudness = 1.0
    for dim, blocks in shards:
        heights = jax.random.uniform(jax.random.fold_in(jax.random.fold_in(stream_key, 6), dim), (blocks,), jnp.float32, least / len(shards), high / len(shards))
        loudness = loudness * jnp.repeat(jnp.exp(heights), shape[dim] // blocks).reshape((-1,) + (1,) * (len(shape) - 1 - dim))
    return loudness


def assign_block(key, own, number, rows, number_of, top, limit, slope):
    ranking = jax.random.permutation(key, number_of)
    heavy_load, usual = load_shares(number_of, rows * top, limit, slope, True), load_shares(number_of, rows * top, limit, slope, False)
    places = jnp.arange(number_of)

    def named(tallies, turn):
        used = int((tallies > 0).sum())
        fixed = max(1, used // 4)
        shifted = fixed + (places - fixed + turn * (used - fixed)) % max(1, number_of - fixed)
        return jnp.zeros((number_of,), jnp.int32).at[ranking[jnp.where(places < fixed, places, shifted)]].set(jnp.asarray(tallies, jnp.int32))

    tallies = jnp.where(number % 4 == 0, named(heavy_load, number // 4), named(usual, number - number // 4 - 1))
    mixed = jax.random.permutation(jax.random.fold_in(own, 3), number_of)
    donor, receiver = mixed[0:number_of // 2 * 2:2], mixed[1:number_of // 2 * 2:2]
    margin = jnp.minimum(tallies[donor] - 1, limit - tallies[receiver]) // 2
    margin = jnp.where((donor == ranking[0]) | (receiver == ranking[0]) | (tallies[receiver] == 0), 0, jnp.maximum(margin, 0))
    shifted = jax.random.randint(jax.random.fold_in(own, 4), (number_of // 2,), 0, 1 << 20) % (margin + 1)
    tallies = tallies.at[donor].add(-shifted).at[receiver].add(shifted)
    labels = jnp.searchsorted(jnp.cumsum(tallies), jnp.arange(rows * top), side="right").astype(jnp.int32)
    table = labels.reshape(top, rows).T
    table = table[jax.random.permutation(jax.random.fold_in(own, 1), rows)]
    turn = jax.random.randint(jax.random.fold_in(own, 2), (rows, 1), 0, top)
    return jnp.take_along_axis(table, (jnp.arange(top)[None, :] + turn) % top, axis=1)


def load_shares(amount, total, most, skew, full):
    weights = [(1 << 20) // math.isqrt(rank ** skew) + 1 for rank in range(1, amount + 1)]
    largest = most if full else min(most, max(-(-total // amount), total * weights[0] // sum(weights)))
    least = 1 if total - largest >= amount - 1 else 0
    counts, rest = [largest] + [least] * (amount - 1), total - largest - least * (amount - 1)
    while rest > 0:
        candidates = [i for i in range(1, amount) if counts[i] < largest] or [i for i in range(1, amount) if counts[i] < most]
        pool, left = sum([weights[i] for i in candidates]), rest
        for i in candidates:
            extra = min(most - counts[i], max(1, left * weights[i] // pool), rest)
            counts[i] = counts[i] + extra
            rest = rest - extra
    return np.array(counts)


def normal_values(stream_key, dims, scale, limit, cuts=(), held_as=jnp.bfloat16):
    level = block_levels(stream_key, dims, cuts, -0.22, 0.18) if cuts else 1.0
    drawn = jax.random.normal(stream_key, dims, jnp.float32) * scale * level
    return jnp.minimum(jnp.maximum(drawn, -limit), limit).astype(held_as)


def setup_inputs(seed: int = 0) -> dict:
    key_list = jax.random.split(jax.random.key(seed), 8)
    latent = normal_values(key_list[0], (TOKENS, L), 1.0, 6.0, ((0, 128),))
    routes_keys = jax.random.split(jax.random.fold_in(key_list[1], 1), TOKENS // TOK_DEV)
    routes_turns = jax.random.permutation(jax.random.fold_in(key_list[1], 3), TOKENS // TOK_DEV)
    routes = jax.vmap(lambda own, number: assign_block(jax.random.fold_in(key_list[1], 2), own, number, TOK_DEV, EXPERTS, K, CAP, 1))(routes_keys, routes_turns).reshape((TOKENS, K))
    gates = jnp.clip(0.05 + 0.45 * jax.random.uniform(key_list[2], (TOKENS, K), jnp.float32) ** block_levels(key_list[2], (TOKENS, K), ((0, 128),), -0.2, 0.2), 0.05, 0.5)
    grad_out = normal_values(key_list[3], (TOKENS, D), 1.0, 6.0, ((0, 128),))
    w_out_t = normal_values(key_list[4], (D, L), L ** -0.5, 0.1875, ((0, 64),))
    expert_up = normal_values(key_list[5], (EXPERTS, L, H), L ** -0.5, 0.1875, ((0, 64),))
    expert_down = normal_values(key_list[6], (EXPERTS, H, L), H ** -0.5, 0.125, ((0, 64),))
    return {"latent": latent, "routes": routes, "gates": gates, "grad_out": grad_out, "w_out_t": w_out_t, "expert_up": expert_up, "expert_down": expert_down}


def expert_forward(rows, up_weight, down_weight):
    pre = jnp.dot(rows.astype(jnp.float32), up_weight.astype(jnp.float32), preferred_element_type=jnp.float32)
    act = (jnp.maximum(pre, 0.0) ** 2).astype(jnp.bfloat16)
    return jnp.dot(act.astype(jnp.float32), down_weight.astype(jnp.float32), preferred_element_type=jnp.float32).astype(jnp.bfloat16)


def expert_backward(rows, grads, up_weight, down_weight):
    pre = jnp.dot(rows.astype(jnp.float32), up_weight.astype(jnp.float32), preferred_element_type=jnp.float32)
    grad_act = jnp.dot(grads.astype(jnp.float32), down_weight.astype(jnp.float32).T, preferred_element_type=jnp.float32)
    grad_pre = (grad_act * 2.0 * jnp.maximum(pre, 0.0)).astype(jnp.bfloat16)
    return jnp.dot(grad_pre.astype(jnp.float32), up_weight.astype(jnp.float32).T, preferred_element_type=jnp.float32).astype(jnp.bfloat16)


def reference(latent, routes, gates, grad_out, w_out_t, expert_up, expert_down):
    blocks = N_DP * N_EXPERT
    width = latent.shape[1]
    flat = routes.reshape(blocks, TOK_DEV * K)
    onehot = (flat[:, :, None] == jnp.arange(EXPERTS, dtype=jnp.int32)[None, None, :]).astype(jnp.int32)
    before = jnp.cumsum(onehot, axis=1) - onehot
    slots = jnp.sum(before * onehot, axis=2).astype(jnp.int32)
    owner = jnp.arange(blocks, dtype=jnp.int32)[:, None]
    target = ((flat * blocks + owner) * CAP + slots).reshape(-1).astype(jnp.int32)
    repeated = jnp.repeat(latent, K, axis=0)
    buffer = jnp.zeros((EXPERTS * blocks * CAP, width), jnp.bfloat16).at[target].set(repeated)
    buffer = buffer.reshape(EXPERTS, blocks * CAP, width)
    outputs = lax.map(lambda item: expert_forward(item[0], item[1], item[2]), (buffer, expert_up, expert_down))
    picked = outputs.reshape(-1, width)[target].astype(jnp.float32).reshape(TOKENS, K, width)
    combined = jnp.sum(picked * gates[:, :, None], axis=1).astype(jnp.bfloat16)
    mixed = jnp.dot(combined, w_out_t.T, preferred_element_type=jnp.float32).astype(jnp.bfloat16)
    grad_combined = jnp.dot(grad_out, w_out_t, preferred_element_type=jnp.float32).astype(jnp.bfloat16)
    grad_w_out = jnp.dot(grad_out.T, combined, preferred_element_type=jnp.float32)
    scaled = (jnp.repeat(grad_combined, K, axis=0).astype(jnp.float32) * gates.reshape(-1, 1)).astype(jnp.bfloat16)
    grad_buffer = jnp.zeros((EXPERTS * blocks * CAP, width), jnp.bfloat16).at[target].set(scaled)
    grad_buffer = grad_buffer.reshape(EXPERTS, blocks * CAP, width)
    grad_rows = lax.map(lambda item: expert_backward(item[0], item[1], item[2], item[3]), (buffer, grad_buffer, expert_up, expert_down))
    gathered = grad_rows.reshape(-1, width)[target].astype(jnp.float32).reshape(TOKENS, K, width)
    grad_latent = jnp.sum(gathered, axis=1).astype(jnp.bfloat16)
    return mixed, grad_latent, grad_w_out
```

```python
import functools

import jax
import jax.numpy as jnp
from jax import lax
from jax.experimental import pallas as pl
from jax.experimental.pallas import tpu as pltpu
from jax.sharding import PartitionSpec as P

BF = jnp.bfloat16
F32 = jnp.float32
MESH = pl.DeviceIdType.MESH
STRIDE = 11
CHUNKS = 4
PER = 16
MAIN = 256
EXTRA = 64
ROWS = 320


def iota(shape, dim):
    return lax.broadcasted_iota(jnp.int32, shape, dim)


def dot(a, b, ca=1, cb=0):
    return lax.dot_general(a, b, (((ca,), (cb,)), ((), ())), preferred_element_type=F32)


def index_of(y, z, x, c):
    return ((y * 2 + z) * 4 + x) * 2 + c


def kernel(
    latent, routes, gates, w_own, grad_out, up_hbm, down_hbm,
    mixed, grad_latent, grad_w,
    s1, r1, o1, b1, s2, r2, o2, b2, up, down, relu, xc, acc, extra,
    go, wj, pgs, pgr, cb, mps, gwp, gwr, dps, dpr,
    sel, selt, p_send, pg_send, p_back, pg_back,
    a2a_ss, a2a_rs, w_ss, w_rs, go_ss, go_rs, pg_ss, pg_rs, cb_ss, cb_rs, mx_ss, mx_rs,
    gw_ss, gw_rs, dp_ss, dp_rs, loc,
):
    dp = lax.axis_index("dp")
    me = lax.axis_index("expert")
    y, z, x, c = me // 16, (me // 8) % 2, (me // 2) % 4, me % 2
    mine = z * 2 + c

    def partner(k, sign):
        off = (STRIDE * k) % 64
        oy, oz, ox, oc = off // 16, (off // 8) % 2, (off // 2) % 4, off % 2
        return index_of((y + sign * oy + 4) % 4, (z + oz) % 2, (x + sign * ox + 4) % 4, (c + oc) % 2)

    def member(d):
        m = (mine + d) % 4
        return m, index_of(y, m // 2, x, m % 2)

    def remote(src, dst, ss, rs, dev):
        return pltpu.make_async_remote_copy(src, dst, ss, rs, device_id=(dp, dev), device_id_type=MESH)

    barrier = pltpu.get_barrier_semaphore()

    def greet(k, carry):
        pl.semaphore_signal(barrier, inc=1, device_id=(dp, partner(k, 1)), device_id_type=MESH)
        return carry

    lax.fori_loop(1, 64, greet, 0)
    pl.semaphore_signal(barrier, inc=1, device_id=(1 - dp, me), device_id_type=MESH)
    up_copy = pltpu.make_async_copy(up_hbm.at[0], up, loc.at[0])
    down_copy = pltpu.make_async_copy(down_hbm.at[0], down, loc.at[1])
    up_copy.start()
    down_copy.start()

    r = routes[...]
    g = gates[...]
    lane = iota((128, 128), 1)
    hot = jnp.zeros((128, 128), F32)
    gate = jnp.zeros((128, 128), F32)
    for k in range(8):
        hit = r[:, k : k + 1] == lane
        hot = hot + jnp.where(hit, 1.0, 0.0)
        gate = gate + jnp.where(hit, g[:, k : k + 1], 0.0)
    lower = jnp.where(iota((128, 128), 0) > lane, 1.0, 0.0).astype(BF)
    count = dot(lower, hot.astype(BF))
    slot = jnp.where(hot > 0.5, count, 255.0)
    gate_hi = gate.astype(BF).astype(F32)
    gate_lo = (gate - gate_hi).astype(BF).astype(F32)

    def names(j):
        return jnp.where(j < 1024, j >> 4, (j - 1024) >> 2), jnp.where(j < 1024, j & 15, 16 + (j & 3))

    e_row, s_row = names(iota((1280, 128), 0))
    spread_t = jnp.where(e_row == iota((1280, 128), 1), 1.0, 0.0).astype(BF)
    hit_t = dot(spread_t, slot.T.astype(BF)) == s_row.astype(F32)
    p_send[...] = jnp.where(hit_t, 1.0, 0.0).astype(BF)
    pg_send[:, 0:128] = jnp.where(hit_t, dot(spread_t, gate_hi.T.astype(BF)), 0.0).astype(BF)
    pg_send[:, 128:256] = jnp.where(hit_t, dot(spread_t, gate_lo.T.astype(BF)), 0.0).astype(BF)
    e_col, s_col = names(iota((128, 1280), 1))
    spread = jnp.where(e_col == iota((128, 1280), 0), 1.0, 0.0).astype(BF)
    hit_b = dot(slot.astype(BF), spread) == s_col.astype(F32)
    p_back[...] = jnp.where(hit_b, 1.0, 0.0).astype(BF)
    pg_back[0:128, :] = jnp.where(hit_b, dot(gate_hi.astype(BF), spread), 0.0).astype(BF)
    pg_back[128:256, :] = jnp.where(hit_b, dot(gate_lo.astype(BF), spread), 0.0).astype(BF)
    i, j = iota((256, 256), 0), iota((256, 256), 1)
    sel[...] = jnp.where(((i & 63) >> 2) * 16 + (i >> 6) * 4 + (i & 3) == j, 1.0, 0.0).astype(BF)
    selt[...] = jnp.where(((j & 63) >> 2) * 16 + (j >> 6) * 4 + (j & 3) == i, 1.0, 0.0).astype(BF)

    def unpack(packed):
        rows = dot(sel[...], packed).astype(BF)
        return jnp.concatenate([rows[q * 64 : (q + 1) * 64] for q in range(4)], axis=1)

    def pack(rows):
        stacked = jnp.concatenate([rows[:, q * 256 : (q + 1) * 256] for q in range(4)], axis=0)
        return dot(selt[...], stacked).astype(BF)

    def main_rows(ci):
        return pl.ds(pl.multiple_of(ci * MAIN, MAIN), MAIN)

    def fill(pick, source, buffer):
        def body(ci, carry):
            buffer[main_rows(ci), 0:1024] = dot(pick[main_rows(ci), :], source).astype(BF)
            more = pick[pl.ds(pl.multiple_of(1024 + ci * EXTRA, EXTRA), EXTRA), :]
            buffer[main_rows(ci), 1024:1280] = pack(dot(more, source).astype(BF))
            return carry

        lax.fori_loop(0, CHUNKS, body, 0)

    def block(k):
        return pl.ds(pl.multiple_of(k * 16, 16), 16)

    def start_out(which, src, dst):
        def body(k, carry):
            to = partner(k, 1)
            remote(src.at[block(to)], dst.at[block(k)], a2a_ss.at[which], a2a_rs.at[which, k // PER], to).start()
            return carry

        lax.fori_loop(1, 64, body, 0)
        dst[0:16, :] = src[block(me), :]

    def start_back(which, src, dst, ci):
        def body(k, carry):
            to = partner(k, -1)
            remote(src.at[block(k)], dst.at[block(me)], a2a_ss.at[which], a2a_rs.at[which, k // PER], to).start()
            return carry

        lax.fori_loop(jnp.maximum(ci * PER, 1), ci * PER + PER, body, 0)

        @pl.when(ci == 0)
        def _():
            dst[block(me), :] = src[0:16, :]

    def arrived(which, ci, src, dst, first):
        rows = pl.ds(0, 240) if first else main_rows(ci)
        remote(src.at[rows], dst.at[rows], a2a_ss.at[which], a2a_rs.at[which, ci], me).wait_recv()

    def all_sent(which, src, dst):
        rows = pl.ds(0, 1008)
        remote(src.at[rows], dst.at[rows], a2a_ss.at[which], a2a_rs.at[which, 0], me).wait_send()

    fill(p_send, latent[...], s1)
    pl.semaphore_wait(barrier, 64)

    half = x // 2
    w_slot = y * 4 + (x % 2) * 2 + c

    def w_rows(s):
        return pl.ds(pl.multiple_of(s * 64, 64), 64)

    def w_copy(i):
        to = index_of((y + i // 4) % 4, z, (x + i % 4) % 4, half)
        return to, remote(w_own, wj.at[w_rows(w_slot)], w_ss.at[i], w_rs.at[w_slot], to)

    def w_start(i, carry):
        to, copy = w_copy(i)

        @pl.when(to != me)
        def _():
            copy.start()

        @pl.when(to == me)
        def _():
            wj[w_rows(w_slot), :] = w_own[...]

        return carry

    lax.fori_loop(0, 16, w_start, 0)

    def feats(m, part):
        return pl.ds(pl.multiple_of(part * 1024 + (m // 2) * 512 + (m % 2) * 256, 256), 256)

    def tokens(m):
        return pl.ds(pl.multiple_of(m * 128, 128), 128)

    own_go = []
    for part in range(4):
        cols = pl.ds(part * 256, 256)
        for d in range(1, 4):
            m, to = member(d)
            remote(grad_out.at[:, feats(m, part)], go.at[tokens(mine), cols], go_ss.at[d], go_rs.at[mine], to).start()
        copy = pltpu.make_async_copy(grad_out.at[:, feats(mine, part)], go.at[tokens(mine), cols], loc.at[2 + part])
        copy.start()
        own_go.append(copy)

    start_out(0, s1, r1)

    def w_wait(i, carry):
        fy, fx, fc = i // 4, half_of(i), i % 2
        src = index_of(fy, z, fx, fc)

        @pl.when(src != me)
        def _():
            remote(w_own, wj.at[w_rows(i)], w_ss.at[0], w_rs.at[i], me).wait_recv()

        return carry

    def half_of(i):
        return c * 2 + (i // 2) % 2

    lax.fori_loop(0, 16, w_wait, 0)
    for copy in own_go:
        copy.wait()
    for d in range(1, 4):
        m, _ = member(d)
        remote(go.at[tokens(m)], go.at[tokens(m)], go_ss.at[d], go_rs.at[m], me).wait_recv()

    def partial_gc(n, carry):
        cols = pl.ds(pl.multiple_of(n * 256, 256), 256)
        pgs[:, cols] = dot(go[...], wj[:, cols]).astype(BF)
        return carry

    lax.fori_loop(0, 4, partial_gc, 0)
    for d in range(1, 4):
        m, to = member(d)
        remote(pgs.at[tokens(m)], pgr.at[tokens(mine)], pg_ss.at[d], pg_rs.at[mine], to).start()
    pgr[tokens(mine), :] = pgs[tokens(mine), :]
    for d in range(1, 4):
        m, _ = member(d)
        remote(pgs.at[tokens(m)], pgr.at[tokens(m)], pg_ss.at[d], pg_rs.at[m], me).wait_recv()
    gc = sum(pgr[m * 128 : (m + 1) * 128, :].astype(F32) for m in range(4)).astype(BF)
    fill(pg_send, jnp.concatenate([gc, gc], axis=0), s2)
    start_out(2, s2, r2)

    up_copy.wait()
    down_copy.wait()

    def load(src, ci):
        xc[0:MAIN, :] = src[main_rows(ci), 0:1024]
        xc[MAIN:ROWS, :] = unpack(src[main_rows(ci), 1024:1280])

    def store(dst, ci):
        dst[main_rows(ci), 0:1024] = acc[0:MAIN, :].astype(BF)
        dst[main_rows(ci), 1024:1280] = pack(acc[MAIN:ROWS, :].astype(BF))

    def hidden(h):
        return pl.ds(pl.multiple_of(h * 512, 512), 512)

    def arrived_chunk(which, ci, src, dst):
        @pl.when(ci == 0)
        def _():
            arrived(which, 0, src, dst, True)

        @pl.when(ci > 0)
        def _():
            arrived(which, ci, src, dst, False)

    def forward(ci, carry):
        arrived_chunk(0, ci, s1, r1)
        load(r1, ci)
        acc[...] = jnp.zeros_like(acc)

        def step(h, inner):
            pos = jnp.maximum(dot(xc[...], up[:, hidden(h)]), 0.0)
            relu[ci, :, hidden(h)] = pos
            acc[...] += dot((pos * pos).astype(BF), down[hidden(h), :])
            return inner

        lax.fori_loop(0, 4, step, 0)
        store(o1, ci)
        start_back(1, o1, b1, ci)
        return carry

    lax.fori_loop(0, CHUNKS, forward, 0)

    def backward(ci, carry):
        arrived_chunk(2, ci, s2, r2)
        load(r2, ci)
        acc[...] = jnp.zeros_like(acc)

        def step(h, inner):
            grad = dot(xc[...], down[hidden(h), :], 1, 1) * 2.0 * relu[ci, :, hidden(h)]
            acc[...] += dot(grad.astype(BF), up[:, hidden(h)], 1, 1)
            return inner

        lax.fori_loop(0, 4, step, 0)
        store(o2, ci)
        start_back(3, o2, b2, ci)
        return carry

    lax.fori_loop(0, CHUNKS, backward, 0)

    def gather_back(which, src, dst):
        for ci in range(CHUNKS):
            arrived(which, ci, src, dst, ci == 0)

        def body(ci, carry):
            rows = pl.ds(pl.multiple_of(ci * EXTRA, EXTRA), EXTRA)
            extra[rows, :] = unpack(dst[main_rows(ci), 1024:1280])
            return carry

        lax.fori_loop(0, CHUNKS, body, 0)

    gather_back(1, o1, b1)
    both = dot(pg_back[:, 0:1024], b1[:, 0:1024]) + dot(pg_back[:, 1024:1280], extra[...])
    cb[tokens(mine), :] = (both[0:128] + both[128:256]).astype(BF)
    for d in range(1, 4):
        m, to = member(d)
        remote(cb.at[tokens(mine)], cb.at[tokens(mine)], cb_ss.at[d], cb_rs.at[mine], to).start()
    for d in range(1, 4):
        m, _ = member(d)
        remote(cb.at[tokens(m)], cb.at[tokens(m)], cb_ss.at[d], cb_rs.at[m], me).wait_recv()

    def gw_to(part, i):
        return index_of(part, z, c * 2 + i // 2, i % 2)

    def weight_grad(n, carry):
        part = (y + n) % 4
        cols = pl.ds(pl.multiple_of(part * 256, 256), 256)
        gwp[cols, :] = dot(go[:, cols], cb[...], 0, 0).astype(BF)
        for i in range(4):
            to = gw_to(part, i)
            rows = w_rows(part * 4 + i)
            from_here = w_rows(y * 4 + x)

            @pl.when(to != me)
            def _():
                remote(gwp.at[rows], gwr.at[from_here], gw_ss.at[part * 4 + i], gw_rs.at[y * 4 + x], to).start()

            @pl.when(to == me)
            def _():
                gwr[from_here, :] = gwp[rows, :]

        return carry

    lax.fori_loop(0, 4, weight_grad, 0)

    def mix(part, carry):
        rows = pl.ds(pl.multiple_of(part * 256, 256), 256)
        mps[:, rows] = dot(cb[...], wj[rows, :], 1, 1).astype(BF)
        for d in range(1, 4):
            m, to = member(d)
            remote(mps.at[tokens(m), rows], mixed.at[:, feats(mine, part)], mx_ss.at[d], mx_rs.at[mine], to).start()
        mixed[:, feats(mine, part)] = mps[tokens(mine), rows]
        return carry

    lax.fori_loop(0, 4, mix, 0)

    def gw_wait(i, carry):
        src = index_of(i // 4, z, i % 4, half)

        @pl.when(src != me)
        def _():
            remote(gwp.at[w_rows(i)], gwr.at[w_rows(i)], gw_ss.at[0], gw_rs.at[i], me).wait_recv()

        return carry

    lax.fori_loop(0, 16, gw_wait, 0)
    total = sum(gwr[i * 64 : (i + 1) * 64, :].astype(F32) for i in range(16))
    dps[...] = total.astype(BF)
    exchange = pltpu.make_async_remote_copy(
        dps, dpr, dp_ss.at[0], dp_rs.at[0], device_id=(1 - dp, me), device_id_type=MESH
    )
    exchange.start()

    gather_back(3, o2, b2)
    grad_latent[...] = (
        dot(p_back[:, 0:1024], b2[:, 0:1024]) + dot(p_back[:, 1024:1280], extra[...])
    ).astype(BF)

    exchange.wait()
    grad_w[...] = dps[...].astype(F32) + dpr[...].astype(F32)

    for d in range(1, 4):
        m, _ = member(d)
        whole = remote(mps.at[tokens(m)], mps.at[tokens(m)], mx_ss.at[d], mx_rs.at[m], me)
        whole.wait_recv()
        whole.wait_send()
        remote(go.at[tokens(m)], go.at[tokens(m)], go_ss.at[d], go_rs.at[m], me).wait_send()
        remote(pgs.at[tokens(m)], pgr.at[tokens(m)], pg_ss.at[d], pg_rs.at[m], me).wait_send()
        remote(cb.at[tokens(m)], cb.at[tokens(m)], cb_ss.at[d], cb_rs.at[m], me).wait_send()

    def last(i, carry):
        to, copy = w_copy(i)

        @pl.when(to != me)
        def _():
            copy.wait_send()

        @pl.when(gw_to(i // 4, i % 4) != me)
        def _():
            remote(gwp.at[w_rows(i)], gwr.at[w_rows(i)], gw_ss.at[i], gw_rs.at[i], me).wait_send()

        return carry

    lax.fori_loop(0, 16, last, 0)
    all_sent(0, s1, r1)
    all_sent(1, o1, b1)
    all_sent(2, s2, r2)
    all_sent(3, o2, b2)


def on_device(latent, routes, gates, grad_out, w_out_t, expert_up, expert_down):
    vm = pl.BlockSpec(memory_space=pltpu.VMEM)
    hbm = pl.BlockSpec(memory_space=pl.ANY)
    dma = pltpu.SemaphoreType.DMA
    buffers = [pltpu.VMEM((1024, 1280), BF)] * 8
    scratch = buffers + [
        pltpu.VMEM((1024, 2048), BF),
        pltpu.VMEM((2048, 1024), BF),
        pltpu.VMEM((CHUNKS, ROWS, 2048), F32),
        pltpu.VMEM((ROWS, 1024), BF),
        pltpu.VMEM((ROWS, 1024), F32),
        pltpu.VMEM((256, 1024), BF),
        pltpu.VMEM((512, 1024), BF),
        pltpu.VMEM((1024, 1024), BF),
        pltpu.VMEM((512, 1024), BF),
        pltpu.VMEM((512, 1024), BF),
        pltpu.VMEM((512, 1024), BF),
        pltpu.VMEM((512, 1024), BF),
        pltpu.VMEM((1024, 1024), BF),
        pltpu.VMEM((1024, 1024), BF),
        pltpu.VMEM((64, 1024), BF),
        pltpu.VMEM((64, 1024), BF),
        pltpu.VMEM((256, 256), BF),
        pltpu.VMEM((256, 256), BF),
        pltpu.VMEM((1280, 128), BF),
        pltpu.VMEM((1280, 256), BF),
        pltpu.VMEM((128, 1280), BF),
        pltpu.VMEM((256, 1280), BF),
        dma((4,)), dma((4, 4)),
        dma((16,)), dma((16,)),
        dma((4,)), dma((4,)),
        dma((4,)), dma((4,)),
        dma((4,)), dma((4,)),
        dma((4,)), dma((4,)),
        dma((16,)), dma((16,)),
        dma((1,)), dma((1,)),
        dma((6,)),
    ]
    return pl.pallas_call(
        kernel,
        out_shape=(
            jax.ShapeDtypeStruct((128, 4096), BF),
            jax.ShapeDtypeStruct((128, 1024), BF),
            jax.ShapeDtypeStruct((64, 1024), F32),
        ),
        in_specs=[vm, vm, vm, vm, hbm, hbm, hbm],
        out_specs=(vm, vm, vm),
        scratch_shapes=scratch,
        compiler_params=pltpu.CompilerParams(
            collective_id=0, has_side_effects=True, vmem_limit_bytes=62 * 1024 * 1024
        ),
        cost_estimate=pl.CostEstimate(flops=25_000_000_000, bytes_accessed=20_000_000, transcendentals=0),
        name="moe_layer",
    )(latent, routes, gates, w_out_t, grad_out, expert_up, expert_down)


def solution(mesh):
    rows = P(("dp", "expert"), None)
    return jax.shard_map(
        on_device,
        mesh=mesh,
        in_specs=(rows, rows, rows, rows, P("expert", None), P("expert", None, None), P("expert", None, None)),
        out_specs=(rows, rows, P("expert", None)),
        check_vma=False,
    )
```

```python
import jax
import jax.numpy as jnp
from jax import lax
from jax.experimental import pallas as pl
from jax.experimental.pallas import tpu as pltpu
from jax.sharding import PartitionSpec as P

BF = jnp.bfloat16
F32 = jnp.float32
I32 = jnp.int32
MESH = pl.DeviceIdType.MESH
STRIDE = 11
CHUNKS = 4
PER = 8
MAIN = 256
EXTRA = 64
ROWS = 320


def iota(shape, dim):
    return lax.broadcasted_iota(I32, shape, dim)


def dot(a, b, ca=1, cb=0):
    return lax.dot_general(a, b, (((ca,), (cb,)), ((), ())), preferred_element_type=F32)


def index_of(y, z, x, c):
    return ((y * 2 + z) * 4 + x) * 2 + c


def rows_at(start, size):
    return pl.ds(pl.multiple_of(start, size), size)


def kernel(
    latent, routes, gates, w_own, grad_out, up_hbm, down_hbm,
    mixed, grad_latent, grad_w,
    s1, r1, b1, s2, r2, b2, up, down, relu, xc, acc, extra,
    routes2, gates2, latent2, gc2, part_f, part_b,
    go, wj, pga, pgb, pgs, pgr, cb, mps, gwp, gwy, gws, gwx, dps, dpr,
    sel, selt, p_send, pg_send, p_back, pg_back,
    a2a_ss, a2a_rs, bud_ss, bud_rs, wx_ss, wx_rs, wy_ss, wy_rs, go_ss, go_rs,
    pga_sem, pg_ss, pg_rs, cb_ss, cb_rs, cf_ss, mx_ss, mx_rs,
    gy_ss, gy_rs, gx_ss, gx_rs, dp_sem, loc,
):
    dp = lax.axis_index("dp")
    me = lax.axis_index("expert")
    y, z, x, c = me // 16, (me // 8) % 2, (me // 2) % 4, me % 2
    ring = dp * 2 + z
    mine = c * 4 + ring
    here = y * 8 + x * 2 + c
    sibling = index_of(y, z, x, 1 - c)
    buddy = index_of(y, 1 - z, x, c)
    half, parity = x // 2, x % 2

    def partner(k, sign):
        off = (STRIDE * k) % 32
        py, px, pc = (y + sign * (off // 8) + 4) % 4, (x + sign * ((off // 2) % 4) + 4) % 4, (c + off) % 2
        return index_of(py, z, px, pc), py * 8 + px * 2 + pc

    def ring_at(d):
        to = (ring + d) % 4
        return to, to // 2, index_of(y, to % 2, x, c)

    def member(dc, dz):
        to, cc = (ring + dz) % 4, (c + dc) % 2
        return cc * 4 + to, to // 2, index_of(y, to % 2, x, cc)

    others = [(dc, dz) for dz in (1, 3, 2, 0) for dc in (0, 1) if dc or dz]

    def remote(src, dst, ss, rs, dev, rep=None):
        rep = dp if rep is None else rep
        return pltpu.make_async_remote_copy(src, dst, ss, rs, device_id=(rep, dev), device_id_type=MESH)

    barrier = pltpu.get_barrier_semaphore()

    def greet(k, carry):
        pl.semaphore_signal(barrier, inc=1, device_id=(dp, partner(k, 1)[0]), device_id_type=MESH)
        return carry

    lax.fori_loop(1, 32, greet, 0)
    for dc, dz in others:
        if dz:
            _, rep, to = member(dc, dz)
            pl.semaphore_signal(barrier, inc=1, device_id=(rep, to), device_id_type=MESH)
    up_copy = pltpu.make_async_copy(up_hbm.at[0], up, loc.at[0])
    down_copy = pltpu.make_async_copy(down_hbm.at[0], down, loc.at[1])
    up_copy.start()
    down_copy.start()
    routes2[z] = routes[...]
    gates2[z] = gates[...]
    latent2[rows_at(z * 128, 128), :] = latent[...]

    i, j = iota((256, 256), 0), iota((256, 256), 1)
    sel[...] = jnp.where(((i & 63) >> 2) * 16 + (i >> 6) * 4 + (i & 3) == j, 1.0, 0.0).astype(BF)
    selt[...] = jnp.where(((j & 63) >> 2) * 16 + (j >> 6) * 4 + (j & 3) == i, 1.0, 0.0).astype(BF)

    pl.semaphore_wait(barrier, 37)

    own_tokens = rows_at(z * 128, 128)
    swap = [
        remote(routes, routes2.at[z], bud_ss.at[0], bud_rs.at[0], buddy),
        remote(gates, gates2.at[z], bud_ss.at[1], bud_rs.at[1], buddy),
        remote(latent, latent2.at[own_tokens], bud_ss.at[2], bud_rs.at[2], buddy),
    ]
    for copy in swap:
        copy.start()

    sends_w = parity == (y + dp) % 2
    w_slot = rows_at(y * 128 + c * 64, 64)

    def wx(d):
        to = index_of(y, z, (x + d) % 4, half)
        return to, remote(w_own, wj.at[w_slot], wx_ss.at[d], wx_rs.at[c], to)

    for d in (1, 3, 2, 0):
        to, copy = wx(d)
        go_on = jnp.logical_and(sends_w, to != me)

        @pl.when(go_on)
        def _():
            copy.start()

        if d == 0:

            @pl.when(jnp.logical_and(sends_w, to == me))
            def _():
                wj[w_slot, :] = w_own[...]

    def feats(m, part):
        to = m % 4
        return rows_at(part * 1024 + (to % 2) * 512 + (m // 4) * 256 + ((part + to // 2) % 2) * 128, 128)

    def tokens(m):
        return rows_at(m * 128, 128)

    own_go = []
    for part in range(4):
        cols = pl.ds(part * 128, 128)
        for n, (dc, dz) in enumerate(others):
            m, rep, to = member(dc, dz)
            remote(grad_out.at[:, feats(m, part)], go.at[tokens(mine), cols], go_ss.at[n], go_rs.at[mine], to, rep).start()
        copy = pltpu.make_async_copy(grad_out.at[:, feats(mine, part)], go.at[tokens(mine), cols], loc.at[2 + part])
        copy.start()
        own_go.append(copy)

    x_own = c * 2 + (y + dp) % 2
    for cc in range(2):
        src = index_of(y, z, x_own, cc)

        @pl.when(src != me)
        def _():
            remote(w_own, wj.at[rows_at(y * 128 + cc * 64, 64)], wx_ss.at[0], wx_rs.at[cc], me).wait_recv()

    def along_y(d):
        py = (y + d) % 4
        return py, index_of(py, z, x, c)

    def wy(d):
        _, to = along_y(d)
        return remote(wj.at[tokens(y)], wj.at[tokens(y)], wy_ss.at[d], wy_rs.at[y], to)

    for d in (1, 3, 2):
        wy(d).start()

    swap[0].wait_recv()
    swap[1].wait_recv()

    def names(j):
        return jnp.where(j < 1024, j >> 4, (j - 1024) >> 2), jnp.where(j < 1024, j & 15, 16 + (j & 3)) + 1

    def expert_of(pair):
        p = pair >> 1
        return (p >> 3) * 16 + z * 8 + (p & 7)

    pair_r, s_row = names(iota((1280, 128), 0))
    pair_c, s_col = names(iota((128, 1280), 1))
    named_r = expert_of(pair_r) == iota((1280, 128), 1)
    named_c = expert_of(pair_c) == iota((128, 1280), 0)
    earlier = jnp.where(iota((128, 128), 0) < iota((128, 128), 1), 1.0, 0.0).astype(BF)
    for zs in range(2):
        rt = routes2[zs]
        gt = gates2[zs]
        expert = iota((128, 128), 0)
        hot = jnp.zeros((128, 128), F32)
        gate = jnp.zeros((128, 128), F32)
        for k in range(8):
            hit = rt[k : k + 1, :] == expert
            hot = hot + jnp.where(hit, 1.0, 0.0)
            gate = gate + jnp.where(hit, gt[k : k + 1, :], 0.0)
        slot = jnp.where(hot > 0.5, dot(hot.astype(BF), earlier) + 1.0, 0.0)
        gate_hi = gate.astype(BF).astype(F32)
        gate_lo = gate - gate_hi
        t0, t1 = zs * 128, zs * 128 + 128
        spread_t = jnp.where(jnp.logical_and(named_r, (pair_r & 1) == zs), 1.0, 0.0).astype(BF)
        hit_t = dot(spread_t, slot.astype(BF)) == s_row.astype(F32)
        p_send[:, t0:t1] = jnp.where(hit_t, 1.0, 0.0).astype(BF)
        pg_send[:, t0:t1] = jnp.where(hit_t, dot(spread_t, gate_hi.astype(BF)), 0.0).astype(BF)
        pg_send[:, 256 + t0 : 256 + t1] = jnp.where(hit_t, dot(spread_t, gate_lo.astype(BF)), 0.0).astype(BF)
        spread = jnp.where(jnp.logical_and(named_c, (pair_c & 1) == zs), 1.0, 0.0).astype(BF)
        hit_b = dot(slot.T.astype(BF), spread) == s_col.astype(F32)
        p_back[t0:t1, :] = jnp.where(hit_b, 1.0, 0.0).astype(BF)
        pg_back[t0:t1, :] = jnp.where(hit_b, dot(gate_hi.T.astype(BF), spread), 0.0).astype(BF)
        pg_back[256 + t0 : 256 + t1, :] = jnp.where(hit_b, dot(gate_lo.T.astype(BF), spread), 0.0).astype(BF)

    def unpack(packed):
        rows = dot(sel[...], packed).astype(BF)
        return jnp.concatenate([rows[q * 64 : (q + 1) * 64] for q in range(4)], axis=1)

    def pack(rows):
        stacked = jnp.concatenate([rows[:, q * 256 : (q + 1) * 256] for q in range(4)], axis=0)
        return dot(selt[...], stacked).astype(BF)

    def main_rows(ci):
        return rows_at(ci * MAIN, MAIN)

    def fill(pick, source, buffer):
        def body(ci, carry):
            buffer[main_rows(ci), 0:1024] = dot(pick[main_rows(ci), :], source[...]).astype(BF)
            more = pick[rows_at(1024 + ci * EXTRA, EXTRA), :]
            buffer[main_rows(ci), 1024:1280] = pack(dot(more, source[...]).astype(BF))
            return carry

        lax.fori_loop(0, CHUNKS, body, 0)

    def block(k):
        return rows_at(k * 32, 32)

    def start_out(which, src, dst):
        def body(k, carry):
            to, p = partner(k, 1)
            remote(src.at[block(p)], dst.at[block(k)], a2a_ss.at[which], a2a_rs.at[which, k // PER], to).start()
            return carry

        lax.fori_loop(1, 32, body, 0)
        dst[0:32, :] = src[block(here), :]

    def start_back(which, src, dst, ci):
        def body(k, carry):
            to, _ = partner(k, -1)
            remote(src.at[block(k)], dst.at[block(here)], a2a_ss.at[which], a2a_rs.at[which, k // PER], to).start()
            return carry

        lax.fori_loop(jnp.maximum(ci * PER, 1), ci * PER + PER, body, 0)

        @pl.when(ci == 0)
        def _():
            dst[block(here), :] = src[0:32, :]

    def arrived(which, ci, src, dst, first):
        rows = pl.ds(0, 224) if first else main_rows(ci)
        remote(src.at[rows], dst.at[rows], a2a_ss.at[which], a2a_rs.at[which, ci], me).wait_recv()

    def all_sent(which, src, dst):
        rows = pl.ds(0, 992)
        remote(src.at[rows], dst.at[rows], a2a_ss.at[which], a2a_rs.at[which, 0], me).wait_send()

    swap[2].wait_recv()
    fill(p_send, latent2, s1)
    start_out(0, s1, r1)

    for d in (1, 3, 2):
        py, _ = along_y(d)
        remote(wj.at[tokens(py)], wj.at[tokens(py)], wy_ss.at[d], wy_rs.at[py], me).wait_recv()
    for copy in own_go:
        copy.wait()
    for n, (dc, dz) in enumerate(others):
        m, _, _ = member(dc, dz)
        remote(go.at[tokens(m)], go.at[tokens(m)], go_ss.at[n], go_rs.at[m], me).wait_recv()

    def quarter(n):
        return rows_at(n * 256, 256)

    def core_rows(cc):
        return rows_at(cc * 512, 512)

    def for_sibling(n, carry):
        pga[:, quarter(n)] = dot(go[core_rows(1 - c), :], wj[:, quarter(n)]).astype(BF)
        return carry

    lax.fori_loop(0, 4, for_sibling, 0)
    to_sibling = remote(pga, pgb, pga_sem.at[0], pga_sem.at[1], sibling)
    to_sibling.start()
    to_sibling.wait_recv()

    def for_own(n, carry):
        pgs[:, quarter(n)] = (dot(go[core_rows(c), :], wj[:, quarter(n)]) + pgb[:, quarter(n)].astype(F32)).astype(BF)
        return carry

    lax.fori_loop(0, 4, for_own, 0)
    for d in (1, 3, 2):
        to, rep, dev = ring_at(d)
        remote(pgs.at[tokens(to)], pgr.at[tokens(ring)], pg_ss.at[d], pg_rs.at[ring], dev, rep).start()
    pgr[tokens(ring), :] = pgs[tokens(ring), :]
    for d in (1, 3, 2):
        to, _, _ = ring_at(d)
        remote(pgs.at[tokens(to)], pgr.at[tokens(to)], pg_ss.at[d], pg_rs.at[to], me).wait_recv()
    gc = sum(pgr[n * 128 : (n + 1) * 128, :].astype(F32) for n in range(4)).astype(BF)
    gc2[own_tokens, :] = gc
    gc2[rows_at(256 + z * 128, 128), :] = gc
    swap_gc = remote(gc2.at[own_tokens], gc2.at[own_tokens], bud_ss.at[3], bud_rs.at[3], buddy)
    swap_gc.start()
    swap_gc.wait_recv()
    gc2[rows_at(256 + (1 - z) * 128, 128), :] = gc2[rows_at((1 - z) * 128, 128), :]
    fill(pg_send, gc2, s2)
    start_out(2, s2, r2)

    up_copy.wait()
    down_copy.wait()

    def load(src, ci):
        xc[0:MAIN, :] = src[main_rows(ci), 0:1024]
        xc[MAIN:ROWS, :] = unpack(src[main_rows(ci), 1024:1280])

    def store(dst, ci):
        dst[main_rows(ci), 0:1024] = acc[0:MAIN, :].astype(BF)
        dst[main_rows(ci), 1024:1280] = pack(acc[MAIN:ROWS, :].astype(BF))

    def hidden(h):
        return rows_at(h * 512, 512)

    def arrived_chunk(which, ci, src, dst):
        @pl.when(ci == 0)
        def _():
            arrived(which, 0, src, dst, True)

        @pl.when(ci > 0)
        def _():
            arrived(which, ci, src, dst, False)

    def forward(ci, carry):
        arrived_chunk(0, ci, s1, r1)
        load(r1, ci)
        acc[...] = jnp.zeros_like(acc)

        def step(h, inner):
            pos = jnp.maximum(dot(xc[...], up[:, hidden(h)]), 0.0)
            relu[ci, :, hidden(h)] = pos
            acc[...] += dot((pos * pos).astype(BF), down[hidden(h), :])
            return inner

        lax.fori_loop(0, 4, step, 0)
        store(r1, ci)
        start_back(1, r1, b1, ci)
        return carry

    lax.fori_loop(0, CHUNKS, forward, 0)

    def backward(ci, carry):
        arrived_chunk(2, ci, s2, r2)
        load(r2, ci)
        acc[...] = jnp.zeros_like(acc)

        def step(h, inner):
            grad = dot(xc[...], down[hidden(h), :], 1, 1) * 2.0 * relu[ci, :, hidden(h)]
            acc[...] += dot(grad.astype(BF), up[:, hidden(h)], 1, 1)
            return inner

        lax.fori_loop(0, 4, step, 0)
        store(r2, ci)
        start_back(3, r2, b2, ci)
        return carry

    lax.fori_loop(0, CHUNKS, backward, 0)

    def gather_back(which, src, dst):
        for ci in range(CHUNKS):
            arrived(which, ci, src, dst, ci == 0)

        def body(ci, carry):
            extra[rows_at(ci * EXTRA, EXTRA), :] = unpack(dst[main_rows(ci), 1024:1280])
            return carry

        lax.fori_loop(0, CHUNKS, body, 0)

    def swap_part(n, slot):
        part_b[slot] = part_f[rows_at((1 - z) * 128, 128), :].astype(BF)
        copy = remote(part_b.at[slot], part_b.at[slot + 1], bud_ss.at[n], bud_rs.at[n], buddy)
        copy.start()
        return copy

    gather_back(1, r1, b1)

    def combine(n, carry):
        cols = quarter(n)
        both = dot(pg_back[:, 0:1024], b1[:, cols])
        both = both + dot(pg_back[:, 1024:1280], extra[:, cols])
        part_f[:, cols] = both[0:256] + both[256:512]
        return carry

    lax.fori_loop(0, 4, combine, 0)
    swap_c = swap_part(4, 0)
    swap_c.wait_recv()
    cb[tokens(mine), :] = (part_f[own_tokens, :] + part_b[1].astype(F32)).astype(BF)

    def cb_copy(m, ss, dev, rep):
        return remote(cb.at[tokens(m)], cb.at[tokens(m)], ss, cb_rs.at[m], dev, rep)

    for d in (1, 3, 2):
        _, rep, dev = ring_at(d)
        cb_copy(mine, cb_ss.at[d], dev, rep).start()
    cb_copy(mine, cb_ss.at[0], sibling, dp).start()
    for d in (1, 3, 2):
        to, _, _ = ring_at(d)
        m = c * 4 + to
        cb_copy(m, cb_ss.at[d], me, dp).wait_recv()
        cb_copy(m, cf_ss.at[d], sibling, dp).start()
    for d in range(4):
        m = (1 - c) * 4 + (ring + d) % 4
        cb_copy(m, cb_ss.at[d], me, dp).wait_recv()

    def gy(d):
        py, to = along_y(d)
        return py, remote(gwp.at[tokens(py)], gwy.at[tokens(y)], gy_ss.at[d], gy_rs.at[y], to)

    def weight_grad(n, carry):
        py = (y + 3 - n) % 4
        gwp[tokens(py), :] = dot(go[:, tokens(py)], cb[...], 0, 0).astype(BF)

        @pl.when(n < 3)
        def _():
            to = index_of(py, z, x, c)
            remote(gwp.at[tokens(py)], gwy.at[tokens(y)], gy_ss.at[3 - n], gy_rs.at[y], to).start()

        return carry

    lax.fori_loop(0, 4, weight_grad, 0)
    gwy[tokens(y), :] = gwp[tokens(y), :]

    def mix(part, carry):
        cols = tokens(part)
        mps[:, cols] = dot(cb[...], wj[cols, :], 1, 1).astype(BF)
        for n, (dc, dz) in enumerate(others):
            m, rep, to = member(dc, dz)
            remote(mps.at[tokens(m), cols], mixed.at[:, feats(mine, part)], mx_ss.at[n], mx_rs.at[mine], to, rep).start()
        mixed[:, feats(mine, part)] = mps[tokens(mine), cols]
        return carry

    lax.fori_loop(0, 4, mix, 0)

    for d in (1, 3, 2):
        py, _ = along_y(d)
        remote(gwp.at[tokens(py)], gwy.at[tokens(py)], gy_ss.at[d], gy_rs.at[py], me).wait_recv()
    gws[...] = sum(gwy[n * 128 : (n + 1) * 128, :].astype(F32) for n in range(4)).astype(BF)
    x_slot = rows_at(x * 64, 64)

    def gx(cc):
        to = index_of(y, z, x_own, cc)
        return to, remote(gws.at[pl.ds(cc * 64, 64)], gwx.at[x_slot], gx_ss.at[cc], gx_rs.at[x], to)

    for cc in range(2):
        to, copy = gx(cc)

        @pl.when(to != me)
        def _():
            copy.start()

        @pl.when(to == me)
        def _():
            gwx[x_slot, :] = gws[cc * 64 : cc * 64 + 64, :]

    exchange = pltpu.make_async_remote_copy(
        dps, dpr, dp_sem.at[0], dp_sem.at[1], device_id=(1 - dp, me), device_id_type=MESH
    )

    @pl.when(sends_w)
    def _():
        for px in range(4):
            src = index_of(y, z, px, half)

            @pl.when(src != me)
            def _():
                rows = pl.ds(px * 64, 64)
                remote(gwx.at[rows], gwx.at[rows], gx_ss.at[0], gx_rs.at[px], me).wait_recv()

        dps[...] = sum(gwx[n * 64 : (n + 1) * 64, :].astype(F32) for n in range(4)).astype(BF)
        exchange.start()

    gather_back(3, r2, b2)

    def combine_back(n, carry):
        cols = quarter(n)
        part_f[:, cols] = dot(p_back[:, 0:1024], b2[:, cols]) + dot(p_back[:, 1024:1280], extra[:, cols])
        return carry

    lax.fori_loop(0, 4, combine_back, 0)
    swap_g = swap_part(5, 2)
    swap_g.wait_recv()
    grad_latent[...] = (part_f[own_tokens, :] + part_b[3].astype(F32)).astype(BF)

    @pl.when(sends_w)
    def _():
        exchange.wait_send()
        grad_w[...] = dps[...].astype(F32)

    @pl.when(jnp.logical_not(sends_w))
    def _():
        exchange.wait_recv()
        grad_w[...] = dpr[...].astype(F32)

    for n, (dc, dz) in enumerate(others):
        m, _, _ = member(dc, dz)
        whole = remote(mps.at[tokens(m)], mps.at[tokens(m)], mx_ss.at[n], mx_rs.at[m], me)
        whole.wait_recv()
        whole.wait_send()
        remote(go.at[tokens(m)], go.at[tokens(m)], go_ss.at[n], go_rs.at[m], me).wait_send()
    for copy in swap + [swap_gc, swap_c, swap_g, to_sibling]:
        copy.wait_send()
    for d in range(4):
        to, copy = wx(d)
        go_on = jnp.logical_and(sends_w, to != me)

        @pl.when(go_on)
        def _():
            copy.wait_send()

        cb_copy(mine, cb_ss.at[d], me, dp).wait_send()
        if d:
            wy(d).wait_send()
            gy(d)[1].wait_send()
            cb_copy(mine, cf_ss.at[d], me, dp).wait_send()
            remote(pgs.at[tokens(0)], pgr.at[tokens(0)], pg_ss.at[d], pg_rs.at[0], me).wait_send()
    for cc in range(2):
        to, copy = gx(cc)

        @pl.when(to != me)
        def _():
            copy.wait_send()

    all_sent(0, s1, r1)
    all_sent(1, r1, b1)
    all_sent(2, s2, r2)
    all_sent(3, r2, b2)


def on_device(latent, routes, gates, grad_out, w_out_t, expert_up, expert_down):
    vm = pl.BlockSpec(memory_space=pltpu.VMEM)
    hbm = pl.BlockSpec(memory_space=pl.ANY)

    def dma(*shape):
        return pltpu.SemaphoreType.DMA(shape)

    def bf(*shape):
        return pltpu.VMEM(shape, BF)

    scratch = [bf(1024, 1280)] * 6 + [
        bf(1024, 2048), bf(2048, 1024), pltpu.VMEM((CHUNKS, ROWS, 2048), F32),
        bf(ROWS, 1024), pltpu.VMEM((ROWS, 1024), F32), bf(256, 1024),
        pltpu.VMEM((2, 8, 128), I32), pltpu.VMEM((2, 8, 128), F32), bf(256, 1024), bf(512, 1024),
        pltpu.VMEM((256, 1024), F32), bf(4, 128, 1024),
        bf(1024, 512), bf(512, 1024), bf(512, 1024), bf(512, 1024), bf(512, 1024), bf(512, 1024),
        bf(1024, 1024), bf(1024, 512), bf(512, 1024), bf(512, 1024), bf(128, 1024), bf(256, 1024),
        bf(64, 1024), bf(64, 1024),
        bf(256, 256), bf(256, 256), bf(1280, 256), bf(1280, 512), bf(256, 1280), bf(512, 1280),
        dma(4), dma(4, 4), dma(6), dma(6), dma(4), dma(2), dma(4), dma(4), dma(7), dma(8),
        dma(2), dma(4), dma(4), dma(4), dma(8), dma(4), dma(7), dma(8),
        dma(4), dma(4), dma(2), dma(4), dma(2), dma(6),
    ]
    return pl.pallas_call(
        kernel,
        out_shape=(
            jax.ShapeDtypeStruct((128, 4096), BF),
            jax.ShapeDtypeStruct((128, 1024), BF),
            jax.ShapeDtypeStruct((64, 1024), F32),
        ),
        in_specs=[vm, vm, vm, vm, hbm, hbm, hbm],
        out_specs=(vm, vm, vm),
        scratch_shapes=scratch,
        compiler_params=pltpu.CompilerParams(
            collective_id=0, has_side_effects=True, vmem_limit_bytes=63 * 1024 * 1024
        ),
        cost_estimate=pl.CostEstimate(flops=25_000_000_000, bytes_accessed=20_000_000, transcendentals=0),
        name="moe_layer",
    )(latent, routes.T, gates.T, w_out_t, grad_out, expert_up, expert_down)


def solution(mesh):
    rows = P(("dp", "expert"), None)
    return jax.shard_map(
        on_device,
        mesh=mesh,
        in_specs=(rows, rows, rows, rows, P("expert", None), P("expert", None, None), P("expert", None, None)),
        out_specs=(rows, rows, P("expert", None)),
        check_vma=False,
    )
```

```python
import jax
import jax.numpy as jnp
from jax import lax
from jax.experimental import pallas as pl
from jax.experimental.pallas import tpu as pltpu
from jax.sharding import PartitionSpec as P

BF = jnp.bfloat16
F32 = jnp.float32
I32 = jnp.int32
MESH = pl.DeviceIdType.MESH
STRIDE = 5
CHUNKS = 4
PER = 4
MAIN = 256
EXTRA = 64
ROWS = 320


def iota(shape, dim):
    return lax.broadcasted_iota(I32, shape, dim)


def dot(a, b, ca=1, cb=0):
    return lax.dot_general(a, b, (((ca,), (cb,)), ((), ())), preferred_element_type=F32)


def index_of(y, z, x, c):
    return ((y * 2 + z) * 4 + x) * 2 + c


def rows_at(start, size):
    return pl.ds(pl.multiple_of(start, size), size)


def kernel(
    latent, routes, gates, w_own, grad_out, up_hbm, down_hbm,
    mixed, grad_latent, grad_w,
    s1, r1, b1, s2, r2, b2, up, down, relu, xc, acc, extra,
    routes4, gates4, latent4, gc4, part_f, part_s, part_r,
    go, wj, pga, pgb, pgs, pgr, cb, mps, gwp, gwy, gws, gwx, dps, dpr,
    slots, gate_tab, sel, selt, p_send, pg_send, p_back, pg_back,
    a2a_ss, a2a_rs, grp_ss, grp_rs, sw_ss, sw_rs, wx_ss, wx_rs, wy_ss, wy_rs, go_ss, go_rs,
    sib_ss, sib_rs, bgc_ss, bgc_rs, pg_ss, pg_rs, cb_ss, cb_rs, cf_ss, mx_ss, mx_rs,
    gy_ss, gy_rs, gx_ss, gx_rs, dp_sem, loc,
):
    dp = lax.axis_index("dp")
    me = lax.axis_index("expert")
    y, z, x, c = me // 16, (me // 8) % 2, (me // 2) % 4, me % 2
    ring = dp * 2 + z
    mine = c * 4 + ring
    sibling = index_of(y, z, x, 1 - c)
    block = x * (1 - c) + y * c
    half, parity = x // 2, x % 2

    def partner(k, sign):
        off = (STRIDE * k) % 16
        along, hop, flip = off // 4, (off // 2) % 2, off % 2
        pc = (c + flip) % 2
        sender, expert = (c, pc) if sign > 0 else (pc, c)
        pr = (ring + sign * hop * (1 - 2 * expert) + 4) % 4
        py, px = (y + sign * along * (1 - sender) + 4) % 4, (x + sign * along * sender + 4) % 4
        return pr // 2, index_of(py, pr % 2, px, pc)

    def group_at(d):
        to = (block + d) % 4
        return to, index_of(y + c * (to - y), z, x + (1 - c) * (to - x), c)

    def ring_at(d):
        to = (ring + d) % 4
        return to, to // 2, index_of(y, to % 2, x, c)

    def member(dc, dz):
        to, cc = (ring + dz) % 4, (c + dc) % 2
        return cc * 4 + to, to // 2, index_of(y, to % 2, x, cc)

    others = [(dc, dz) for dz in (1, 3, 2, 0) for dc in (0, 1) if dc or dz]

    def remote(src, dst, ss, rs, dev, rep=None):
        rep = dp if rep is None else rep
        return pltpu.make_async_remote_copy(src, dst, ss, rs, device_id=(rep, dev), device_id_type=MESH)

    barrier = pltpu.get_barrier_semaphore()

    def signal(rep, dev):
        pl.semaphore_signal(barrier, inc=1, device_id=(rep, dev), device_id_type=MESH)

    def greet(k, carry):
        for sign in (1, -1):
            signal(*partner(k, sign))
        return carry

    lax.fori_loop(1, 16, greet, 0)
    for dc, dz in others:
        _, rep, to = member(dc, dz)
        signal(rep, to)
    for d in range(1, 8):
        near = (x * 2 + c + d) % 8
        signal(dp, index_of(y, z, near // 2, near % 2))
    for d in range(1, 4):
        signal(dp, index_of((y + d) % 4, z, x, c))
    up_copy = pltpu.make_async_copy(up_hbm.at[0], up, loc.at[0])
    down_copy = pltpu.make_async_copy(down_hbm.at[0], down, loc.at[1])
    up_copy.start()
    down_copy.start()
    own_tokens = rows_at(block * 128, 128)
    routes4[block] = routes[...]
    gates4[block] = gates[...]
    latent4[own_tokens, :] = latent[...]

    i, j = iota((256, 256), 0), iota((256, 256), 1)
    sel[...] = jnp.where(((i & 63) >> 2) * 16 + (i >> 6) * 4 + (i & 3) == j, 1.0, 0.0).astype(BF)
    selt[...] = jnp.where(((j & 63) >> 2) * 16 + (j >> 6) * 4 + (j & 3) == i, 1.0, 0.0).astype(BF)

    pl.semaphore_wait(barrier, 47)

    swap = []
    for d in (1, 3, 2):
        _, to = group_at(d)
        swap.append(remote(routes, routes4.at[block], grp_ss.at[0, d], grp_rs.at[0, block], to))
        swap.append(remote(gates, gates4.at[block], grp_ss.at[1, d], grp_rs.at[1, block], to))
    for d in (1, 3, 2):
        _, to = group_at(d)
        swap.append(remote(latent, latent4.at[own_tokens], grp_ss.at[2, d], grp_rs.at[2, block], to))
    for copy in swap:
        copy.start()

    def from_group(n, dst):
        for d in (1, 3, 2):
            g, _ = group_at(d)
            remote(dst(g), dst(g), grp_ss.at[n, d], grp_rs.at[n, g], me).wait_recv()

    sends_w = parity == (y + dp) % 2
    w_slot = rows_at(y * 128 + c * 64, 64)

    def wx(d):
        to = index_of(y, z, (x + d) % 4, half)
        return to, remote(w_own, wj.at[w_slot], wx_ss.at[d], wx_rs.at[c], to)

    for d in (1, 3, 2, 0):
        to, copy = wx(d)
        go_on = jnp.logical_and(sends_w, to != me)

        @pl.when(go_on)
        def _():
            copy.start()

        if d == 0:

            @pl.when(jnp.logical_and(sends_w, to == me))
            def _():
                wj[w_slot, :] = w_own[...]

    def feats(m, part):
        to = m % 4
        return rows_at(part * 1024 + (to % 2) * 512 + (m // 4) * 256 + ((part + to // 2) % 2) * 128, 128)

    def tokens(m):
        return rows_at(m * 128, 128)

    own_go = []
    for part in range(4):
        cols = pl.ds(part * 128, 128)
        for n, (dc, dz) in enumerate(others):
            m, rep, to = member(dc, dz)
            remote(grad_out.at[:, feats(m, part)], go.at[tokens(mine), cols], go_ss.at[n], go_rs.at[mine], to, rep).start()
        copy = pltpu.make_async_copy(grad_out.at[:, feats(mine, part)], go.at[tokens(mine), cols], loc.at[2 + part])
        copy.start()
        own_go.append(copy)

    from_group(0, lambda g: routes4.at[g])
    from_group(1, lambda g: gates4.at[g])

    def names(j):
        return jnp.where(j < 256, j >> 4, (j - 256) >> 2), jnp.where(j < 256, j & 15, 16 + (j & 3)) + 1

    def expert_of(k):
        off = (STRIDE * k) & 15
        along, hop, pc = off >> 2, (off >> 1) & 1, (c + off) & 1
        py, px = (y + along * (1 - c)) & 3, (x + along * c) & 3
        return ((py * 2 + ((z + hop) & 1)) * 4 + px) * 2 + pc

    k_row, s_row = names(iota((320, 128), 0))
    k_col, s_col = names(iota((128, 320), 1))
    spread_t = jnp.where(expert_of(k_row) == iota((320, 128), 1), 1.0, 0.0).astype(BF)
    spread = jnp.where(expert_of(k_col) == iota((128, 320), 0), 1.0, 0.0).astype(BF)
    earlier = jnp.where(iota((128, 128), 0) < iota((128, 128), 1), 1.0, 0.0).astype(BF)

    def table(g):
        hot = jnp.zeros((128, 128), F32)
        gate = jnp.zeros((128, 128), F32)
        for k in range(8):
            hit = routes4[g, k : k + 1, :] == iota((128, 128), 0)
            hot = hot + jnp.where(hit, 1.0, 0.0)
            gate = gate + jnp.where(hit, gates4[g, k : k + 1, :], 0.0)
        slot = jnp.where(hot > 0.5, dot(hot.astype(BF), earlier) + 1.0, 0.0)
        return slot, gate

    for g in range(4):
        slots[g], gate_tab[g] = table(g)
        hit = dot(spread_t, slots[g].astype(BF)) == s_row.astype(F32)
        p_send[g] = jnp.where(hit, 1.0, 0.0).astype(BF)

    def routing_rest():
        for g in range(4):
            gate_hi = gate_tab[g].astype(BF).astype(F32)
            gate_lo = gate_tab[g] - gate_hi
            hit = p_send[g].astype(F32) > 0.5
            pg_send[g, :, 0:128] = jnp.where(hit, dot(spread_t, gate_hi.astype(BF)), 0.0).astype(BF)
            pg_send[g, :, 128:256] = jnp.where(hit, dot(spread_t, gate_lo.astype(BF)), 0.0).astype(BF)
            hit = dot(slots[g].T.astype(BF), spread) == s_col.astype(F32)
            p_back[g] = jnp.where(hit, 1.0, 0.0).astype(BF)
            pg_back[g, 0:128, :] = jnp.where(hit, dot(gate_hi.T.astype(BF), spread), 0.0).astype(BF)
            pg_back[g, 128:256, :] = jnp.where(hit, dot(gate_lo.T.astype(BF), spread), 0.0).astype(BF)

    def unpack(packed):
        rows = dot(sel[...], packed).astype(BF)
        return jnp.concatenate([rows[q * 64 : (q + 1) * 64] for q in range(4)], axis=1)

    def pack(rows):
        stacked = jnp.concatenate([rows[:, q * 256 : (q + 1) * 256] for q in range(4)], axis=0)
        return dot(selt[...], stacked).astype(BF)

    def message(k):
        return rows_at(k * 16, 16)

    def start(which, src, dst, ci, sign):
        def body(k, carry):
            rep, to = partner(k, sign)
            piece = (slice(None), message(k))
            remote(src.at[piece], dst.at[piece], a2a_ss.at[which], a2a_rs.at[which, ci], to, rep).start()
            return carry

        lax.fori_loop(max(ci * PER, 1), ci * PER + PER, body, 0)
        if ci == 0:
            dst[:, 0:16, :] = src[:, 0:16, :]

    def dispatch(which, pick, source, src, dst):
        for g in range(4):
            values = source[g * 128 : g * 128 + 128, :]
            if pick.shape[2] == 256:
                values = jnp.concatenate([values, values], axis=0)
            src[g, :, 0:1024] = dot(pick[g, 0:256, :], values).astype(BF)
            src[g, :, 1024:1280] = pack(dot(pick[g, 256:320, :], values).astype(BF))
        for ci in range(CHUNKS):
            start(which, src, dst, ci, 1)

    def arrived(which, ci, src, dst):
        rows = (slice(None), pl.ds(0, 48) if ci == 0 else pl.ds(ci * 64, 64))
        remote(src.at[rows], dst.at[rows], a2a_ss.at[which], a2a_rs.at[which, ci], me).wait_recv()

    def all_sent(which, src, dst):
        rows = (slice(None), pl.ds(0, 240))
        remote(src.at[rows], dst.at[rows], a2a_ss.at[which], a2a_rs.at[which, 0], me).wait_send()

    x_own = c * 2 + (y + dp) % 2
    for cc in range(2):
        src = index_of(y, z, x_own, cc)

        @pl.when(src != me)
        def _():
            remote(w_own, wj.at[rows_at(y * 128 + cc * 64, 64)], wx_ss.at[0], wx_rs.at[cc], me).wait_recv()

    def along_y(d):
        py = (y + d) % 4
        return py, index_of(py, z, x, c)

    def wy(d):
        _, to = along_y(d)
        return remote(wj.at[tokens(y)], wj.at[tokens(y)], wy_ss.at[d], wy_rs.at[y], to)

    for d in (1, 3, 2):
        wy(d).start()

    from_group(2, lambda g: latent4.at[rows_at(g * 128, 128)])
    dispatch(0, p_send, latent4, s1, r1)
    routing_rest()

    def quarter(n):
        return rows_at(n * 256, 256)

    def core_rows(cc):
        return rows_at(cc * 512, 512)

    def cols_of(q):
        return pl.ds(q * 256, 256)

    to_sibling = []
    swap_gc = []
    for q in range(4):
        cols = cols_of(q)
        to_sibling.append(remote(pga.at[:, cols], pgb.at[:, cols], sib_ss.at[q], sib_rs.at[q], sibling))
        for d in (1, 3, 2):
            piece = gc4.at[own_tokens, cols]
            swap_gc.append(remote(piece, piece, bgc_ss.at[d, q], bgc_rs.at[block, q], group_at(d)[1]))

    def load(src, ci):
        rows = pl.ds(ci * 64, 64)
        for g in range(4):
            xc[g * 64 : g * 64 + 64, :] = src[g, rows, 0:1024]
        xc[MAIN:ROWS, :] = unpack(jnp.concatenate([src[g, rows, 1024:1280] for g in range(4)], axis=0))

    def store(dst, ci):
        rows = pl.ds(ci * 64, 64)
        more = pack(acc[MAIN:ROWS, :].astype(BF))
        for g in range(4):
            dst[g, rows, 0:1024] = acc[g * 64 : g * 64 + 64, :].astype(BF)
            dst[g, rows, 1024:1280] = more[g * 64 : g * 64 + 64, :]

    def hidden(h):
        return rows_at(h * 512, 512)

    def forward(ci):
        arrived(0, ci, s1, r1)
        load(r1, ci)
        acc[...] = jnp.zeros_like(acc)

        def step(h, inner):
            pos = jnp.maximum(dot(xc[...], up[:, hidden(h)]), 0.0)
            relu[ci, :, hidden(h)] = pos
            acc[...] += dot((pos * pos).astype(BF), down[hidden(h), :])
            return inner

        lax.fori_loop(0, 4, step, 0)
        store(r1, ci)
        start(1, r1, b1, ci, -1)

    def backward(ci):
        arrived(2, ci, s2, r2)
        load(r2, ci)
        acc[...] = jnp.zeros_like(acc)

        def step(h, inner):
            grad = dot(xc[...], down[hidden(h), :], 1, 1) * 2.0 * relu[ci, :, hidden(h)]
            acc[...] += dot(grad.astype(BF), up[:, hidden(h)], 1, 1)
            return inner

        lax.fori_loop(0, 4, step, 0)
        store(r2, ci)
        start(3, r2, b2, ci, -1)

    def gc_sibling():
        for d in (1, 3, 2):
            py, _ = along_y(d)
            remote(wj.at[tokens(py)], wj.at[tokens(py)], wy_ss.at[d], wy_rs.at[py], me).wait_recv()
        for copy in own_go:
            copy.wait()
        for n, (dc, dz) in enumerate(others):
            m, _, _ = member(dc, dz)
            remote(go.at[tokens(m)], go.at[tokens(m)], go_ss.at[n], go_rs.at[m], me).wait_recv()
        for q in range(4):
            pga[:, cols_of(q)] = dot(go[core_rows(1 - c), :], wj[:, cols_of(q)]).astype(BF)
            to_sibling[q].start()

    def pg_copy(d, q):
        to, rep, dev = ring_at(d)
        cols = cols_of(q)
        src, dst = pgs.at[tokens(to), cols], pgr.at[tokens(ring), cols]
        return remote(src, dst, pg_ss.at[d, q], pg_rs.at[ring, q], dev, rep)

    def gc_ring():
        for q in range(4):
            cols = cols_of(q)
            to_sibling[q].wait_recv()
            pgs[:, cols] = (dot(go[core_rows(c), :], wj[:, cols]) + pgb[:, cols].astype(F32)).astype(BF)
            for d in (1, 3, 2):
                pg_copy(d, q).start()
            pgr[tokens(ring), cols] = pgs[tokens(ring), cols]

    def gc_swap():
        for q in range(4):
            cols = cols_of(q)
            for d in (1, 3, 2):
                to, _, _ = ring_at(d)
                piece = pgr.at[tokens(to), cols]
                remote(piece, piece, pg_ss.at[d, q], pg_rs.at[to, q], me).wait_recv()
            gc = sum(pgr[n * 128 : (n + 1) * 128, cols].astype(F32) for n in range(4)).astype(BF)
            gc4[own_tokens, cols] = gc
            for n in range(3):
                swap_gc[q * 3 + n].start()

    def gc_dispatch():
        for q in range(4):
            for d in (1, 3, 2):
                g, _ = group_at(d)
                piece = gc4.at[rows_at(g * 128, 128), cols_of(q)]
                remote(piece, piece, bgc_ss.at[d, q], bgc_rs.at[g, q], me).wait_recv()
        dispatch(2, pg_send, gc4, s2, r2)

    def gather_back(which, src, dst):
        for ci in range(CHUNKS):
            arrived(which, ci, src, dst)

        for g in range(4):
            extra[g * EXTRA : g * EXTRA + EXTRA, :] = unpack(dst[g, :, 1024:1280])

    def part_copy(n, d, q):
        g, to = group_at(d)
        cols = cols_of(q)
        src, dst = part_s.at[n, g, :, cols], part_r.at[n, block, :, cols]
        return remote(src, dst, sw_ss.at[n, d, q], sw_rs.at[n, block, q], to)

    def part_sums(n, weights, src):
        for q in range(4):
            cols = cols_of(q)
            for g in range(4):
                both = dot(weights[g, :, 0:256], src[g, :, cols])
                both = both + dot(weights[g, :, 256:320], extra[g * EXTRA : g * EXTRA + EXTRA, cols])
                if weights.shape[1] == 256:
                    both = both[0:128] + both[128:256]
                part_f[g * 128 : g * 128 + 128, cols] = both
                part_s[n, g, :, cols] = both.astype(BF)
            for d in (1, 3, 2):
                part_copy(n, d, q).start()

    def part_total(n, q):
        cols = cols_of(q)
        total = part_f[own_tokens, cols]
        for d in (1, 3, 2):
            g, _ = group_at(d)
            piece = part_r.at[n, g, :, cols]
            remote(piece, piece, sw_ss.at[n, d, q], sw_rs.at[n, g, q], me).wait_recv()
        for d in (1, 3, 2):
            g, _ = group_at(d)
            total = total + part_r[n, g, :, cols].astype(F32)
        return total.astype(BF)

    def combine():
        gather_back(1, r1, b1)
        part_sums(0, pg_back, b1)

    def cb_copy(m, q, ss, dev, rep):
        piece = cb.at[tokens(m), cols_of(q)]
        return remote(piece, piece, ss, cb_rs.at[m, q], dev, rep)

    def share_start():
        for q in range(4):
            cb[tokens(mine), cols_of(q)] = part_total(0, q)
            for d in (1, 3, 2):
                _, rep, dev = ring_at(d)
                cb_copy(mine, q, cb_ss.at[d, q], dev, rep).start()
            cb_copy(mine, q, cb_ss.at[0, q], sibling, dp).start()

    def share_pass():
        for q in range(4):
            for d in (1, 3, 2):
                m = c * 4 + (ring + d) % 4
                cb_copy(m, q, cb_ss.at[d, q], me, dp).wait_recv()
                cb_copy(m, q, cf_ss.at[d, q], sibling, dp).start()

    def gy(d, q):
        py, to = along_y(d)
        cols = cols_of(q)
        src, dst = gwp.at[tokens(py), cols], gwy.at[tokens(y), cols]
        return py, remote(src, dst, gy_ss.at[d, q], gy_rs.at[y, q], to)

    def weight_grad():
        for q in range(4):
            for d in range(4):
                m = (1 - c) * 4 + (ring + d) % 4
                cb_copy(m, q, cb_ss.at[d, q], me, dp).wait_recv()
            cols = cols_of(q)
            gwp[:, cols] = dot(go[...], cb[:, cols], 0, 0).astype(BF)
            for d in (1, 3, 2):
                gy(d, q)[1].start()
            gwy[tokens(y), cols] = gwp[tokens(y), cols]

    def mix_all():
        def mix(part, carry):
            cols = tokens(part)
            mps[:, cols] = dot(cb[...], wj[cols, :], 1, 1).astype(BF)
            for n, (dc, dz) in enumerate(others):
                m, rep, to = member(dc, dz)
                src, dst = mps.at[tokens(m), cols], mixed.at[:, feats(mine, part)]
                remote(src, dst, mx_ss.at[n], mx_rs.at[mine], to, rep).start()
            mixed[:, feats(mine, part)] = mps[tokens(mine), cols]
            return carry

        lax.fori_loop(0, 4, mix, 0)

    up_copy.wait()
    down_copy.wait()
    gc_sibling()
    gc_ring()
    forward(0)
    gc_swap()
    forward(1)
    gc_dispatch()
    forward(2)
    forward(3)
    backward(0)
    backward(1)
    combine()
    backward(2)
    share_start()
    backward(3)
    share_pass()
    weight_grad()
    mix_all()

    for q in range(4):
        for d in (1, 3, 2):
            py, _ = along_y(d)
            piece = gwy.at[tokens(py), cols_of(q)]
            remote(piece, piece, gy_ss.at[d, q], gy_rs.at[py, q], me).wait_recv()
    gws[...] = sum(gwy[n * 128 : (n + 1) * 128, :].astype(F32) for n in range(4)).astype(BF)
    x_slot = rows_at(x * 64, 64)

    def gx(cc):
        to = index_of(y, z, x_own, cc)
        return to, remote(gws.at[pl.ds(cc * 64, 64)], gwx.at[x_slot], gx_ss.at[cc], gx_rs.at[x], to)

    for cc in range(2):
        to, copy = gx(cc)

        @pl.when(to != me)
        def _():
            copy.start()

        @pl.when(to == me)
        def _():
            gwx[x_slot, :] = gws[cc * 64 : cc * 64 + 64, :]

    gather_back(3, r2, b2)
    part_sums(1, p_back, b2)

    exchange = pltpu.make_async_remote_copy(
        dps, dpr, dp_sem.at[0], dp_sem.at[1], device_id=(1 - dp, me), device_id_type=MESH
    )

    @pl.when(sends_w)
    def _():
        for px in range(4):
            src = index_of(y, z, px, half)

            @pl.when(src != me)
            def _():
                rows = pl.ds(px * 64, 64)
                remote(gwx.at[rows], gwx.at[rows], gx_ss.at[0], gx_rs.at[px], me).wait_recv()

        dps[...] = sum(gwx[n * 64 : (n + 1) * 64, :].astype(F32) for n in range(4)).astype(BF)
        exchange.start()
        grad_w[...] = dps[...].astype(F32)

    for q in range(4):
        grad_latent[:, cols_of(q)] = part_total(1, q)

    @pl.when(sends_w)
    def _():
        exchange.wait_send()

    @pl.when(jnp.logical_not(sends_w))
    def _():
        exchange.wait_recv()
        grad_w[...] = dpr[...].astype(F32)

    for n, (dc, dz) in enumerate(others):
        m, _, _ = member(dc, dz)
        whole = remote(mps.at[tokens(m)], mps.at[tokens(m)], mx_ss.at[n], mx_rs.at[m], me)
        whole.wait_recv()
        whole.wait_send()
        remote(go.at[tokens(m)], go.at[tokens(m)], go_ss.at[n], go_rs.at[m], me).wait_send()
    for copy in swap + swap_gc + to_sibling:
        copy.wait_send()
    for d in range(4):
        to, copy = wx(d)
        go_on = jnp.logical_and(sends_w, to != me)

        @pl.when(go_on)
        def _():
            copy.wait_send()

        for q in range(4):
            cb_copy(mine, q, cb_ss.at[d, q], me, dp).wait_send()
            if d:
                gy(d, q)[1].wait_send()
                cb_copy(mine, q, cf_ss.at[d, q], me, dp).wait_send()
        if d:
            wy(d).wait_send()
            for q in range(4):
                pg_copy(d, q).wait_send()
                part_copy(0, d, q).wait_send()
                part_copy(1, d, q).wait_send()
    for cc in range(2):
        to, copy = gx(cc)

        @pl.when(to != me)
        def _():
            copy.wait_send()

    all_sent(0, s1, r1)
    all_sent(1, r1, b1)
    all_sent(2, s2, r2)
    all_sent(3, r2, b2)


def on_device(latent, routes, gates, grad_out, w_out_t, expert_up, expert_down):
    vm = pl.BlockSpec(memory_space=pltpu.VMEM)
    hbm = pl.BlockSpec(memory_space=pl.ANY)

    def dma(*shape):
        return pltpu.SemaphoreType.DMA(shape)

    def bf(*shape):
        return pltpu.VMEM(shape, BF)

    scratch = [bf(4, 256, 1280)] * 6 + [
        bf(1024, 2048), bf(2048, 1024), pltpu.VMEM((CHUNKS, ROWS, 2048), F32),
        bf(ROWS, 1024), pltpu.VMEM((ROWS, 1024), F32), bf(256, 1024),
        pltpu.VMEM((4, 8, 128), I32), pltpu.VMEM((4, 8, 128), F32), bf(512, 1024), bf(512, 1024),
        pltpu.VMEM((512, 1024), F32), bf(2, 4, 128, 1024), bf(2, 4, 128, 1024),
        bf(1024, 512), bf(512, 1024), bf(512, 1024), bf(512, 1024), bf(512, 1024), bf(512, 1024),
        bf(1024, 1024), bf(1024, 512), bf(512, 1024), bf(512, 1024), bf(128, 1024), bf(256, 1024),
        bf(64, 1024), bf(64, 1024),
        pltpu.VMEM((4, 128, 128), F32), pltpu.VMEM((4, 128, 128), F32), bf(256, 256), bf(256, 256),
        bf(4, 320, 128), bf(4, 320, 256), bf(4, 128, 320), bf(4, 256, 320),
        dma(4), dma(4, 4), dma(3, 4), dma(3, 4), dma(2, 4, 4), dma(2, 4, 4), dma(4), dma(2), dma(4), dma(4), dma(7), dma(8),
        dma(4), dma(4), dma(4, 4), dma(4, 4), dma(4, 4), dma(4, 4), dma(4, 4), dma(8, 4), dma(4, 4), dma(7), dma(8),
        dma(4, 4), dma(4, 4), dma(2), dma(4), dma(2), dma(6),
    ]
    return pl.pallas_call(
        kernel,
        out_shape=(
            jax.ShapeDtypeStruct((128, 4096), BF),
            jax.ShapeDtypeStruct((128, 1024), BF),
            jax.ShapeDtypeStruct((64, 1024), F32),
        ),
        in_specs=[vm, vm, vm, vm, hbm, hbm, hbm],
        out_specs=(vm, vm, vm),
        scratch_shapes=scratch,
        compiler_params=pltpu.CompilerParams(
            collective_id=0, has_side_effects=True, vmem_limit_bytes=63 * 1024 * 1024
        ),
        cost_estimate=pl.CostEstimate(flops=25_000_000_000, bytes_accessed=20_000_000, transcendentals=0),
        name="moe_layer",
    )(latent, routes.T, gates.T, w_out_t, grad_out, expert_up, expert_down)


def solution(mesh):
    rows = P(("dp", "expert"), None)
    return jax.shard_map(
        on_device,
        mesh=mesh,
        in_specs=(rows, rows, rows, rows, P("expert", None), P("expert", None, None), P("expert", None, None)),
        out_specs=(rows, rows, P("expert", None)),
        check_vma=False,
    )
```

```python
import jax
import jax.numpy as jnp
from jax import lax
from jax.experimental import pallas as pl
from jax.experimental.pallas import tpu as pltpu
from jax.sharding import PartitionSpec as P

BF = jnp.bfloat16
F32 = jnp.float32
I32 = jnp.int32
MESH = pl.DeviceIdType.MESH
STRIDE = 5
CHUNKS = 4
PER = 4
MAIN = 256
EXTRA = 64
ROWS = 320


def iota(shape, dim):
    return lax.broadcasted_iota(I32, shape, dim)


def dot(a, b, ca=1, cb=0):
    return lax.dot_general(a, b, (((ca,), (cb,)), ((), ())), preferred_element_type=F32)


def index_of(y, z, x, c):
    return ((y * 2 + z) * 4 + x) * 2 + c


def rows_at(start, size):
    return pl.ds(pl.multiple_of(start, size), size)


def kernel(
    latent, routes, gates, w_own, grad_out, up_hbm, down_hbm,
    mixed, grad_latent, grad_w,
    s1, r1, b1, s2, r2, b2, up, down, relu, xc, acc, extra,
    routes4, gates4, latent4, gc4, part_f, part_s, part_r,
    go, wj, pga, pgb, pgs, pgr, cb, mps, gwp, gwy, gws, gwx, gwb, gwbs, gwby, dps, dpr,
    slots, gate_tab, sel, selt, p_send, pg_send, p_back, pg_back,
    a2a_ss, a2a_rs, grp_ss, grp_rs, sw_ss, sw_rs, wx_ss, wx_rs, wb_ss, wb_rs, wbx_ss, wbx_rs, wy_ss, wy_rs, go_ss, go_rs,
    sib_ss, sib_rs, bgc_ss, bgc_rs, pg_ss, pg_rs, cb_ss, cb_rs, cf_ss, mx_ss, mx_rs,
    gy_ss, gy_rs, gb_ss, gb_rs, gby_ss, gby_rs, gx_ss, gx_rs, dp_sem, loc,
):
    dp = lax.axis_index("dp")
    me = lax.axis_index("expert")
    y, z, x, c = me // 16, (me // 8) % 2, (me // 2) % 4, me % 2
    ring = dp * 2 + z
    mine = c * 4 + ring
    sibling = index_of(y, z, x, 1 - c)
    block = x * (1 - c) + y * c
    half, parity = x // 2, x % 2

    def partner(k, sign):
        off = (STRIDE * k) % 16
        along, hop, flip = off // 4, (off // 2) % 2, off % 2
        pc = (c + flip) % 2
        sender, expert = (c, pc) if sign > 0 else (pc, c)
        pr = (ring + sign * hop * (1 - 2 * expert) + 4) % 4
        py, px = (y + sign * along * (1 - sender) + 4) % 4, (x + sign * along * sender + 4) % 4
        return pr // 2, index_of(py, pr % 2, px, pc)

    def group_at(d):
        to = (block + d) % 4
        return to, index_of(y + c * (to - y), z, x + (1 - c) * (to - x), c)

    def ring_at(d):
        to = (ring + d) % 4
        return to, to // 2, index_of(y, to % 2, x, c)

    def member(dc, dz):
        to, cc = (ring + dz) % 4, (c + dc) % 2
        return cc * 4 + to, to // 2, index_of(y, to % 2, x, cc)

    others = [(dc, dz) for dz in (1, 3, 2, 0) for dc in (0, 1) if dc or dz]

    def remote(src, dst, ss, rs, dev, rep=None):
        rep = dp if rep is None else rep
        return pltpu.make_async_remote_copy(src, dst, ss, rs, device_id=(rep, dev), device_id_type=MESH)

    barrier = pltpu.get_barrier_semaphore()

    def signal(rep, dev):
        pl.semaphore_signal(barrier, inc=1, device_id=(rep, dev), device_id_type=MESH)

    def greet(k, carry):
        for sign in (1, -1):
            signal(*partner(k, sign))
        return carry

    lax.fori_loop(1, 16, greet, 0)
    for dc, dz in others:
        _, rep, to = member(dc, dz)
        signal(rep, to)
    for d in range(1, 8):
        near = (x * 2 + c + d) % 8
        signal(dp, index_of(y, z, near // 2, near % 2))
    for d in range(1, 4):
        for cc in range(2):
            signal(dp, index_of((y + d) % 4, z, x, cc))
    up_copy = pltpu.make_async_copy(up_hbm.at[0], up, loc.at[0])
    down_copy = pltpu.make_async_copy(down_hbm.at[0], down, loc.at[1])
    up_copy.start()
    down_copy.start()
    own_tokens = rows_at(block * 128, 128)
    routes4[block] = routes[...]
    gates4[block] = gates[...]
    latent4[own_tokens, :] = latent[...]

    i, j = iota((256, 256), 0), iota((256, 256), 1)
    sel[...] = jnp.where(((i & 63) >> 2) * 16 + (i >> 6) * 4 + (i & 3) == j, 1.0, 0.0).astype(BF)
    selt[...] = jnp.where(((j & 63) >> 2) * 16 + (j >> 6) * 4 + (j & 3) == i, 1.0, 0.0).astype(BF)

    pl.semaphore_wait(barrier, 50)

    sends_w = parity == (y + dp) % 2
    w_slot = rows_at(y * 128 + c * 64, 64)

    near_half, far_half = pl.ds(0, 512), pl.ds(512, 512)

    def wx(d):
        to = index_of(y, z, (x + d) % 4, half)
        return to, remote(w_own.at[:, near_half], wj.at[w_slot, near_half], wx_ss.at[d], wx_rs.at[c], to)

    def wb(d):
        to = index_of((y + d) % 4, z, x, half)
        return to, remote(w_own.at[:, far_half], wj.at[w_slot, far_half], wb_ss.at[d], wb_rs.at[y * 2 + c], to)

    for d in (1, 3, 2, 0):
        for to, copy in (wx(d), wb(d)):

            @pl.when(jnp.logical_and(sends_w, to != me))
            def _():
                copy.start()

    @pl.when(jnp.logical_and(sends_w, c == half))
    def _():
        wj[w_slot, :] = w_own[...]

    swap = []
    for d in (1, 3, 2):
        _, to = group_at(d)
        swap.append(remote(routes, routes4.at[block], grp_ss.at[0, d], grp_rs.at[0, block], to))
        swap.append(remote(gates, gates4.at[block], grp_ss.at[1, d], grp_rs.at[1, block], to))
    for d in (1, 3, 2):
        _, to = group_at(d)
        swap.append(remote(latent, latent4.at[own_tokens], grp_ss.at[2, d], grp_rs.at[2, block], to))
    for copy in swap:
        copy.start()

    def from_group(n, dst):
        for d in (1, 3, 2):
            g, _ = group_at(d)
            remote(dst(g), dst(g), grp_ss.at[n, d], grp_rs.at[n, g], me).wait_recv()

    def feats(m, part):
        to = m % 4
        return rows_at(part * 1024 + (to % 2) * 512 + (m // 4) * 256 + ((part + to // 2) % 2) * 128, 128)

    def tokens(m):
        return rows_at(m * 128, 128)

    own_go = []
    for part in range(4):
        cols = pl.ds(part * 128, 128)
        for n, (dc, dz) in enumerate(others):
            m, rep, to = member(dc, dz)
            remote(grad_out.at[:, feats(m, part)], go.at[tokens(mine), cols], go_ss.at[n], go_rs.at[mine], to, rep).start()
        copy = pltpu.make_async_copy(grad_out.at[:, feats(mine, part)], go.at[tokens(mine), cols], loc.at[2 + part])
        copy.start()
        own_go.append(copy)

    from_group(0, lambda g: routes4.at[g])
    from_group(1, lambda g: gates4.at[g])

    def names(j):
        return jnp.where(j < 256, j >> 4, (j - 256) >> 2), jnp.where(j < 256, j & 15, 16 + (j & 3)) + 1

    def expert_of(k):
        off = (STRIDE * k) & 15
        along, hop, pc = off >> 2, (off >> 1) & 1, (c + off) & 1
        py, px = (y + along * (1 - c)) & 3, (x + along * c) & 3
        return ((py * 2 + ((z + hop) & 1)) * 4 + px) * 2 + pc

    k_row, s_row = names(iota((320, 128), 0))
    k_col, s_col = names(iota((128, 320), 1))
    spread_t = jnp.where(expert_of(k_row) == iota((320, 128), 1), 1.0, 0.0).astype(BF)
    spread = jnp.where(expert_of(k_col) == iota((128, 320), 0), 1.0, 0.0).astype(BF)
    earlier = jnp.where(iota((128, 128), 0) < iota((128, 128), 1), 1.0, 0.0).astype(BF)

    def table(g):
        hot = jnp.zeros((128, 128), F32)
        gate = jnp.zeros((128, 128), F32)
        for k in range(8):
            hit = routes4[g, k : k + 1, :] == iota((128, 128), 0)
            hot = hot + jnp.where(hit, 1.0, 0.0)
            gate = gate + jnp.where(hit, gates4[g, k : k + 1, :], 0.0)
        slot = jnp.where(hot > 0.5, dot(hot.astype(BF), earlier) + 1.0, 0.0)
        return slot, gate

    for g in range(4):
        slots[g], gate_tab[g] = table(g)
        hit = dot(spread_t, slots[g].astype(BF)) == s_row.astype(F32)
        p_send[g] = jnp.where(hit, 1.0, 0.0).astype(BF)

    def routing_rest():
        for g in range(4):
            gate_hi = gate_tab[g].astype(BF).astype(F32)
            gate_lo = gate_tab[g] - gate_hi
            hit = p_send[g].astype(F32) > 0.5
            pg_send[g, :, 0:128] = jnp.where(hit, dot(spread_t, gate_hi.astype(BF)), 0.0).astype(BF)
            pg_send[g, :, 128:256] = jnp.where(hit, dot(spread_t, gate_lo.astype(BF)), 0.0).astype(BF)
            hit = dot(slots[g].T.astype(BF), spread) == s_col.astype(F32)
            p_back[g] = jnp.where(hit, 1.0, 0.0).astype(BF)
            pg_back[g, 0:128, :] = jnp.where(hit, dot(gate_hi.T.astype(BF), spread), 0.0).astype(BF)
            pg_back[g, 128:256, :] = jnp.where(hit, dot(gate_lo.T.astype(BF), spread), 0.0).astype(BF)

    def unpack(packed):
        rows = dot(sel[...], packed).astype(BF)
        return jnp.concatenate([rows[q * 64 : (q + 1) * 64] for q in range(4)], axis=1)

    def pack(rows):
        stacked = jnp.concatenate([rows[:, q * 256 : (q + 1) * 256] for q in range(4)], axis=0)
        return dot(selt[...], stacked).astype(BF)

    def message(k):
        return rows_at(k * 16, 16)

    def start(which, src, dst, ci, sign):
        def body(k, carry):
            rep, to = partner(k, sign)
            piece = (slice(None), message(k))
            remote(src.at[piece], dst.at[piece], a2a_ss.at[which], a2a_rs.at[which, ci], to, rep).start()
            return carry

        lax.fori_loop(max(ci * PER, 1), ci * PER + PER, body, 0)
        if ci == 0:
            dst[:, 0:16, :] = src[:, 0:16, :]

    def dispatch(which, pick, source, src, dst):
        for g in range(4):
            values = source[g * 128 : g * 128 + 128, :]
            if pick.shape[2] == 256:
                values = jnp.concatenate([values, values], axis=0)
            src[g, :, 0:1024] = dot(pick[g, 0:256, :], values).astype(BF)
            src[g, :, 1024:1280] = pack(dot(pick[g, 256:320, :], values).astype(BF))
        for ci in range(CHUNKS):
            start(which, src, dst, ci, 1)

    def arrived(which, ci, src, dst):
        rows = (slice(None), pl.ds(0, 48) if ci == 0 else pl.ds(ci * 64, 64))
        remote(src.at[rows], dst.at[rows], a2a_ss.at[which], a2a_rs.at[which, ci], me).wait_recv()

    def all_sent(which, src, dst):
        rows = (slice(None), pl.ds(0, 240))
        remote(src.at[rows], dst.at[rows], a2a_ss.at[which], a2a_rs.at[which, 0], me).wait_send()

    x_own = c * 2 + (y + dp) % 2
    for cc in range(2):
        src = index_of(y, z, x_own, cc)

        @pl.when(src != me)
        def _():
            piece = wj.at[rows_at(y * 128 + cc * 64, 64), near_half]
            remote(piece, piece, wx_ss.at[0], wx_rs.at[cc], me).wait_recv()

    def along_y(d):
        py = (y + d) % 4
        return py, index_of(py, z, x, c)

    def wy(d):
        _, to = along_y(d)
        piece = wj.at[tokens(y), near_half]
        return remote(piece, piece, wy_ss.at[d], wy_rs.at[y], to)

    for d in (1, 3, 2):
        wy(d).start()

    def own_y(n):
        return (x + dp) % 2 + 2 * n

    def wbx(n, d):
        py = own_y(n)
        piece = wj.at[tokens(py), far_half]
        return remote(piece, piece, wbx_ss.at[n, d], wbx_rs.at[py], index_of(y, z, (x + d) % 4, c))

    def far_source(py):
        return 2 * c + (py + dp) % 2

    @pl.when(c == half)
    def _():
        for n in range(2):
            py = own_y(n)
            for cc in range(2):

                @pl.when(index_of(py, z, x, cc) != me)
                def _():
                    piece = wj.at[rows_at(py * 128 + cc * 64, 64), far_half]
                    remote(piece, piece, wb_ss.at[0], wb_rs.at[py * 2 + cc], me).wait_recv()

            for d in (1, 3, 2):
                wbx(n, d).start()

    from_group(2, lambda g: latent4.at[rows_at(g * 128, 128)])
    dispatch(0, p_send, latent4, s1, r1)
    routing_rest()

    def quarter(n):
        return rows_at(n * 256, 256)

    def core_rows(cc):
        return rows_at(cc * 512, 512)

    def cols_of(q):
        return pl.ds(q * 256, 256)

    to_sibling = []
    swap_gc = []
    for q in range(4):
        cols = cols_of(q)
        to_sibling.append(remote(pga.at[:, cols], pgb.at[:, cols], sib_ss.at[q], sib_rs.at[q], sibling))
        for d in (1, 3, 2):
            piece = gc4.at[own_tokens, cols]
            swap_gc.append(remote(piece, piece, bgc_ss.at[d, q], bgc_rs.at[block, q], group_at(d)[1]))

    def load(src, ci):
        rows = pl.ds(ci * 64, 64)
        for g in range(4):
            xc[g * 64 : g * 64 + 64, :] = src[g, rows, 0:1024]
        xc[MAIN:ROWS, :] = unpack(jnp.concatenate([src[g, rows, 1024:1280] for g in range(4)], axis=0))

    def store(dst, ci):
        rows = pl.ds(ci * 64, 64)
        more = pack(acc[MAIN:ROWS, :].astype(BF))
        for g in range(4):
            dst[g, rows, 0:1024] = acc[g * 64 : g * 64 + 64, :].astype(BF)
            dst[g, rows, 1024:1280] = more[g * 64 : g * 64 + 64, :]

    def hidden(h):
        return rows_at(h * 512, 512)

    def forward(ci):
        arrived(0, ci, s1, r1)
        load(r1, ci)
        acc[...] = jnp.zeros_like(acc)

        def step(h, inner):
            pos = jnp.maximum(dot(xc[...], up[:, hidden(h)]), 0.0)
            relu[ci, :, hidden(h)] = pos
            acc[...] += dot((pos * pos).astype(BF), down[hidden(h), :])
            return inner

        lax.fori_loop(0, 4, step, 0)
        store(r1, ci)
        start(1, r1, b1, ci, -1)

    def backward(ci):
        arrived(2, ci, s2, r2)
        load(r2, ci)
        acc[...] = jnp.zeros_like(acc)

        def step(h, inner):
            grad = dot(xc[...], down[hidden(h), :], 1, 1) * 2.0 * relu[ci, :, hidden(h)]
            acc[...] += dot(grad.astype(BF), up[:, hidden(h)], 1, 1)
            return inner

        lax.fori_loop(0, 4, step, 0)
        store(r2, ci)
        start(3, r2, b2, ci, -1)

    def gc_sibling():
        for d in (1, 3, 2):
            py, _ = along_y(d)
            piece = wj.at[tokens(py), near_half]
            remote(piece, piece, wy_ss.at[d], wy_rs.at[py], me).wait_recv()
        for py in range(4):

            @pl.when(x != far_source(py))
            def _():
                piece = wj.at[tokens(py), far_half]
                remote(piece, piece, wbx_ss.at[0, 1], wbx_rs.at[py], me).wait_recv()

        for copy in own_go:
            copy.wait()
        for n, (dc, dz) in enumerate(others):
            m, _, _ = member(dc, dz)
            remote(go.at[tokens(m)], go.at[tokens(m)], go_ss.at[n], go_rs.at[m], me).wait_recv()
        for q in range(4):
            pga[:, cols_of(q)] = dot(go[core_rows(1 - c), :], wj[:, cols_of(q)]).astype(BF)
            to_sibling[q].start()

    def pg_copy(d, q):
        to, rep, dev = ring_at(d)
        cols = cols_of(q)
        src, dst = pgs.at[tokens(to), cols], pgr.at[tokens(ring), cols]
        return remote(src, dst, pg_ss.at[d, q], pg_rs.at[ring, q], dev, rep)

    def gc_ring():
        for q in range(4):
            cols = cols_of(q)
            to_sibling[q].wait_recv()
            pgs[:, cols] = (dot(go[core_rows(c), :], wj[:, cols]) + pgb[:, cols].astype(F32)).astype(BF)
            for d in (1, 3, 2):
                pg_copy(d, q).start()
            pgr[tokens(ring), cols] = pgs[tokens(ring), cols]

    def gc_swap():
        for q in range(4):
            cols = cols_of(q)
            for d in (1, 3, 2):
                to, _, _ = ring_at(d)
                piece = pgr.at[tokens(to), cols]
                remote(piece, piece, pg_ss.at[d, q], pg_rs.at[to, q], me).wait_recv()
            gc = sum(pgr[n * 128 : (n + 1) * 128, cols].astype(F32) for n in range(4)).astype(BF)
            gc4[own_tokens, cols] = gc
            for n in range(3):
                swap_gc[q * 3 + n].start()

    def gc_dispatch():
        for q in range(4):
            for d in (1, 3, 2):
                g, _ = group_at(d)
                piece = gc4.at[rows_at(g * 128, 128), cols_of(q)]
                remote(piece, piece, bgc_ss.at[d, q], bgc_rs.at[g, q], me).wait_recv()
        dispatch(2, pg_send, gc4, s2, r2)

    def gather_back(which, src, dst):
        for ci in range(CHUNKS):
            arrived(which, ci, src, dst)

        for g in range(4):
            extra[g * EXTRA : g * EXTRA + EXTRA, :] = unpack(dst[g, :, 1024:1280])

    def part_copy(n, d, q):
        g, to = group_at(d)
        cols = cols_of(q)
        src, dst = part_s.at[n, g, :, cols], part_r.at[n, block, :, cols]
        return remote(src, dst, sw_ss.at[n, d, q], sw_rs.at[n, block, q], to)

    def part_sums(n, weights, src):
        for q in range(4):
            cols = cols_of(q)
            for g in range(4):
                both = dot(weights[g, :, 0:256], src[g, :, cols])
                both = both + dot(weights[g, :, 256:320], extra[g * EXTRA : g * EXTRA + EXTRA, cols])
                if weights.shape[1] == 256:
                    both = both[0:128] + both[128:256]
                part_f[g * 128 : g * 128 + 128, cols] = both
                part_s[n, g, :, cols] = both.astype(BF)
            for d in (1, 3, 2):
                part_copy(n, d, q).start()

    def part_total(n, q):
        cols = cols_of(q)
        total = part_f[own_tokens, cols]
        for d in (1, 3, 2):
            g, _ = group_at(d)
            piece = part_r.at[n, g, :, cols]
            remote(piece, piece, sw_ss.at[n, d, q], sw_rs.at[n, g, q], me).wait_recv()
        for d in (1, 3, 2):
            g, _ = group_at(d)
            total = total + part_r[n, g, :, cols].astype(F32)
        return total.astype(BF)

    def combine():
        gather_back(1, r1, b1)
        part_sums(0, pg_back, b1)

    def cb_copy(m, q, ss, dev, rep):
        piece = cb.at[tokens(m), cols_of(q)]
        return remote(piece, piece, ss, cb_rs.at[m, q], dev, rep)

    def share_start():
        for q in range(4):
            cb[tokens(mine), cols_of(q)] = part_total(0, q)
            for d in (1, 3, 2):
                _, rep, dev = ring_at(d)
                cb_copy(mine, q, cb_ss.at[d, q], dev, rep).start()
            cb_copy(mine, q, cb_ss.at[0, q], sibling, dp).start()

    def share_pass():
        for q in range(4):
            for d in (1, 3, 2):
                m = c * 4 + (ring + d) % 4
                cb_copy(m, q, cb_ss.at[d, q], me, dp).wait_recv()
                cb_copy(m, q, cf_ss.at[d, q], sibling, dp).start()

    def gy(d, q):
        py, to = along_y(d)
        cols = cols_of(q)
        src, dst = gwp.at[tokens(py), cols], gwy.at[tokens(y), cols]
        return py, remote(src, dst, gy_ss.at[d, q], gy_rs.at[y, q], to)

    def far_cols(q):
        return pl.ds(q * 256 - 512, 256)

    def gb(py, q):
        to = index_of(y, z, far_source(py), c)
        src, dst = gwp.at[tokens(py), cols_of(q)], gwb.at[py // 2, tokens(x), far_cols(q)]
        return to, remote(src, dst, gb_ss.at[py, q - 2], gb_rs.at[py // 2, x, q - 2], to)

    def weight_grad():
        for q in range(4):
            for d in range(4):
                m = (1 - c) * 4 + (ring + d) % 4
                cb_copy(m, q, cb_ss.at[d, q], me, dp).wait_recv()
            cols = cols_of(q)
            gwp[:, cols] = dot(go[...], cb[:, cols], 0, 0).astype(BF)
            if q < 2:
                for d in (1, 3, 2):
                    gy(d, q)[1].start()
                gwy[tokens(y), cols] = gwp[tokens(y), cols]
            else:
                for py in range(4):
                    to, copy = gb(py, q)

                    @pl.when(to != me)
                    def _():
                        copy.start()

                    @pl.when(to == me)
                    def _():
                        gwb[py // 2, tokens(x), far_cols(q)] = gwp[tokens(py), cols]

    def mix_all():
        def mix(part, carry):
            cols = tokens(part)
            mps[:, cols] = dot(cb[...], wj[cols, :], 1, 1).astype(BF)
            for n, (dc, dz) in enumerate(others):
                m, rep, to = member(dc, dz)
                src, dst = mps.at[tokens(m), cols], mixed.at[:, feats(mine, part)]
                remote(src, dst, mx_ss.at[n], mx_rs.at[mine], to, rep).start()
            mixed[:, feats(mine, part)] = mps[tokens(mine), cols]
            return carry

        lax.fori_loop(0, 4, mix, 0)

    up_copy.wait()
    down_copy.wait()
    gc_sibling()
    gc_ring()
    forward(0)
    forward(1)
    forward(2)
    gc_swap()
    forward(3)
    gc_dispatch()
    backward(0)
    backward(1)
    combine()
    backward(2)
    backward(3)
    share_start()
    share_pass()
    weight_grad()
    mix_all()

    for q in range(2):
        for d in (1, 3, 2):
            py, _ = along_y(d)
            piece = gwy.at[tokens(py), cols_of(q)]
            remote(piece, piece, gy_ss.at[d, q], gy_rs.at[py, q], me).wait_recv()
    gws[...] = sum(gwy[n * 128 : (n + 1) * 128, 0:512].astype(F32) for n in range(4)).astype(BF)
    x_slot = rows_at(x * 64, 64)

    def gx(cc):
        to = index_of(y, z, x_own, cc)
        return to, remote(gws.at[pl.ds(cc * 64, 64)], gwx.at[x_slot], gx_ss.at[cc], gx_rs.at[x], to)

    for cc in range(2):
        to, copy = gx(cc)

        @pl.when(to != me)
        def _():
            copy.start()

        @pl.when(to == me)
        def _():
            gwx[x_slot, :] = gws[cc * 64 : cc * 64 + 64, :]

    def gby(n, cc):
        to = index_of(own_y(n), z, x, cc)
        src = gwbs.at[n, pl.ds(cc * 64, 64)]
        return to, remote(src, gwby.at[rows_at(y * 64, 64)], gby_ss.at[n, cc], gby_rs.at[y], to)

    @pl.when(c == half)
    def _():
        for n in range(2):
            for px in range(4):

                @pl.when(x != px)
                def _():
                    for q in range(2):
                        piece = gwb.at[n, pl.ds(px * 128, 128), cols_of(q)]
                        remote(piece, piece, gb_ss.at[0, q], gb_rs.at[n, px, q], me).wait_recv()

            gwbs[n] = sum(gwb[n, px * 128 : px * 128 + 128, :].astype(F32) for px in range(4)).astype(BF)
            for cc in range(2):
                to, copy = gby(n, cc)

                @pl.when(to != me)
                def _():
                    copy.start()

                @pl.when(to == me)
                def _():
                    gwby[rows_at(y * 64, 64), :] = gwbs[n, cc * 64 : cc * 64 + 64, :]


    gather_back(3, r2, b2)
    part_sums(1, p_back, b2)

    exchange = pltpu.make_async_remote_copy(
        dps, dpr, dp_sem.at[0], dp_sem.at[1], device_id=(1 - dp, me), device_id_type=MESH
    )

    @pl.when(sends_w)
    def _():
        for px in range(4):
            src = index_of(y, z, px, half)

            @pl.when(src != me)
            def _():
                rows = pl.ds(px * 64, 64)
                remote(gwx.at[rows], gwx.at[rows], gx_ss.at[0], gx_rs.at[px], me).wait_recv()

        for py in range(4):

            @pl.when(index_of(py, z, x, half) != me)
            def _():
                rows = pl.ds(py * 64, 64)
                remote(gwby.at[rows], gwby.at[rows], gby_ss.at[0, 0], gby_rs.at[py], me).wait_recv()

        dps[:, 0:512] = sum(gwx[n * 64 : (n + 1) * 64, :].astype(F32) for n in range(4)).astype(BF)
        dps[:, 512:1024] = sum(gwby[n * 64 : (n + 1) * 64, :].astype(F32) for n in range(4)).astype(BF)
        exchange.start()
        grad_w[...] = dps[...].astype(F32)

    for q in range(4):
        grad_latent[:, cols_of(q)] = part_total(1, q)

    @pl.when(sends_w)
    def _():
        exchange.wait_send()

    @pl.when(jnp.logical_not(sends_w))
    def _():
        exchange.wait_recv()
        grad_w[...] = dpr[...].astype(F32)

    for n, (dc, dz) in enumerate(others):
        m, _, _ = member(dc, dz)
        whole = remote(mps.at[tokens(m)], mps.at[tokens(m)], mx_ss.at[n], mx_rs.at[m], me)
        whole.wait_recv()
        whole.wait_send()
        remote(go.at[tokens(m)], go.at[tokens(m)], go_ss.at[n], go_rs.at[m], me).wait_send()
    for copy in swap + swap_gc + to_sibling:
        copy.wait_send()
    for d in range(4):
        for to, copy in (wx(d), wb(d)):

            @pl.when(jnp.logical_and(sends_w, to != me))
            def _():
                copy.wait_send()

        for q in range(2):
            to, copy = gb(d, q + 2)

            @pl.when(to != me)
            def _():
                copy.wait_send()

        for q in range(4):
            cb_copy(mine, q, cb_ss.at[d, q], me, dp).wait_send()
            if d:
                if q < 2:
                    gy(d, q)[1].wait_send()
                cb_copy(mine, q, cf_ss.at[d, q], me, dp).wait_send()
        if d:
            wy(d).wait_send()
            for q in range(4):
                pg_copy(d, q).wait_send()
                part_copy(0, d, q).wait_send()
                part_copy(1, d, q).wait_send()
    @pl.when(c == half)
    def _():
        for n in range(2):
            for d in (1, 2, 3):
                wbx(n, d).wait_send()
            for cc in range(2):
                to, copy = gby(n, cc)

                @pl.when(to != me)
                def _():
                    copy.wait_send()

    for cc in range(2):
        to, copy = gx(cc)

        @pl.when(to != me)
        def _():
            copy.wait_send()

    all_sent(0, s1, r1)
    all_sent(1, r1, b1)
    all_sent(2, s2, r2)
    all_sent(3, r2, b2)


def settle(mixed_in, latent_in, w_in, mixed, grad_latent, grad_w, sems):
    pairs = ((mixed_in, mixed), (latent_in, grad_latent), (w_in, grad_w))
    copies = [pltpu.make_async_copy(src, dst, sems.at[n]) for n, (src, dst) in enumerate(pairs)]
    for copy in copies:
        copy.start()
    for copy in copies:
        copy.wait()


def on_device(latent, routes, gates, grad_out, w_out_t, expert_up, expert_down):
    vm = pl.BlockSpec(memory_space=pltpu.VMEM)
    hbm = pl.BlockSpec(memory_space=pl.ANY)

    def dma(*shape):
        return pltpu.SemaphoreType.DMA(shape)

    def bf(*shape):
        return pltpu.VMEM(shape, BF)

    scratch = [bf(4, 256, 1280)] * 6 + [
        bf(1024, 2048), bf(2048, 1024), pltpu.VMEM((CHUNKS, ROWS, 2048), F32),
        bf(ROWS, 1024), pltpu.VMEM((ROWS, 1024), F32), bf(256, 1024),
        pltpu.VMEM((4, 8, 128), I32), pltpu.VMEM((4, 8, 128), F32), bf(512, 1024), bf(512, 1024),
        pltpu.VMEM((512, 1024), F32), bf(2, 4, 128, 1024), bf(2, 4, 128, 1024),
        bf(1024, 512), bf(512, 1024), bf(512, 1024), bf(512, 1024), bf(512, 1024), bf(512, 1024),
        bf(1024, 1024), bf(1024, 512), bf(512, 1024), bf(512, 512), bf(128, 512), bf(256, 512), bf(2, 512, 512), bf(2, 128, 512), bf(256, 512),
        bf(64, 1024), bf(64, 1024),
        pltpu.VMEM((4, 128, 128), F32), pltpu.VMEM((4, 128, 128), F32), bf(256, 256), bf(256, 256),
        bf(4, 320, 128), bf(4, 320, 256), bf(4, 128, 320), bf(4, 256, 320),
        dma(4), dma(4, 4), dma(3, 4), dma(3, 4), dma(2, 4, 4), dma(2, 4, 4), dma(4), dma(2), dma(4), dma(8), dma(2, 4), dma(4), dma(4), dma(4), dma(7), dma(8),
        dma(4), dma(4), dma(4, 4), dma(4, 4), dma(4, 4), dma(4, 4), dma(4, 4), dma(8, 4), dma(4, 4), dma(7), dma(8),
        dma(4, 4), dma(4, 4), dma(4, 2), dma(2, 4, 2), dma(2, 2), dma(4), dma(2), dma(4), dma(2), dma(6),
    ]
    shapes = (
        jax.ShapeDtypeStruct((128, 4096), BF),
        jax.ShapeDtypeStruct((128, 1024), BF),
        jax.ShapeDtypeStruct((64, 1024), F32),
    )
    results = pl.pallas_call(
        kernel,
        out_shape=shapes,
        in_specs=[vm, vm, vm, vm, hbm, hbm, hbm],
        out_specs=(vm, vm, vm),
        scratch_shapes=scratch,
        compiler_params=pltpu.CompilerParams(
            collective_id=0, has_side_effects=True, vmem_limit_bytes=63 * 1024 * 1024
        ),
        cost_estimate=pl.CostEstimate(flops=25_000_000_000, bytes_accessed=20_000_000, transcendentals=0),
        name="moe_layer",
    )(latent, routes.T, gates.T, w_out_t, grad_out, expert_up, expert_down)
    return pl.pallas_call(
        settle,
        out_shape=shapes,
        in_specs=[vm] * 3,
        out_specs=(hbm,) * 3,
        scratch_shapes=[dma(3)],
        name="settle",
    )(*results)


def solution(mesh):
    rows = P(("dp", "expert"), None)
    return jax.shard_map(
        on_device,
        mesh=mesh,
        in_specs=(rows, rows, rows, rows, P("expert", None), P("expert", None, None), P("expert", None, None)),
        out_specs=(rows, rows, P("expert", None)),
        check_vma=False,
    )
```

```python
import jax
import jax.numpy as jnp
from jax import lax
from jax.experimental import pallas as pl
from jax.experimental.pallas import tpu as pltpu
from jax.sharding import PartitionSpec as P

BF = jnp.bfloat16
F32 = jnp.float32
I32 = jnp.int32
MESH = pl.DeviceIdType.MESH
STRIDE = 5
CHUNKS = 4
PER = 4
MAIN = 256
EXTRA = 64
ROWS = 320


def iota(shape, dim):
    return lax.broadcasted_iota(I32, shape, dim)


def dot(a, b, ca=1, cb=0):
    return lax.dot_general(a, b, (((ca,), (cb,)), ((), ())), preferred_element_type=F32)


def index_of(y, z, x, c):
    return ((y * 2 + z) * 4 + x) * 2 + c


def rows_at(start, size):
    return pl.ds(pl.multiple_of(start, size), size)


def kernel(
    latent, routes, gates, w_own, grad_out, up_hbm, down_hbm,
    mixed, grad_latent, grad_w,
    s1, r1, b1, s2, r2, b2, up, down, relu, xc, acc, extra,
    routes4, gates4, latent4, gc4, part_f, part_s, part_r,
    go, wj, pga, pgb, pgs, pgr, cb, mps, gwp, gwy, gws, gwx, gwb, gwbs, gwby, dps, dpr,
    slots, gate_tab, sel, selt, p_send, pg_send, p_back, pg_back,
    a2a_ss, a2a_rs, grp_ss, grp_rs, sw_ss, sw_rs, wx_ss, wx_rs, wb_ss, wb_rs, wbx_ss, wbx_rs, wy_ss, wy_rs, go_ss, go_rs,
    sib_ss, sib_rs, bgc_ss, bgc_rs, pg_ss, pg_rs, cb_ss, cb_rs, cf_ss, mx_ss, mx_rs,
    gy_ss, gy_rs, gb_ss, gb_rs, gby_ss, gby_rs, gx_ss, gx_rs, dp_sem, loc,
):
    dp = lax.axis_index("dp")
    me = lax.axis_index("expert")
    y, z, x, c = me // 16, (me // 8) % 2, (me // 2) % 4, me % 2
    ring = dp * 2 + z
    mine = c * 4 + ring
    sibling = index_of(y, z, x, 1 - c)
    block = x * (1 - c) + y * c
    half, parity = x // 2, x % 2

    def partner(k, sign):
        off = (STRIDE * k) % 16
        along, hop, flip = off // 4, (off // 2) % 2, off % 2
        pc = (c + flip) % 2
        sender, expert = (c, pc) if sign > 0 else (pc, c)
        pr = (ring + sign * hop * (1 - 2 * expert) + 4) % 4
        py, px = (y + sign * along * (1 - sender) + 4) % 4, (x + sign * along * sender + 4) % 4
        return pr // 2, index_of(py, pr % 2, px, pc)

    def group_at(d):
        to = (block + d) % 4
        return to, index_of(y + c * (to - y), z, x + (1 - c) * (to - x), c)

    def ring_at(d):
        to = (ring + d) % 4
        return to, to // 2, index_of(y, to % 2, x, c)

    def member(dc, dz):
        to, cc = (ring + dz) % 4, (c + dc) % 2
        return cc * 4 + to, to // 2, index_of(y, to % 2, x, cc)

    others = [(dc, dz) for dz in (1, 3, 2, 0) for dc in (0, 1) if dc or dz]

    def remote(src, dst, ss, rs, dev, rep=None):
        rep = dp if rep is None else rep
        return pltpu.make_async_remote_copy(src, dst, ss, rs, device_id=(rep, dev), device_id_type=MESH)

    barrier = pltpu.get_barrier_semaphore()

    def signal(rep, dev):
        pl.semaphore_signal(barrier, inc=1, device_id=(rep, dev), device_id_type=MESH)

    def greet(k, carry):
        for sign in (1, -1):
            signal(*partner(k, sign))
        return carry

    lax.fori_loop(1, 16, greet, 0)
    for dc, dz in others:
        _, rep, to = member(dc, dz)
        signal(rep, to)
    for d in range(1, 8):
        near = (x * 2 + c + d) % 8
        signal(dp, index_of(y, z, near // 2, near % 2))
    for d in range(1, 4):
        for cc in range(2):
            signal(dp, index_of((y + d) % 4, z, x, cc))
    up_copy = pltpu.make_async_copy(up_hbm.at[0], up, loc.at[0])
    down_copy = pltpu.make_async_copy(down_hbm.at[0], down, loc.at[1])
    up_copy.start()
    down_copy.start()
    own_tokens = rows_at(block * 128, 128)
    routes4[block] = routes[...]
    gates4[block] = gates[...]
    latent4[own_tokens, :] = latent[...]

    i, j = iota((256, 256), 0), iota((256, 256), 1)
    sel[...] = jnp.where(((i & 63) >> 2) * 16 + (i >> 6) * 4 + (i & 3) == j, 1.0, 0.0).astype(BF)
    selt[...] = jnp.where(((j & 63) >> 2) * 16 + (j >> 6) * 4 + (j & 3) == i, 1.0, 0.0).astype(BF)

    pl.semaphore_wait(barrier, 50)

    sends_w = parity == (y + dp) % 2
    w_slot = rows_at(y * 128 + c * 64, 64)

    near_half, far_half = pl.ds(0, 512), pl.ds(512, 512)

    def wx(d):
        to = index_of(y, z, (x + d) % 4, half)
        return to, remote(w_own.at[:, near_half], wj.at[w_slot, near_half], wx_ss.at[d], wx_rs.at[c], to)

    def wb(d):
        to = index_of((y + d) % 4, z, x, half)
        return to, remote(w_own.at[:, far_half], wj.at[w_slot, far_half], wb_ss.at[d], wb_rs.at[y * 2 + c], to)

    for d in (1, 3, 2, 0):
        for to, copy in (wx(d), wb(d)):

            @pl.when(jnp.logical_and(sends_w, to != me))
            def _():
                copy.start()

    @pl.when(jnp.logical_and(sends_w, c == half))
    def _():
        wj[w_slot, :] = w_own[...]

    swap = []
    for d in (1, 3, 2):
        _, to = group_at(d)
        swap.append(remote(routes, routes4.at[block], grp_ss.at[0, d], grp_rs.at[0, block], to))
        swap.append(remote(gates, gates4.at[block], grp_ss.at[1, d], grp_rs.at[1, block], to))
    for d in (1, 3, 2):
        _, to = group_at(d)
        swap.append(remote(latent, latent4.at[own_tokens], grp_ss.at[2, d], grp_rs.at[2, block], to))
    for copy in swap:
        copy.start()

    def from_group(n, dst):
        for d in (1, 3, 2):
            g, _ = group_at(d)
            remote(dst(g), dst(g), grp_ss.at[n, d], grp_rs.at[n, g], me).wait_recv()

    def feats(m, part):
        to = m % 4
        return rows_at(part * 1024 + (to % 2) * 512 + (m // 4) * 256 + ((part + to // 2) % 2) * 128, 128)

    def tokens(m):
        return rows_at(m * 128, 128)

    own_go = []
    for part in range(4):
        cols = pl.ds(part * 128, 128)
        for n, (dc, dz) in enumerate(others):
            m, rep, to = member(dc, dz)
            remote(grad_out.at[:, feats(m, part)], go.at[tokens(mine), cols], go_ss.at[n], go_rs.at[mine], to, rep).start()
        copy = pltpu.make_async_copy(grad_out.at[:, feats(mine, part)], go.at[tokens(mine), cols], loc.at[2 + part])
        copy.start()
        own_go.append(copy)

    from_group(0, lambda g: routes4.at[g])
    from_group(1, lambda g: gates4.at[g])

    def names(j):
        return jnp.where(j < 256, j >> 4, (j - 256) >> 2), jnp.where(j < 256, j & 15, 16 + (j & 3)) + 1

    def expert_of(k):
        off = (STRIDE * k) & 15
        along, hop, pc = off >> 2, (off >> 1) & 1, (c + off) & 1
        py, px = (y + along * (1 - c)) & 3, (x + along * c) & 3
        return ((py * 2 + ((z + hop) & 1)) * 4 + px) * 2 + pc

    k_row, s_row = names(iota((320, 128), 0))
    k_col, s_col = names(iota((128, 320), 1))
    spread_t = jnp.where(expert_of(k_row) == iota((320, 128), 1), 1.0, 0.0).astype(BF)
    spread = jnp.where(expert_of(k_col) == iota((128, 320), 0), 1.0, 0.0).astype(BF)
    earlier = jnp.where(iota((128, 128), 0) < iota((128, 128), 1), 1.0, 0.0).astype(BF)

    def table(g):
        hot = jnp.zeros((128, 128), F32)
        gate = jnp.zeros((128, 128), F32)
        for k in range(8):
            hit = routes4[g, k : k + 1, :] == iota((128, 128), 0)
            hot = hot + jnp.where(hit, 1.0, 0.0)
            gate = gate + jnp.where(hit, gates4[g, k : k + 1, :], 0.0)
        slot = jnp.where(hot > 0.5, dot(hot.astype(BF), earlier) + 1.0, 0.0)
        return slot, gate

    for g in range(4):
        slots[g], gate_tab[g] = table(g)
        hit = dot(spread_t, slots[g].astype(BF)) == s_row.astype(F32)
        p_send[g] = jnp.where(hit, 1.0, 0.0).astype(BF)

    def routing_rest():
        for g in range(4):
            gate_hi = gate_tab[g].astype(BF).astype(F32)
            gate_lo = gate_tab[g] - gate_hi
            hit = p_send[g].astype(F32) > 0.5
            pg_send[g, :, 0:128] = jnp.where(hit, dot(spread_t, gate_hi.astype(BF)), 0.0).astype(BF)
            pg_send[g, :, 128:256] = jnp.where(hit, dot(spread_t, gate_lo.astype(BF)), 0.0).astype(BF)
            hit = dot(slots[g].T.astype(BF), spread) == s_col.astype(F32)
            p_back[g] = jnp.where(hit, 1.0, 0.0).astype(BF)
            pg_back[g, 0:128, :] = jnp.where(hit, dot(gate_hi.T.astype(BF), spread), 0.0).astype(BF)
            pg_back[g, 128:256, :] = jnp.where(hit, dot(gate_lo.T.astype(BF), spread), 0.0).astype(BF)

    def unpack(packed):
        rows = dot(sel[...], packed).astype(BF)
        return jnp.concatenate([rows[q * 64 : (q + 1) * 64] for q in range(4)], axis=1)

    def pack(rows):
        stacked = jnp.concatenate([rows[:, q * 256 : (q + 1) * 256] for q in range(4)], axis=0)
        return dot(selt[...], stacked).astype(BF)

    def message(k):
        return rows_at(k * 16, 16)

    def start(which, src, dst, ci, sign):
        def body(k, carry):
            rep, to = partner(k, sign)
            piece = (slice(None), message(k))
            remote(src.at[piece], dst.at[piece], a2a_ss.at[which], a2a_rs.at[which, ci], to, rep).start()
            return carry

        lax.fori_loop(max(ci * PER, 1), ci * PER + PER, body, 0)
        if ci == 0:
            dst[:, 0:16, :] = src[:, 0:16, :]

    def dispatch(which, pick, source, src, dst):
        for g in range(4):
            values = source[g * 128 : g * 128 + 128, :]
            if pick.shape[2] == 256:
                values = jnp.concatenate([values, values], axis=0)
            src[g, :, 0:1024] = dot(pick[g, 0:256, :], values).astype(BF)
            src[g, :, 1024:1280] = pack(dot(pick[g, 256:320, :], values).astype(BF))
        for ci in range(CHUNKS):
            start(which, src, dst, ci, 1)

    def arrived(which, ci, src, dst):
        rows = (slice(None), pl.ds(0, 48) if ci == 0 else pl.ds(ci * 64, 64))
        remote(src.at[rows], dst.at[rows], a2a_ss.at[which], a2a_rs.at[which, ci], me).wait_recv()

    def all_sent(which, src, dst):
        rows = (slice(None), pl.ds(0, 240))
        remote(src.at[rows], dst.at[rows], a2a_ss.at[which], a2a_rs.at[which, 0], me).wait_send()

    x_own = c * 2 + (y + dp) % 2
    for cc in range(2):
        src = index_of(y, z, x_own, cc)

        @pl.when(src != me)
        def _():
            piece = wj.at[rows_at(y * 128 + cc * 64, 64), near_half]
            remote(piece, piece, wx_ss.at[0], wx_rs.at[cc], me).wait_recv()

    def along_y(d):
        py = (y + d) % 4
        return py, index_of(py, z, x, c)

    def wy(d):
        _, to = along_y(d)
        piece = wj.at[tokens(y), near_half]
        return remote(piece, piece, wy_ss.at[d], wy_rs.at[y], to)

    for d in (1, 3, 2):
        wy(d).start()

    def own_y(n):
        return (x + dp) % 2 + 2 * n

    def wbx(n, d):
        py = own_y(n)
        piece = wj.at[tokens(py), far_half]
        return remote(piece, piece, wbx_ss.at[n, d], wbx_rs.at[py], index_of(y, z, (x + d) % 4, c))

    def far_source(py):
        return 2 * c + (py + dp) % 2

    @pl.when(c == half)
    def _():
        for n in range(2):
            py = own_y(n)
            for cc in range(2):

                @pl.when(index_of(py, z, x, cc) != me)
                def _():
                    piece = wj.at[rows_at(py * 128 + cc * 64, 64), far_half]
                    remote(piece, piece, wb_ss.at[0], wb_rs.at[py * 2 + cc], me).wait_recv()

            for d in (1, 3, 2):
                wbx(n, d).start()

    from_group(2, lambda g: latent4.at[rows_at(g * 128, 128)])
    dispatch(0, p_send, latent4, s1, r1)
    routing_rest()

    def quarter(n):
        return rows_at(n * 256, 256)

    def core_rows(cc):
        return rows_at(cc * 512, 512)

    def cols_of(q):
        return pl.ds(q * 256, 256)

    to_sibling = []
    swap_gc = []
    for q in range(4):
        cols = cols_of(q)
        to_sibling.append(remote(pga.at[:, cols], pgb.at[:, cols], sib_ss.at[q], sib_rs.at[q], sibling))
        for d in (1, 3, 2):
            piece = gc4.at[own_tokens, cols]
            swap_gc.append(remote(piece, piece, bgc_ss.at[d, q], bgc_rs.at[block, q], group_at(d)[1]))

    def load(src, ci):
        rows = pl.ds(ci * 64, 64)
        for g in range(4):
            xc[g * 64 : g * 64 + 64, :] = src[g, rows, 0:1024]
        xc[MAIN:ROWS, :] = unpack(jnp.concatenate([src[g, rows, 1024:1280] for g in range(4)], axis=0))

    def store(dst, ci):
        rows = pl.ds(ci * 64, 64)
        more = pack(acc[MAIN:ROWS, :].astype(BF))
        for g in range(4):
            dst[g, rows, 0:1024] = acc[g * 64 : g * 64 + 64, :].astype(BF)
            dst[g, rows, 1024:1280] = more[g * 64 : g * 64 + 64, :]

    def hidden(h):
        return rows_at(h * 512, 512)

    def forward(ci):
        arrived(0, ci, s1, r1)
        load(r1, ci)
        acc[...] = jnp.zeros_like(acc)

        def step(h, inner):
            pos = jnp.maximum(dot(xc[...], up[:, hidden(h)]), 0.0)
            relu[ci, :, hidden(h)] = pos
            acc[...] += dot((pos * pos).astype(BF), down[hidden(h), :])
            return inner

        lax.fori_loop(0, 4, step, 0)
        store(r1, ci)
        start(1, r1, b1, ci, -1)

    def backward(ci):
        arrived(2, ci, s2, r2)
        load(r2, ci)
        acc[...] = jnp.zeros_like(acc)

        def step(h, inner):
            grad = dot(xc[...], down[hidden(h), :], 1, 1) * 2.0 * relu[ci, :, hidden(h)]
            acc[...] += dot(grad.astype(BF), up[:, hidden(h)], 1, 1)
            return inner

        lax.fori_loop(0, 4, step, 0)
        store(r2, ci)
        start(3, r2, b2, ci, -1)

    def gc_sibling():
        for d in (1, 3, 2):
            py, _ = along_y(d)
            piece = wj.at[tokens(py), near_half]
            remote(piece, piece, wy_ss.at[d], wy_rs.at[py], me).wait_recv()
        for py in range(4):

            @pl.when(x != far_source(py))
            def _():
                piece = wj.at[tokens(py), far_half]
                remote(piece, piece, wbx_ss.at[0, 1], wbx_rs.at[py], me).wait_recv()

        for copy in own_go:
            copy.wait()
        for n, (dc, dz) in enumerate(others):
            m, _, _ = member(dc, dz)
            remote(go.at[tokens(m)], go.at[tokens(m)], go_ss.at[n], go_rs.at[m], me).wait_recv()
        for q in range(4):
            pga[:, cols_of(q)] = dot(go[core_rows(1 - c), :], wj[:, cols_of(q)]).astype(BF)
            to_sibling[q].start()

    def pg_copy(d, q):
        to, rep, dev = ring_at(d)
        cols = cols_of(q)
        src, dst = pgs.at[tokens(to), cols], pgr.at[tokens(ring), cols]
        return remote(src, dst, pg_ss.at[d, q], pg_rs.at[ring, q], dev, rep)

    def gc_ring():
        for q in range(4):
            cols = cols_of(q)
            to_sibling[q].wait_recv()
            pgs[:, cols] = (dot(go[core_rows(c), :], wj[:, cols]) + pgb[:, cols].astype(F32)).astype(BF)
            for d in (1, 3, 2):
                pg_copy(d, q).start()
            pgr[tokens(ring), cols] = pgs[tokens(ring), cols]

    def gc_swap():
        for q in range(4):
            cols = cols_of(q)
            for d in (1, 3, 2):
                to, _, _ = ring_at(d)
                piece = pgr.at[tokens(to), cols]
                remote(piece, piece, pg_ss.at[d, q], pg_rs.at[to, q], me).wait_recv()
            gc = sum(pgr[n * 128 : (n + 1) * 128, cols].astype(F32) for n in range(4)).astype(BF)
            gc4[own_tokens, cols] = gc
            for n in range(3):
                swap_gc[q * 3 + n].start()

    def gc_dispatch():
        for q in range(4):
            for d in (1, 3, 2):
                g, _ = group_at(d)
                piece = gc4.at[rows_at(g * 128, 128), cols_of(q)]
                remote(piece, piece, bgc_ss.at[d, q], bgc_rs.at[g, q], me).wait_recv()
        dispatch(2, pg_send, gc4, s2, r2)

    def gather_back(which, src, dst):
        for ci in range(CHUNKS):
            arrived(which, ci, src, dst)

        for g in range(4):
            extra[g * EXTRA : g * EXTRA + EXTRA, :] = unpack(dst[g, :, 1024:1280])

    def part_copy(n, d, q):
        g, to = group_at(d)
        cols = cols_of(q)
        src, dst = part_s.at[n, g, :, cols], part_r.at[n, block, :, cols]
        return remote(src, dst, sw_ss.at[n, d, q], sw_rs.at[n, block, q], to)

    def part_sums(n, weights, src):
        for q in range(4):
            cols = cols_of(q)
            for g in range(4):
                both = dot(weights[g, :, 0:256], src[g, :, cols])
                both = both + dot(weights[g, :, 256:320], extra[g * EXTRA : g * EXTRA + EXTRA, cols])
                if weights.shape[1] == 256:
                    both = both[0:128] + both[128:256]
                part_f[g * 128 : g * 128 + 128, cols] = both
                part_s[n, g, :, cols] = both.astype(BF)
            for d in (1, 3, 2):
                part_copy(n, d, q).start()

    def part_total(n, q):
        cols = cols_of(q)
        total = part_f[own_tokens, cols]
        for d in (1, 3, 2):
            g, _ = group_at(d)
            piece = part_r.at[n, g, :, cols]
            remote(piece, piece, sw_ss.at[n, d, q], sw_rs.at[n, g, q], me).wait_recv()
        for d in (1, 3, 2):
            g, _ = group_at(d)
            total = total + part_r[n, g, :, cols].astype(F32)
        return total.astype(BF)

    def combine():
        gather_back(1, r1, b1)
        part_sums(0, pg_back, b1)

    def combine_back():
        gather_back(3, r2, b2)
        part_sums(1, p_back, b2)

    def cb_copy(m, q, ss, dev, rep):
        piece = cb.at[tokens(m), cols_of(q)]
        return remote(piece, piece, ss, cb_rs.at[m, q], dev, rep)

    def share_start():
        for q in range(4):
            cb[tokens(mine), cols_of(q)] = part_total(0, q)
            for d in (1, 3, 2):
                _, rep, dev = ring_at(d)
                cb_copy(mine, q, cb_ss.at[d, q], dev, rep).start()
            cb_copy(mine, q, cb_ss.at[0, q], sibling, dp).start()

    def share_pass():
        for q in range(4):
            for d in (1, 3, 2):
                m = c * 4 + (ring + d) % 4
                cb_copy(m, q, cb_ss.at[d, q], me, dp).wait_recv()
                cb_copy(m, q, cf_ss.at[d, q], sibling, dp).start()

    def gy(d, q):
        py, to = along_y(d)
        cols = cols_of(q)
        src, dst = gwp.at[tokens(py), cols], gwy.at[tokens(y), cols]
        return py, remote(src, dst, gy_ss.at[d, q], gy_rs.at[y, q], to)

    def far_cols(q):
        return pl.ds(q * 256 - 512, 256)

    def gb(py, q):
        to = index_of(y, z, far_source(py), c)
        src, dst = gwp.at[tokens(py), cols_of(q)], gwb.at[py // 2, tokens(x), far_cols(q)]
        return to, remote(src, dst, gb_ss.at[py, q - 2], gb_rs.at[py // 2, x, q - 2], to)

    def weight_grad():
        for q in range(4):
            for d in range(4):
                m = (1 - c) * 4 + (ring + d) % 4
                cb_copy(m, q, cb_ss.at[d, q], me, dp).wait_recv()
            cols = cols_of(q)
            gwp[:, cols] = dot(go[...], cb[:, cols], 0, 0).astype(BF)
            if q < 2:
                for d in (1, 3, 2):
                    gy(d, q)[1].start()
                gwy[tokens(y), cols] = gwp[tokens(y), cols]
            else:
                for py in range(4):
                    to, copy = gb(py, q)

                    @pl.when(to != me)
                    def _():
                        copy.start()

                    @pl.when(to == me)
                    def _():
                        gwb[py // 2, tokens(x), far_cols(q)] = gwp[tokens(py), cols]

    def mix_all():
        def mix(part, carry):
            cols = tokens(part)
            mps[:, cols] = dot(cb[...], wj[cols, :], 1, 1).astype(BF)
            for n, (dc, dz) in enumerate(others):
                m, rep, to = member(dc, dz)
                src, dst = mps.at[tokens(m), cols], mixed.at[:, feats(mine, part)]
                remote(src, dst, mx_ss.at[n], mx_rs.at[mine], to, rep).start()
            mixed[:, feats(mine, part)] = mps[tokens(mine), cols]
            return carry

        lax.fori_loop(0, 4, mix, 0)

    up_copy.wait()
    down_copy.wait()
    gc_sibling()
    gc_ring()
    forward(0)
    forward(1)
    forward(2)
    gc_swap()
    forward(3)
    gc_dispatch()
    combine()
    backward(0)
    share_start()
    backward(1)
    backward(2)
    share_pass()
    backward(3)
    weight_grad()
    mix_all()
    combine_back()

    for q in range(2):
        for d in (1, 3, 2):
            py, _ = along_y(d)
            piece = gwy.at[tokens(py), cols_of(q)]
            remote(piece, piece, gy_ss.at[d, q], gy_rs.at[py, q], me).wait_recv()
    gws[...] = sum(gwy[n * 128 : (n + 1) * 128, 0:512].astype(F32) for n in range(4)).astype(BF)
    x_slot = rows_at(x * 64, 64)

    def gx(cc):
        to = index_of(y, z, x_own, cc)
        return to, remote(gws.at[pl.ds(cc * 64, 64)], gwx.at[x_slot], gx_ss.at[cc], gx_rs.at[x], to)

    for cc in range(2):
        to, copy = gx(cc)

        @pl.when(to != me)
        def _():
            copy.start()

        @pl.when(to == me)
        def _():
            gwx[x_slot, :] = gws[cc * 64 : cc * 64 + 64, :]

    def gby(n, cc):
        to = index_of(own_y(n), z, x, cc)
        src = gwbs.at[n, pl.ds(cc * 64, 64)]
        return to, remote(src, gwby.at[rows_at(y * 64, 64)], gby_ss.at[n, cc], gby_rs.at[y], to)

    @pl.when(c == half)
    def _():
        for n in range(2):
            for px in range(4):

                @pl.when(x != px)
                def _():
                    for q in range(2):
                        piece = gwb.at[n, pl.ds(px * 128, 128), cols_of(q)]
                        remote(piece, piece, gb_ss.at[0, q], gb_rs.at[n, px, q], me).wait_recv()

            gwbs[n] = sum(gwb[n, px * 128 : px * 128 + 128, :].astype(F32) for px in range(4)).astype(BF)
            for cc in range(2):
                to, copy = gby(n, cc)

                @pl.when(to != me)
                def _():
                    copy.start()

                @pl.when(to == me)
                def _():
                    gwby[rows_at(y * 64, 64), :] = gwbs[n, cc * 64 : cc * 64 + 64, :]


    exchange = pltpu.make_async_remote_copy(
        dps, dpr, dp_sem.at[0], dp_sem.at[1], device_id=(1 - dp, me), device_id_type=MESH
    )

    @pl.when(sends_w)
    def _():
        for px in range(4):
            src = index_of(y, z, px, half)

            @pl.when(src != me)
            def _():
                rows = pl.ds(px * 64, 64)
                remote(gwx.at[rows], gwx.at[rows], gx_ss.at[0], gx_rs.at[px], me).wait_recv()

        for py in range(4):

            @pl.when(index_of(py, z, x, half) != me)
            def _():
                rows = pl.ds(py * 64, 64)
                remote(gwby.at[rows], gwby.at[rows], gby_ss.at[0, 0], gby_rs.at[py], me).wait_recv()

        dps[:, 0:512] = sum(gwx[n * 64 : (n + 1) * 64, :].astype(F32) for n in range(4)).astype(BF)
        dps[:, 512:1024] = sum(gwby[n * 64 : (n + 1) * 64, :].astype(F32) for n in range(4)).astype(BF)
        exchange.start()
        grad_w[...] = dps[...].astype(F32)

    for q in range(4):
        grad_latent[:, cols_of(q)] = part_total(1, q)

    @pl.when(sends_w)
    def _():
        exchange.wait_send()

    @pl.when(jnp.logical_not(sends_w))
    def _():
        exchange.wait_recv()
        grad_w[...] = dpr[...].astype(F32)

    for n, (dc, dz) in enumerate(others):
        m, _, _ = member(dc, dz)
        whole = remote(mps.at[tokens(m)], mps.at[tokens(m)], mx_ss.at[n], mx_rs.at[m], me)
        whole.wait_recv()
        whole.wait_send()
        remote(go.at[tokens(m)], go.at[tokens(m)], go_ss.at[n], go_rs.at[m], me).wait_send()
    for copy in swap + swap_gc + to_sibling:
        copy.wait_send()
    for d in range(4):
        for to, copy in (wx(d), wb(d)):

            @pl.when(jnp.logical_and(sends_w, to != me))
            def _():
                copy.wait_send()

        for q in range(2):
            to, copy = gb(d, q + 2)

            @pl.when(to != me)
            def _():
                copy.wait_send()

        for q in range(4):
            cb_copy(mine, q, cb_ss.at[d, q], me, dp).wait_send()
            if d:
                if q < 2:
                    gy(d, q)[1].wait_send()
                cb_copy(mine, q, cf_ss.at[d, q], me, dp).wait_send()
        if d:
            wy(d).wait_send()
            for q in range(4):
                pg_copy(d, q).wait_send()
                part_copy(0, d, q).wait_send()
                part_copy(1, d, q).wait_send()
    @pl.when(c == half)
    def _():
        for n in range(2):
            for d in (1, 2, 3):
                wbx(n, d).wait_send()
            for cc in range(2):
                to, copy = gby(n, cc)

                @pl.when(to != me)
                def _():
                    copy.wait_send()

    for cc in range(2):
        to, copy = gx(cc)

        @pl.when(to != me)
        def _():
            copy.wait_send()

    all_sent(0, s1, r1)
    all_sent(1, r1, b1)
    all_sent(2, s2, r2)
    all_sent(3, r2, b2)


def settle(mixed_in, latent_in, w_in, mixed, grad_latent, grad_w, sems):
    pairs = ((mixed_in, mixed), (latent_in, grad_latent), (w_in, grad_w))
    copies = [pltpu.make_async_copy(src, dst, sems.at[n]) for n, (src, dst) in enumerate(pairs)]
    for copy in copies:
        copy.start()
    for copy in copies:
        copy.wait()


def on_device(latent, routes, gates, grad_out, w_out_t, expert_up, expert_down):
    vm = pl.BlockSpec(memory_space=pltpu.VMEM)
    hbm = pl.BlockSpec(memory_space=pl.ANY)

    def dma(*shape):
        return pltpu.SemaphoreType.DMA(shape)

    def bf(*shape):
        return pltpu.VMEM(shape, BF)

    scratch = [bf(4, 256, 1280)] * 6 + [
        bf(1024, 2048), bf(2048, 1024), pltpu.VMEM((CHUNKS, ROWS, 2048), F32),
        bf(ROWS, 1024), pltpu.VMEM((ROWS, 1024), F32), bf(256, 1024),
        pltpu.VMEM((4, 8, 128), I32), pltpu.VMEM((4, 8, 128), F32), bf(512, 1024), bf(512, 1024),
        pltpu.VMEM((512, 1024), F32), bf(2, 4, 128, 1024), bf(2, 4, 128, 1024),
        bf(1024, 512), bf(512, 1024), bf(512, 1024), bf(512, 1024), bf(512, 1024), bf(512, 1024),
        bf(1024, 1024), bf(1024, 512), bf(512, 1024), bf(512, 512), bf(128, 512), bf(256, 512), bf(2, 512, 512), bf(2, 128, 512), bf(256, 512),
        bf(64, 1024), bf(64, 1024),
        pltpu.VMEM((4, 128, 128), F32), pltpu.VMEM((4, 128, 128), F32), bf(256, 256), bf(256, 256),
        bf(4, 320, 128), bf(4, 320, 256), bf(4, 128, 320), bf(4, 256, 320),
        dma(4), dma(4, 4), dma(3, 4), dma(3, 4), dma(2, 4, 4), dma(2, 4, 4), dma(4), dma(2), dma(4), dma(8), dma(2, 4), dma(4), dma(4), dma(4), dma(7), dma(8),
        dma(4), dma(4), dma(4, 4), dma(4, 4), dma(4, 4), dma(4, 4), dma(4, 4), dma(8, 4), dma(4, 4), dma(7), dma(8),
        dma(4, 4), dma(4, 4), dma(4, 2), dma(2, 4, 2), dma(2, 2), dma(4), dma(2), dma(4), dma(2), dma(6),
    ]
    shapes = (
        jax.ShapeDtypeStruct((128, 4096), BF),
        jax.ShapeDtypeStruct((128, 1024), BF),
        jax.ShapeDtypeStruct((64, 1024), F32),
    )
    results = pl.pallas_call(
        kernel,
        out_shape=shapes,
        in_specs=[vm, vm, vm, vm, hbm, hbm, hbm],
        out_specs=(vm, vm, vm),
        scratch_shapes=scratch,
        compiler_params=pltpu.CompilerParams(
            collective_id=0, has_side_effects=True, vmem_limit_bytes=63 * 1024 * 1024
        ),
        cost_estimate=pl.CostEstimate(flops=25_000_000_000, bytes_accessed=20_000_000, transcendentals=0),
        name="moe_layer",
    )(latent, routes.T, gates.T, w_out_t, grad_out, expert_up, expert_down)
    return pl.pallas_call(
        settle,
        out_shape=shapes,
        in_specs=[vm] * 3,
        out_specs=(hbm,) * 3,
        scratch_shapes=[dma(3)],
        name="settle",
    )(*results)


def solution(mesh):
    rows = P(("dp", "expert"), None)
    return jax.shard_map(
        on_device,
        mesh=mesh,
        in_specs=(rows, rows, rows, rows, P("expert", None), P("expert", None, None), P("expert", None, None)),
        out_specs=(rows, rows, P("expert", None)),
        check_vma=False,
    )
```

```python
import jax
import jax.numpy as jnp
from jax import lax
from jax.experimental import pallas as pl
from jax.experimental.pallas import tpu as pltpu
from jax.sharding import PartitionSpec as P

BF = jnp.bfloat16
F32 = jnp.float32
I32 = jnp.int32
MESH = pl.DeviceIdType.MESH
STRIDE = 5
CHUNKS = 4
PER = 4
MAIN = 256
EXTRA = 64
ROWS = 320


def iota(shape, dim):
    return lax.broadcasted_iota(I32, shape, dim)


def dot(a, b, ca=1, cb=0):
    return lax.dot_general(a, b, (((ca,), (cb,)), ((), ())), preferred_element_type=F32)


def index_of(y, z, x, c):
    return ((y * 2 + z) * 4 + x) * 2 + c


def rows_at(start, size):
    return pl.ds(pl.multiple_of(start, size), size)


def kernel(
    latent, routes, gates, w_own, grad_out, up_hbm, down_hbm,
    mixed, grad_latent, grad_w,
    s1, r1, b1, s2, r2, b2, up, down, relu, xc, acc, extra,
    routes4, gates4, latent4, gc4, part_f, part_s, part_r,
    go, wj, pga, pgb, pgs, pgr, cb, mps, gwp, gwy, gws, gwx, gwb, gwbs, gwby, dps, dpr,
    slots, gate_tab, sel, selt, p_send, pg_send, p_back, pg_back,
    a2a_ss, a2a_rs, grp_ss, grp_rs, sw_ss, sw_rs, wx_ss, wx_rs, wb_ss, wb_rs, wbx_ss, wbx_rs, wy_ss, wy_rs, go_ss, go_rs,
    sib_ss, sib_rs, bgc_ss, bgc_rs, pg_ss, pg_rs, cb_ss, cb_rs, cf_ss, mx_ss, mx_rs,
    gy_ss, gy_rs, gb_ss, gb_rs, gby_ss, gby_rs, gx_ss, gx_rs, dp_sem, loc,
):
    dp = lax.axis_index("dp")
    me = lax.axis_index("expert")
    y, z, x, c = me // 16, (me // 8) % 2, (me // 2) % 4, me % 2
    ring = dp * 2 + z
    mine = c * 4 + ring
    sibling = index_of(y, z, x, 1 - c)
    block = x * (1 - c) + y * c
    half, parity = x // 2, x % 2

    def partner(k, sign):
        off = (STRIDE * k) % 16
        along, hop, flip = off // 4, (off // 2) % 2, off % 2
        pc = (c + flip) % 2
        sender, expert = (c, pc) if sign > 0 else (pc, c)
        pr = (ring + sign * hop * (1 - 2 * expert) + 4) % 4
        py, px = (y + sign * along * (1 - sender) + 4) % 4, (x + sign * along * sender + 4) % 4
        return pr // 2, index_of(py, pr % 2, px, pc)

    def group_at(d):
        to = (block + d) % 4
        return to, index_of(y + c * (to - y), z, x + (1 - c) * (to - x), c)

    def ring_at(d):
        to = (ring + d) % 4
        return to, to // 2, index_of(y, to % 2, x, c)

    def member(dc, dz):
        to, cc = (ring + dz) % 4, (c + dc) % 2
        return cc * 4 + to, to // 2, index_of(y, to % 2, x, cc)

    others = [(dc, dz) for dz in (1, 3, 2, 0) for dc in (0, 1) if dc or dz]

    def remote(src, dst, ss, rs, dev, rep=None):
        rep = dp if rep is None else rep
        return pltpu.make_async_remote_copy(src, dst, ss, rs, device_id=(rep, dev), device_id_type=MESH)

    barrier = pltpu.get_barrier_semaphore()

    def signal(rep, dev):
        pl.semaphore_signal(barrier, inc=1, device_id=(rep, dev), device_id_type=MESH)

    def greet(k, carry):
        for sign in (1, -1):
            signal(*partner(k, sign))
        return carry

    lax.fori_loop(1, 16, greet, 0)
    for dc, dz in others:
        _, rep, to = member(dc, dz)
        signal(rep, to)
    for d in range(1, 8):
        near = (x * 2 + c + d) % 8
        signal(dp, index_of(y, z, near // 2, near % 2))
    for d in range(1, 4):
        for cc in range(2):
            signal(dp, index_of((y + d) % 4, z, x, cc))
    up_copy = pltpu.make_async_copy(up_hbm.at[0], up, loc.at[0])
    down_copy = pltpu.make_async_copy(down_hbm.at[0], down, loc.at[1])
    up_copy.start()
    down_copy.start()
    own_tokens = rows_at(block * 128, 128)
    routes4[block] = routes[...]
    gates4[block] = gates[...]
    latent4[own_tokens, :] = latent[...]

    i, j = iota((256, 256), 0), iota((256, 256), 1)
    sel[...] = jnp.where(((i & 63) >> 2) * 16 + (i >> 6) * 4 + (i & 3) == j, 1.0, 0.0).astype(BF)
    selt[...] = jnp.where(((j & 63) >> 2) * 16 + (j >> 6) * 4 + (j & 3) == i, 1.0, 0.0).astype(BF)

    pl.semaphore_wait(barrier, 50)

    sends_w = parity == (y + dp) % 2
    w_slot = rows_at(y * 128 + c * 64, 64)

    near_half, far_half = pl.ds(0, 512), pl.ds(512, 512)

    def wx(d):
        to = index_of(y, z, (x + d) % 4, half)
        return to, remote(w_own.at[:, near_half], wj.at[w_slot, near_half], wx_ss.at[d], wx_rs.at[c], to)

    def wb(d):
        to = index_of((y + d) % 4, z, x, half)
        return to, remote(w_own.at[:, far_half], wj.at[w_slot, far_half], wb_ss.at[d], wb_rs.at[y * 2 + c], to)

    for d in (1, 3, 2, 0):
        for to, copy in (wx(d), wb(d)):

            @pl.when(jnp.logical_and(sends_w, to != me))
            def _():
                copy.start()

    @pl.when(jnp.logical_and(sends_w, c == half))
    def _():
        wj[w_slot, :] = w_own[...]

    swap = []
    for d in (1, 3, 2):
        _, to = group_at(d)
        swap.append(remote(routes, routes4.at[block], grp_ss.at[0, d], grp_rs.at[0, block], to))
        swap.append(remote(gates, gates4.at[block], grp_ss.at[1, d], grp_rs.at[1, block], to))
    for d in (1, 3, 2):
        _, to = group_at(d)
        swap.append(remote(latent, latent4.at[own_tokens], grp_ss.at[2, d], grp_rs.at[2, block], to))
    for copy in swap:
        copy.start()

    def from_group(n, dst):
        for d in (1, 3, 2):
            g, _ = group_at(d)
            remote(dst(g), dst(g), grp_ss.at[n, d], grp_rs.at[n, g], me).wait_recv()

    def feats(m, part):
        to = m % 4
        return rows_at(part * 1024 + (to % 2) * 512 + (m // 4) * 256 + ((part + to // 2) % 2) * 128, 128)

    def tokens(m):
        return rows_at(m * 128, 128)

    own_go = []
    for part in range(4):
        cols = pl.ds(part * 128, 128)
        for n, (dc, dz) in enumerate(others):
            m, rep, to = member(dc, dz)
            remote(grad_out.at[:, feats(m, part)], go.at[tokens(mine), cols], go_ss.at[n], go_rs.at[mine], to, rep).start()
        copy = pltpu.make_async_copy(grad_out.at[:, feats(mine, part)], go.at[tokens(mine), cols], loc.at[2 + part])
        copy.start()
        own_go.append(copy)

    from_group(0, lambda g: routes4.at[g])
    from_group(1, lambda g: gates4.at[g])

    def names(j):
        return jnp.where(j < 256, j >> 4, (j - 256) >> 2), jnp.where(j < 256, j & 15, 16 + (j & 3)) + 1

    def expert_of(k):
        off = (STRIDE * k) & 15
        along, hop, pc = off >> 2, (off >> 1) & 1, (c + off) & 1
        py, px = (y + along * (1 - c)) & 3, (x + along * c) & 3
        return ((py * 2 + ((z + hop) & 1)) * 4 + px) * 2 + pc

    k_row, s_row = names(iota((320, 128), 0))
    k_col, s_col = names(iota((128, 320), 1))
    spread_t = jnp.where(expert_of(k_row) == iota((320, 128), 1), 1.0, 0.0).astype(BF)
    spread = jnp.where(expert_of(k_col) == iota((128, 320), 0), 1.0, 0.0).astype(BF)
    earlier = jnp.where(iota((128, 128), 0) < iota((128, 128), 1), 1.0, 0.0).astype(BF)

    def table(g):
        hot = jnp.zeros((128, 128), F32)
        gate = jnp.zeros((128, 128), F32)
        for k in range(8):
            hit = routes4[g, k : k + 1, :] == iota((128, 128), 0)
            hot = hot + jnp.where(hit, 1.0, 0.0)
            gate = gate + jnp.where(hit, gates4[g, k : k + 1, :], 0.0)
        slot = jnp.where(hot > 0.5, dot(hot.astype(BF), earlier) + 1.0, 0.0)
        return slot, gate

    for g in range(4):
        slots[g], gate_tab[g] = table(g)
        hit = dot(spread_t, slots[g].astype(BF)) == s_row.astype(F32)
        p_send[g] = jnp.where(hit, 1.0, 0.0).astype(BF)

    def routing_rest():
        for g in range(4):
            gate_hi = gate_tab[g].astype(BF).astype(F32)
            gate_lo = gate_tab[g] - gate_hi
            hit = p_send[g].astype(F32) > 0.5
            pg_send[g, :, 0:128] = jnp.where(hit, dot(spread_t, gate_hi.astype(BF)), 0.0).astype(BF)
            pg_send[g, :, 128:256] = jnp.where(hit, dot(spread_t, gate_lo.astype(BF)), 0.0).astype(BF)
            hit = dot(slots[g].T.astype(BF), spread) == s_col.astype(F32)
            p_back[g] = jnp.where(hit, 1.0, 0.0).astype(BF)
            pg_back[g, 0:128, :] = jnp.where(hit, dot(gate_hi.T.astype(BF), spread), 0.0).astype(BF)
            pg_back[g, 128:256, :] = jnp.where(hit, dot(gate_lo.T.astype(BF), spread), 0.0).astype(BF)

    def unpack(packed):
        rows = dot(sel[...], packed).astype(BF)
        return jnp.concatenate([rows[q * 64 : (q + 1) * 64] for q in range(4)], axis=1)

    def pack(rows):
        stacked = jnp.concatenate([rows[:, q * 256 : (q + 1) * 256] for q in range(4)], axis=0)
        return dot(selt[...], stacked).astype(BF)

    def message(k):
        return rows_at(k * 16, 16)

    def start(which, src, dst, ci, sign):
        def body(k, carry):
            rep, to = partner(k, sign)
            piece = (slice(None), message(k))
            remote(src.at[piece], dst.at[piece], a2a_ss.at[which], a2a_rs.at[which, ci], to, rep).start()
            return carry

        lax.fori_loop(max(ci * PER, 1), ci * PER + PER, body, 0)
        if ci == 0:
            dst[:, 0:16, :] = src[:, 0:16, :]

    def dispatch(which, pick, source, src, dst):
        for g in range(4):
            values = source[g * 128 : g * 128 + 128, :]
            if pick.shape[2] == 256:
                values = jnp.concatenate([values, values], axis=0)
            src[g, :, 0:1024] = dot(pick[g, 0:256, :], values).astype(BF)
            src[g, :, 1024:1280] = pack(dot(pick[g, 256:320, :], values).astype(BF))
        for ci in range(CHUNKS):
            start(which, src, dst, ci, 1)

    def arrived(which, ci, src, dst):
        rows = (slice(None), pl.ds(0, 48) if ci == 0 else pl.ds(ci * 64, 64))
        remote(src.at[rows], dst.at[rows], a2a_ss.at[which], a2a_rs.at[which, ci], me).wait_recv()

    def all_sent(which, src, dst):
        rows = (slice(None), pl.ds(0, 240))
        remote(src.at[rows], dst.at[rows], a2a_ss.at[which], a2a_rs.at[which, 0], me).wait_send()

    x_own = c * 2 + (y + dp) % 2
    for cc in range(2):
        src = index_of(y, z, x_own, cc)

        @pl.when(src != me)
        def _():
            piece = wj.at[rows_at(y * 128 + cc * 64, 64), near_half]
            remote(piece, piece, wx_ss.at[0], wx_rs.at[cc], me).wait_recv()

    def along_y(d):
        py = (y + d) % 4
        return py, index_of(py, z, x, c)

    def wy(d):
        _, to = along_y(d)
        piece = wj.at[tokens(y), near_half]
        return remote(piece, piece, wy_ss.at[d], wy_rs.at[y], to)

    for d in (1, 3, 2):
        wy(d).start()

    def own_y(n):
        return (x + dp) % 2 + 2 * n

    def wbx(n, d):
        py = own_y(n)
        piece = wj.at[tokens(py), far_half]
        return remote(piece, piece, wbx_ss.at[n, d], wbx_rs.at[py], index_of(y, z, (x + d) % 4, c))

    def far_source(py):
        return 2 * c + (py + dp) % 2

    @pl.when(c == half)
    def _():
        for n in range(2):
            py = own_y(n)
            for cc in range(2):

                @pl.when(index_of(py, z, x, cc) != me)
                def _():
                    piece = wj.at[rows_at(py * 128 + cc * 64, 64), far_half]
                    remote(piece, piece, wb_ss.at[0], wb_rs.at[py * 2 + cc], me).wait_recv()

            for d in (1, 3, 2):
                wbx(n, d).start()

    from_group(2, lambda g: latent4.at[rows_at(g * 128, 128)])
    dispatch(0, p_send, latent4, s1, r1)
    routing_rest()

    def quarter(n):
        return rows_at(n * 256, 256)

    def core_rows(cc):
        return rows_at(cc * 512, 512)

    def cols_of(q):
        return pl.ds(q * 256, 256)

    to_sibling = []
    swap_gc = []
    for q in range(4):
        cols = cols_of(q)
        to_sibling.append(remote(pga.at[:, cols], pgb.at[:, cols], sib_ss.at[q], sib_rs.at[q], sibling))
        for d in (1, 3, 2):
            piece = gc4.at[own_tokens, cols]
            swap_gc.append(remote(piece, piece, bgc_ss.at[d, q], bgc_rs.at[block, q], group_at(d)[1]))

    def load(src, ci):
        rows = pl.ds(ci * 64, 64)
        for g in range(4):
            xc[g * 64 : g * 64 + 64, :] = src[g, rows, 0:1024]
        xc[MAIN:ROWS, :] = unpack(jnp.concatenate([src[g, rows, 1024:1280] for g in range(4)], axis=0))

    def store(dst, ci):
        rows = pl.ds(ci * 64, 64)
        more = pack(acc[MAIN:ROWS, :].astype(BF))
        for g in range(4):
            dst[g, rows, 0:1024] = acc[g * 64 : g * 64 + 64, :].astype(BF)
            dst[g, rows, 1024:1280] = more[g * 64 : g * 64 + 64, :]

    def hidden(h):
        return rows_at(h * 512, 512)

    def forward(ci):
        arrived(0, ci, s1, r1)
        load(r1, ci)
        acc[...] = jnp.zeros_like(acc)

        def step(h, inner):
            pos = jnp.maximum(dot(xc[...], up[:, hidden(h)]), 0.0)
            relu[ci, :, hidden(h)] = pos
            acc[...] += dot((pos * pos).astype(BF), down[hidden(h), :])
            return inner

        lax.fori_loop(0, 4, step, 0)
        store(r1, ci)
        start(1, r1, b1, ci, -1)

    def backward(ci):
        arrived(2, ci, s2, r2)
        load(r2, ci)
        acc[...] = jnp.zeros_like(acc)

        def step(h, inner):
            grad = dot(xc[...], down[hidden(h), :], 1, 1) * 2.0 * relu[ci, :, hidden(h)]
            acc[...] += dot(grad.astype(BF), up[:, hidden(h)], 1, 1)
            return inner

        lax.fori_loop(0, 4, step, 0)
        store(r2, ci)
        start(3, r2, b2, ci, -1)

    def gc_sibling():
        for d in (1, 3, 2):
            py, _ = along_y(d)
            piece = wj.at[tokens(py), near_half]
            remote(piece, piece, wy_ss.at[d], wy_rs.at[py], me).wait_recv()
        for py in range(4):

            @pl.when(x != far_source(py))
            def _():
                piece = wj.at[tokens(py), far_half]
                remote(piece, piece, wbx_ss.at[0, 1], wbx_rs.at[py], me).wait_recv()

        for copy in own_go:
            copy.wait()
        for n, (dc, dz) in enumerate(others):
            m, _, _ = member(dc, dz)
            remote(go.at[tokens(m)], go.at[tokens(m)], go_ss.at[n], go_rs.at[m], me).wait_recv()
        for q in range(4):
            pga[:, cols_of(q)] = dot(go[core_rows(1 - c), :], wj[:, cols_of(q)]).astype(BF)
            to_sibling[q].start()

    def pg_copy(d, q):
        to, rep, dev = ring_at(d)
        cols = cols_of(q)
        src, dst = pgs.at[tokens(to), cols], pgr.at[tokens(ring), cols]
        return remote(src, dst, pg_ss.at[d, q], pg_rs.at[ring, q], dev, rep)

    def gc_ring():
        for q in range(4):
            cols = cols_of(q)
            to_sibling[q].wait_recv()
            pgs[:, cols] = (dot(go[core_rows(c), :], wj[:, cols]) + pgb[:, cols].astype(F32)).astype(BF)
            for d in (1, 3, 2):
                pg_copy(d, q).start()
            pgr[tokens(ring), cols] = pgs[tokens(ring), cols]

    def gc_swap():
        for q in range(4):
            cols = cols_of(q)
            for d in (1, 3, 2):
                to, _, _ = ring_at(d)
                piece = pgr.at[tokens(to), cols]
                remote(piece, piece, pg_ss.at[d, q], pg_rs.at[to, q], me).wait_recv()
            gc = sum(pgr[n * 128 : (n + 1) * 128, cols].astype(F32) for n in range(4)).astype(BF)
            gc4[own_tokens, cols] = gc
            for n in range(3):
                swap_gc[q * 3 + n].start()

    def gc_dispatch():
        for q in range(4):
            for d in (1, 3, 2):
                g, _ = group_at(d)
                piece = gc4.at[rows_at(g * 128, 128), cols_of(q)]
                remote(piece, piece, bgc_ss.at[d, q], bgc_rs.at[g, q], me).wait_recv()
        dispatch(2, pg_send, gc4, s2, r2)

    def gather_back(which, src, dst):
        for ci in range(CHUNKS):
            arrived(which, ci, src, dst)

        for g in range(4):
            extra[g * EXTRA : g * EXTRA + EXTRA, :] = unpack(dst[g, :, 1024:1280])

    def part_copy(n, d, q):
        g, to = group_at(d)
        cols = cols_of(q)
        src, dst = part_s.at[n, g, :, cols], part_r.at[n, block, :, cols]
        return remote(src, dst, sw_ss.at[n, d, q], sw_rs.at[n, block, q], to)

    def part_sums(n, weights, src):
        for q in range(4):
            cols = cols_of(q)
            for g in range(4):
                both = dot(weights[g, :, 0:256], src[g, :, cols])
                both = both + dot(weights[g, :, 256:320], extra[g * EXTRA : g * EXTRA + EXTRA, cols])
                if weights.shape[1] == 256:
                    both = both[0:128] + both[128:256]
                part_f[g * 128 : g * 128 + 128, cols] = both
                part_s[n, g, :, cols] = both.astype(BF)
            for d in (1, 3, 2):
                part_copy(n, d, q).start()

    def part_total(n, q):
        cols = cols_of(q)
        total = part_f[own_tokens, cols]
        for d in (1, 3, 2):
            g, _ = group_at(d)
            piece = part_r.at[n, g, :, cols]
            remote(piece, piece, sw_ss.at[n, d, q], sw_rs.at[n, g, q], me).wait_recv()
        for d in (1, 3, 2):
            g, _ = group_at(d)
            total = total + part_r[n, g, :, cols].astype(F32)
        return total.astype(BF)

    def combine():
        gather_back(1, r1, b1)
        part_sums(0, pg_back, b1)

    def combine_back():
        gather_back(3, r2, b2)
        part_sums(1, p_back, b2)

    def cb_copy(m, q, ss, dev, rep):
        piece = cb.at[tokens(m), cols_of(q)]
        return remote(piece, piece, ss, cb_rs.at[m, q], dev, rep)

    def share_start():
        for q in range(4):
            cb[tokens(mine), cols_of(q)] = part_total(0, q)
            for d in (1, 3, 2):
                _, rep, dev = ring_at(d)
                cb_copy(mine, q, cb_ss.at[d, q], dev, rep).start()
            cb_copy(mine, q, cb_ss.at[0, q], sibling, dp).start()

    def share_pass():
        for q in range(4):
            for d in (1, 3, 2):
                m = c * 4 + (ring + d) % 4
                cb_copy(m, q, cb_ss.at[d, q], me, dp).wait_recv()
                cb_copy(m, q, cf_ss.at[d, q], sibling, dp).start()

    def gy(d, q):
        py, to = along_y(d)
        cols = cols_of(q)
        src, dst = gwp.at[tokens(py), cols], gwy.at[tokens(y), cols]
        return py, remote(src, dst, gy_ss.at[d, q], gy_rs.at[y, q], to)

    def far_cols(q):
        return pl.ds(q * 256 - 512, 256)

    def gb(py, q):
        to = index_of(y, z, far_source(py), c)
        src, dst = gwp.at[tokens(py), cols_of(q)], gwb.at[py // 2, tokens(x), far_cols(q)]
        return to, remote(src, dst, gb_ss.at[py, q - 2], gb_rs.at[py // 2, x, q - 2], to)

    def weight_grad():
        for q in range(4):
            for d in range(4):
                m = (1 - c) * 4 + (ring + d) % 4
                cb_copy(m, q, cb_ss.at[d, q], me, dp).wait_recv()
            cols = cols_of(q)
            gwp[:, cols] = dot(go[...], cb[:, cols], 0, 0).astype(BF)
            if q < 2:
                for d in (1, 3, 2):
                    gy(d, q)[1].start()
                gwy[tokens(y), cols] = gwp[tokens(y), cols]
            else:
                for py in range(4):
                    to, copy = gb(py, q)

                    @pl.when(to != me)
                    def _():
                        copy.start()

                    @pl.when(to == me)
                    def _():
                        gwb[py // 2, tokens(x), far_cols(q)] = gwp[tokens(py), cols]

    def mix_all():
        def mix(part, carry):
            cols = tokens(part)
            mps[:, cols] = dot(cb[...], wj[cols, :], 1, 1).astype(BF)
            for n, (dc, dz) in enumerate(others):
                m, rep, to = member(dc, dz)
                src, dst = mps.at[tokens(m), cols], mixed.at[:, feats(mine, part)]
                remote(src, dst, mx_ss.at[n], mx_rs.at[mine], to, rep).start()
            mixed[:, feats(mine, part)] = mps[tokens(mine), cols]
            return carry

        lax.fori_loop(0, 4, mix, 0)

    up_copy.wait()
    down_copy.wait()
    gc_sibling()
    gc_ring()
    forward(0)
    forward(1)
    forward(2)
    gc_swap()
    forward(3)
    gc_dispatch()
    combine()
    backward(0)
    share_start()
    backward(1)
    backward(2)
    backward(3)
    share_pass()
    weight_grad()
    mix_all()
    combine_back()

    for q in range(2):
        for d in (1, 3, 2):
            py, _ = along_y(d)
            piece = gwy.at[tokens(py), cols_of(q)]
            remote(piece, piece, gy_ss.at[d, q], gy_rs.at[py, q], me).wait_recv()
    gws[...] = sum(gwy[n * 128 : (n + 1) * 128, 0:512].astype(F32) for n in range(4)).astype(BF)
    x_slot = rows_at(x * 64, 64)

    def gx(cc):
        to = index_of(y, z, x_own, cc)
        return to, remote(gws.at[pl.ds(cc * 64, 64)], gwx.at[x_slot], gx_ss.at[cc], gx_rs.at[x], to)

    for cc in range(2):
        to, copy = gx(cc)

        @pl.when(to != me)
        def _():
            copy.start()

        @pl.when(to == me)
        def _():
            gwx[x_slot, :] = gws[cc * 64 : cc * 64 + 64, :]

    def gby(n, cc):
        to = index_of(own_y(n), z, x, cc)
        src = gwbs.at[n, pl.ds(cc * 64, 64)]
        return to, remote(src, gwby.at[rows_at(y * 64, 64)], gby_ss.at[n, cc], gby_rs.at[y], to)

    @pl.when(c == half)
    def _():
        for n in range(2):
            for px in range(4):

                @pl.when(x != px)
                def _():
                    for q in range(2):
                        piece = gwb.at[n, pl.ds(px * 128, 128), cols_of(q)]
                        remote(piece, piece, gb_ss.at[0, q], gb_rs.at[n, px, q], me).wait_recv()

            gwbs[n] = sum(gwb[n, px * 128 : px * 128 + 128, :].astype(F32) for px in range(4)).astype(BF)
            for cc in range(2):
                to, copy = gby(n, cc)

                @pl.when(to != me)
                def _():
                    copy.start()

                @pl.when(to == me)
                def _():
                    gwby[rows_at(y * 64, 64), :] = gwbs[n, cc * 64 : cc * 64 + 64, :]


    exchange = pltpu.make_async_remote_copy(
        dps, dpr, dp_sem.at[0], dp_sem.at[1], device_id=(1 - dp, me), device_id_type=MESH
    )

    @pl.when(sends_w)
    def _():
        for px in range(4):
            src = index_of(y, z, px, half)

            @pl.when(src != me)
            def _():
                rows = pl.ds(px * 64, 64)
                remote(gwx.at[rows], gwx.at[rows], gx_ss.at[0], gx_rs.at[px], me).wait_recv()

        for py in range(4):

            @pl.when(index_of(py, z, x, half) != me)
            def _():
                rows = pl.ds(py * 64, 64)
                remote(gwby.at[rows], gwby.at[rows], gby_ss.at[0, 0], gby_rs.at[py], me).wait_recv()

        dps[:, 0:512] = sum(gwx[n * 64 : (n + 1) * 64, :].astype(F32) for n in range(4)).astype(BF)
        dps[:, 512:1024] = sum(gwby[n * 64 : (n + 1) * 64, :].astype(F32) for n in range(4)).astype(BF)
        exchange.start()
        grad_w[...] = dps[...].astype(F32)

    for q in range(4):
        grad_latent[:, cols_of(q)] = part_total(1, q)

    @pl.when(sends_w)
    def _():
        exchange.wait_send()

    @pl.when(jnp.logical_not(sends_w))
    def _():
        exchange.wait_recv()
        grad_w[...] = dpr[...].astype(F32)

    for n, (dc, dz) in enumerate(others):
        m, _, _ = member(dc, dz)
        whole = remote(mps.at[tokens(m)], mps.at[tokens(m)], mx_ss.at[n], mx_rs.at[m], me)
        whole.wait_recv()
        whole.wait_send()
        remote(go.at[tokens(m)], go.at[tokens(m)], go_ss.at[n], go_rs.at[m], me).wait_send()
    for copy in swap + swap_gc + to_sibling:
        copy.wait_send()
    for d in range(4):
        for to, copy in (wx(d), wb(d)):

            @pl.when(jnp.logical_and(sends_w, to != me))
            def _():
                copy.wait_send()

        for q in range(2):
            to, copy = gb(d, q + 2)

            @pl.when(to != me)
            def _():
                copy.wait_send()

        for q in range(4):
            cb_copy(mine, q, cb_ss.at[d, q], me, dp).wait_send()
            if d:
                if q < 2:
                    gy(d, q)[1].wait_send()
                cb_copy(mine, q, cf_ss.at[d, q], me, dp).wait_send()
        if d:
            wy(d).wait_send()
            for q in range(4):
                pg_copy(d, q).wait_send()
                part_copy(0, d, q).wait_send()
                part_copy(1, d, q).wait_send()
    @pl.when(c == half)
    def _():
        for n in range(2):
            for d in (1, 2, 3):
                wbx(n, d).wait_send()
            for cc in range(2):
                to, copy = gby(n, cc)

                @pl.when(to != me)
                def _():
                    copy.wait_send()

    for cc in range(2):
        to, copy = gx(cc)

        @pl.when(to != me)
        def _():
            copy.wait_send()

    all_sent(0, s1, r1)
    all_sent(1, r1, b1)
    all_sent(2, s2, r2)
    all_sent(3, r2, b2)


def settle(mixed_in, latent_in, w_in, mixed, grad_latent, grad_w, sems):
    pairs = ((mixed_in, mixed), (latent_in, grad_latent), (w_in, grad_w))
    copies = [pltpu.make_async_copy(src, dst, sems.at[n]) for n, (src, dst) in enumerate(pairs)]
    for copy in copies:
        copy.start()
    for copy in copies:
        copy.wait()


def on_device(latent, routes, gates, grad_out, w_out_t, expert_up, expert_down):
    vm = pl.BlockSpec(memory_space=pltpu.VMEM)
    hbm = pl.BlockSpec(memory_space=pl.ANY)

    def dma(*shape):
        return pltpu.SemaphoreType.DMA(shape)

    def bf(*shape):
        return pltpu.VMEM(shape, BF)

    scratch = [bf(4, 256, 1280)] * 6 + [
        bf(1024, 2048), bf(2048, 1024), pltpu.VMEM((CHUNKS, ROWS, 2048), F32),
        bf(ROWS, 1024), pltpu.VMEM((ROWS, 1024), F32), bf(256, 1024),
        pltpu.VMEM((4, 8, 128), I32), pltpu.VMEM((4, 8, 128), F32), bf(512, 1024), bf(512, 1024),
        pltpu.VMEM((512, 1024), F32), bf(2, 4, 128, 1024), bf(2, 4, 128, 1024),
        bf(1024, 512), bf(512, 1024), bf(512, 1024), bf(512, 1024), bf(512, 1024), bf(512, 1024),
        bf(1024, 1024), bf(1024, 512), bf(512, 1024), bf(512, 512), bf(128, 512), bf(256, 512), bf(2, 512, 512), bf(2, 128, 512), bf(256, 512),
        bf(64, 1024), bf(64, 1024),
        pltpu.VMEM((4, 128, 128), F32), pltpu.VMEM((4, 128, 128), F32), bf(256, 256), bf(256, 256),
        bf(4, 320, 128), bf(4, 320, 256), bf(4, 128, 320), bf(4, 256, 320),
        dma(4), dma(4, 4), dma(3, 4), dma(3, 4), dma(2, 4, 4), dma(2, 4, 4), dma(4), dma(2), dma(4), dma(8), dma(2, 4), dma(4), dma(4), dma(4), dma(7), dma(8),
        dma(4), dma(4), dma(4, 4), dma(4, 4), dma(4, 4), dma(4, 4), dma(4, 4), dma(8, 4), dma(4, 4), dma(7), dma(8),
        dma(4, 4), dma(4, 4), dma(4, 2), dma(2, 4, 2), dma(2, 2), dma(4), dma(2), dma(4), dma(2), dma(6),
    ]
    shapes = (
        jax.ShapeDtypeStruct((128, 4096), BF),
        jax.ShapeDtypeStruct((128, 1024), BF),
        jax.ShapeDtypeStruct((64, 1024), F32),
    )
    results = pl.pallas_call(
        kernel,
        out_shape=shapes,
        in_specs=[vm, vm, vm, vm, hbm, hbm, hbm],
        out_specs=(vm, vm, vm),
        scratch_shapes=scratch,
        compiler_params=pltpu.CompilerParams(
            collective_id=0, has_side_effects=True, vmem_limit_bytes=63 * 1024 * 1024
        ),
        cost_estimate=pl.CostEstimate(flops=25_000_000_000, bytes_accessed=20_000_000, transcendentals=0),
        name="moe_layer",
    )(latent, routes.T, gates.T, w_out_t, grad_out, expert_up, expert_down)
    return pl.pallas_call(
        settle,
        out_shape=shapes,
        in_specs=[vm] * 3,
        out_specs=(hbm,) * 3,
        scratch_shapes=[dma(3)],
        name="settle",
    )(*results)


def solution(mesh):
    rows = P(("dp", "expert"), None)
    return jax.shard_map(
        on_device,
        mesh=mesh,
        in_specs=(rows, rows, rows, rows, P("expert", None), P("expert", None, None), P("expert", None, None)),
        out_specs=(rows, rows, P("expert", None)),
        check_vma=False,
    )
```

```python
import jax
import jax.numpy as jnp
from jax import lax
from jax.experimental import pallas as pl
from jax.experimental.pallas import tpu as pltpu
from jax.sharding import PartitionSpec as P

BF = jnp.bfloat16
F32 = jnp.float32
I32 = jnp.int32
MESH = pl.DeviceIdType.MESH
STRIDE = 5
CHUNKS = 4
PER = 4
MAIN = 256
EXTRA = 64
ROWS = 320


def iota(shape, dim):
    return lax.broadcasted_iota(I32, shape, dim)


def dot(a, b, ca=1, cb=0):
    return lax.dot_general(a, b, (((ca,), (cb,)), ((), ())), preferred_element_type=F32)


def index_of(y, z, x, c):
    return ((y * 2 + z) * 4 + x) * 2 + c


def rows_at(start, size):
    return pl.ds(pl.multiple_of(start, size), size)


def kernel(
    latent, routes, gates, w_own, grad_out, up_hbm, down_hbm,
    mixed, grad_latent, grad_w,
    s1, r1, b1, s2, r2, b2, up, down, relu, xc, acc, extra,
    routes4, gates4, latent4, gc4, part_f, part_s, part_r,
    go, wj, pga, pgb, pgs, pgr, cb, mps, gwp, gwy, gws, gwx, gwb, gwbs, gwby, dps, dpr,
    slots, gate_tab, sel, selt, p_send, pg_send, p_back, pg_back,
    a2a_ss, a2a_rs, grp_ss, grp_rs, sw_ss, sw_rs, wx_ss, wx_rs, wb_ss, wb_rs, wbx_ss, wbx_rs, wy_ss, wy_rs, go_ss, go_rs,
    sib_ss, sib_rs, bgc_ss, bgc_rs, pg_ss, pg_rs, cb_ss, cb_rs, cf_ss, mx_ss, mx_rs,
    gy_ss, gy_rs, gb_ss, gb_rs, gby_ss, gby_rs, gx_ss, gx_rs, dp_sem, loc,
):
    dp = lax.axis_index("dp")
    me = lax.axis_index("expert")
    y, z, x, c = me // 16, (me // 8) % 2, (me // 2) % 4, me % 2
    ring = dp * 2 + z
    mine = c * 4 + ring
    sibling = index_of(y, z, x, 1 - c)
    block = x * (1 - c) + y * c
    half, parity = x // 2, x % 2

    def partner(k, sign):
        off = (STRIDE * k) % 16
        along, hop, flip = off // 4, (off // 2) % 2, off % 2
        pc = (c + flip) % 2
        sender, expert = (c, pc) if sign > 0 else (pc, c)
        pr = (ring + sign * hop * (1 - 2 * expert) + 4) % 4
        py, px = (y + sign * along * (1 - sender) + 4) % 4, (x + sign * along * sender + 4) % 4
        return pr // 2, index_of(py, pr % 2, px, pc)

    def group_at(d):
        to = (block + d) % 4
        return to, index_of(y + c * (to - y), z, x + (1 - c) * (to - x), c)

    def ring_at(d):
        to = (ring + d) % 4
        return to, to // 2, index_of(y, to % 2, x, c)

    def member(dc, dz):
        to, cc = (ring + dz) % 4, (c + dc) % 2
        return cc * 4 + to, to // 2, index_of(y, to % 2, x, cc)

    others = [(dc, dz) for dz in (1, 3, 2, 0) for dc in (0, 1) if dc or dz]

    def remote(src, dst, ss, rs, dev, rep=None):
        rep = dp if rep is None else rep
        return pltpu.make_async_remote_copy(src, dst, ss, rs, device_id=(rep, dev), device_id_type=MESH)

    barrier = pltpu.get_barrier_semaphore()

    def signal(rep, dev):
        pl.semaphore_signal(barrier, inc=1, device_id=(rep, dev), device_id_type=MESH)

    def greet(k, carry):
        for sign in (1, -1):
            signal(*partner(k, sign))
        return carry

    lax.fori_loop(1, 16, greet, 0)
    for dc, dz in others:
        _, rep, to = member(dc, dz)
        signal(rep, to)
    for d in range(1, 8):
        near = (x * 2 + c + d) % 8
        signal(dp, index_of(y, z, near // 2, near % 2))
    for d in range(1, 4):
        for cc in range(2):
            signal(dp, index_of((y + d) % 4, z, x, cc))
    up_copy = pltpu.make_async_copy(up_hbm.at[0], up, loc.at[0])
    down_copy = pltpu.make_async_copy(down_hbm.at[0], down, loc.at[1])
    up_copy.start()
    down_copy.start()
    own_tokens = rows_at(block * 128, 128)
    routes4[block] = routes[...]
    gates4[block] = gates[...]
    latent4[own_tokens, :] = latent[...]

    i, j = iota((256, 256), 0), iota((256, 256), 1)
    sel[...] = jnp.where(((i & 63) >> 2) * 16 + (i >> 6) * 4 + (i & 3) == j, 1.0, 0.0).astype(BF)
    selt[...] = jnp.where(((j & 63) >> 2) * 16 + (j >> 6) * 4 + (j & 3) == i, 1.0, 0.0).astype(BF)

    pl.semaphore_wait(barrier, 50)

    sends_w = parity == (y + dp) % 2
    w_slot = rows_at(y * 128 + c * 64, 64)

    near_half, far_half = pl.ds(0, 512), pl.ds(512, 512)

    def wx(d):
        to = index_of(y, z, (x + d) % 4, half)
        return to, remote(w_own.at[:, near_half], wj.at[w_slot, near_half], wx_ss.at[d], wx_rs.at[c], to)

    def wb(d):
        to = index_of((y + d) % 4, z, x, half)
        return to, remote(w_own.at[:, far_half], wj.at[w_slot, far_half], wb_ss.at[d], wb_rs.at[y * 2 + c], to)

    for d in (1, 3, 2, 0):
        for to, copy in (wx(d), wb(d)):

            @pl.when(jnp.logical_and(sends_w, to != me))
            def _():
                copy.start()

    @pl.when(jnp.logical_and(sends_w, c == half))
    def _():
        wj[w_slot, :] = w_own[...]

    swap = []
    for d in (1, 3, 2):
        _, to = group_at(d)
        swap.append(remote(routes, routes4.at[block], grp_ss.at[0, d], grp_rs.at[0, block], to))
        swap.append(remote(gates, gates4.at[block], grp_ss.at[1, d], grp_rs.at[1, block], to))
    for d in (1, 3, 2):
        _, to = group_at(d)
        swap.append(remote(latent, latent4.at[own_tokens], grp_ss.at[2, d], grp_rs.at[2, block], to))
    for copy in swap:
        copy.start()

    def from_group(n, dst):
        for d in (1, 3, 2):
            g, _ = group_at(d)
            remote(dst(g), dst(g), grp_ss.at[n, d], grp_rs.at[n, g], me).wait_recv()

    def feats(m, part):
        to = m % 4
        return rows_at(part * 1024 + (to % 2) * 512 + (m // 4) * 256 + ((part + to // 2) % 2) * 128, 128)

    def tokens(m):
        return rows_at(m * 128, 128)

    own_go = []
    for part in range(4):
        cols = pl.ds(part * 128, 128)
        for n, (dc, dz) in enumerate(others):
            m, rep, to = member(dc, dz)
            remote(grad_out.at[:, feats(m, part)], go.at[tokens(mine), cols], go_ss.at[n], go_rs.at[mine], to, rep).start()
        copy = pltpu.make_async_copy(grad_out.at[:, feats(mine, part)], go.at[tokens(mine), cols], loc.at[2 + part])
        copy.start()
        own_go.append(copy)

    from_group(0, lambda g: routes4.at[g])
    from_group(1, lambda g: gates4.at[g])

    def names(j):
        return jnp.where(j < 256, j >> 4, (j - 256) >> 2), jnp.where(j < 256, j & 15, 16 + (j & 3)) + 1

    def expert_of(k):
        off = (STRIDE * k) & 15
        along, hop, pc = off >> 2, (off >> 1) & 1, (c + off) & 1
        py, px = (y + along * (1 - c)) & 3, (x + along * c) & 3
        return ((py * 2 + ((z + hop) & 1)) * 4 + px) * 2 + pc

    k_row, s_row = names(iota((320, 128), 0))
    k_col, s_col = names(iota((128, 320), 1))
    spread_t = jnp.where(expert_of(k_row) == iota((320, 128), 1), 1.0, 0.0).astype(BF)
    spread = jnp.where(expert_of(k_col) == iota((128, 320), 0), 1.0, 0.0).astype(BF)
    earlier = jnp.where(iota((128, 128), 0) < iota((128, 128), 1), 1.0, 0.0).astype(BF)

    def table(g):
        hot = jnp.zeros((128, 128), F32)
        gate = jnp.zeros((128, 128), F32)
        for k in range(8):
            hit = routes4[g, k : k + 1, :] == iota((128, 128), 0)
            hot = hot + jnp.where(hit, 1.0, 0.0)
            gate = gate + jnp.where(hit, gates4[g, k : k + 1, :], 0.0)
        slot = jnp.where(hot > 0.5, dot(hot.astype(BF), earlier) + 1.0, 0.0)
        return slot, gate

    for g in range(4):
        slots[g], gate_tab[g] = table(g)
        hit = dot(spread_t, slots[g].astype(BF)) == s_row.astype(F32)
        p_send[g] = jnp.where(hit, 1.0, 0.0).astype(BF)

    def routing_rest():
        for g in range(4):
            gate_hi = gate_tab[g].astype(BF).astype(F32)
            gate_lo = gate_tab[g] - gate_hi
            hit = p_send[g].astype(F32) > 0.5
            pg_send[g, :, 0:128] = jnp.where(hit, dot(spread_t, gate_hi.astype(BF)), 0.0).astype(BF)
            pg_send[g, :, 128:256] = jnp.where(hit, dot(spread_t, gate_lo.astype(BF)), 0.0).astype(BF)
            hit = dot(slots[g].T.astype(BF), spread) == s_col.astype(F32)
            p_back[g] = jnp.where(hit, 1.0, 0.0).astype(BF)
            pg_back[g, 0:128, :] = jnp.where(hit, dot(gate_hi.T.astype(BF), spread), 0.0).astype(BF)
            pg_back[g, 128:256, :] = jnp.where(hit, dot(gate_lo.T.astype(BF), spread), 0.0).astype(BF)

    def unpack(packed):
        rows = dot(sel[...], packed).astype(BF)
        return jnp.concatenate([rows[q * 64 : (q + 1) * 64] for q in range(4)], axis=1)

    def pack(rows):
        stacked = jnp.concatenate([rows[:, q * 256 : (q + 1) * 256] for q in range(4)], axis=0)
        return dot(selt[...], stacked).astype(BF)

    def message(k):
        return rows_at(k * 16, 16)

    def start(which, src, dst, ci, sign):
        def body(k, carry):
            rep, to = partner(k, sign)
            piece = (slice(None), message(k))
            remote(src.at[piece], dst.at[piece], a2a_ss.at[which], a2a_rs.at[which, ci], to, rep).start()
            return carry

        lax.fori_loop(max(ci * PER, 1), ci * PER + PER, body, 0)
        if ci == 0:
            dst[:, 0:16, :] = src[:, 0:16, :]

    def dispatch(which, pick, source, src, dst):
        for g in range(4):
            values = source[g * 128 : g * 128 + 128, :]
            if pick.shape[2] == 256:
                values = jnp.concatenate([values, values], axis=0)
            src[g, :, 0:1024] = dot(pick[g, 0:256, :], values).astype(BF)
            src[g, :, 1024:1280] = pack(dot(pick[g, 256:320, :], values).astype(BF))
        for ci in range(CHUNKS):
            start(which, src, dst, ci, 1)

    def arrived(which, ci, src, dst):
        rows = (slice(None), pl.ds(0, 48) if ci == 0 else pl.ds(ci * 64, 64))
        remote(src.at[rows], dst.at[rows], a2a_ss.at[which], a2a_rs.at[which, ci], me).wait_recv()

    def all_sent(which, src, dst):
        rows = (slice(None), pl.ds(0, 240))
        remote(src.at[rows], dst.at[rows], a2a_ss.at[which], a2a_rs.at[which, 0], me).wait_send()

    x_own = c * 2 + (y + dp) % 2
    for cc in range(2):
        src = index_of(y, z, x_own, cc)

        @pl.when(src != me)
        def _():
            piece = wj.at[rows_at(y * 128 + cc * 64, 64), near_half]
            remote(piece, piece, wx_ss.at[0], wx_rs.at[cc], me).wait_recv()

    def along_y(d):
        py = (y + d) % 4
        return py, index_of(py, z, x, c)

    def wy(d):
        _, to = along_y(d)
        piece = wj.at[tokens(y), near_half]
        return remote(piece, piece, wy_ss.at[d], wy_rs.at[y], to)

    for d in (1, 3, 2):
        wy(d).start()

    def own_y(n):
        return (x + dp) % 2 + 2 * n

    def wbx(n, d):
        py = own_y(n)
        piece = wj.at[tokens(py), far_half]
        return remote(piece, piece, wbx_ss.at[n, d], wbx_rs.at[py], index_of(y, z, (x + d) % 4, c))

    def far_source(py):
        return 2 * c + (py + dp) % 2

    @pl.when(c == half)
    def _():
        for n in range(2):
            py = own_y(n)
            for cc in range(2):

                @pl.when(index_of(py, z, x, cc) != me)
                def _():
                    piece = wj.at[rows_at(py * 128 + cc * 64, 64), far_half]
                    remote(piece, piece, wb_ss.at[0], wb_rs.at[py * 2 + cc], me).wait_recv()

            for d in (1, 3, 2):
                wbx(n, d).start()

    from_group(2, lambda g: latent4.at[rows_at(g * 128, 128)])
    dispatch(0, p_send, latent4, s1, r1)
    routing_rest()

    def quarter(n):
        return rows_at(n * 256, 256)

    def core_rows(cc):
        return rows_at(cc * 512, 512)

    def cols_of(q):
        return pl.ds(q * 256, 256)

    to_sibling = []
    swap_gc = []
    for q in range(4):
        cols = cols_of(q)
        to_sibling.append(remote(pga.at[:, cols], pgb.at[:, cols], sib_ss.at[q], sib_rs.at[q], sibling))
        for d in (1, 3, 2):
            piece = gc4.at[own_tokens, cols]
            swap_gc.append(remote(piece, piece, bgc_ss.at[d, q], bgc_rs.at[block, q], group_at(d)[1]))

    def load(src, ci):
        rows = pl.ds(ci * 64, 64)
        for g in range(4):
            xc[g * 64 : g * 64 + 64, :] = src[g, rows, 0:1024]
        xc[MAIN:ROWS, :] = unpack(jnp.concatenate([src[g, rows, 1024:1280] for g in range(4)], axis=0))

    def store(dst, ci):
        rows = pl.ds(ci * 64, 64)
        more = pack(acc[MAIN:ROWS, :].astype(BF))
        for g in range(4):
            dst[g, rows, 0:1024] = acc[g * 64 : g * 64 + 64, :].astype(BF)
            dst[g, rows, 1024:1280] = more[g * 64 : g * 64 + 64, :]

    def hidden(h):
        return rows_at(h * 512, 512)

    def forward(ci):
        arrived(0, ci, s1, r1)
        load(r1, ci)
        acc[...] = jnp.zeros_like(acc)

        def step(h, inner):
            pos = jnp.maximum(dot(xc[...], up[:, hidden(h)]), 0.0)
            relu[ci, :, hidden(h)] = pos
            acc[...] += dot((pos * pos).astype(BF), down[hidden(h), :])
            return inner

        lax.fori_loop(0, 4, step, 0)
        store(r1, ci)
        start(1, r1, b1, ci, -1)

    def backward(ci):
        arrived(2, ci, s2, r2)
        load(r2, ci)
        acc[...] = jnp.zeros_like(acc)

        def step(h, inner):
            grad = dot(xc[...], down[hidden(h), :], 1, 1) * 2.0 * relu[ci, :, hidden(h)]
            acc[...] += dot(grad.astype(BF), up[:, hidden(h)], 1, 1)
            return inner

        lax.fori_loop(0, 4, step, 0)
        store(r2, ci)
        start(3, r2, b2, ci, -1)

    def gc_sibling():
        for d in (1, 3, 2):
            py, _ = along_y(d)
            piece = wj.at[tokens(py), near_half]
            remote(piece, piece, wy_ss.at[d], wy_rs.at[py], me).wait_recv()
        for py in range(4):

            @pl.when(x != far_source(py))
            def _():
                piece = wj.at[tokens(py), far_half]
                remote(piece, piece, wbx_ss.at[0, 1], wbx_rs.at[py], me).wait_recv()

        for copy in own_go:
            copy.wait()
        for n, (dc, dz) in enumerate(others):
            m, _, _ = member(dc, dz)
            remote(go.at[tokens(m)], go.at[tokens(m)], go_ss.at[n], go_rs.at[m], me).wait_recv()
        for q in range(4):
            pga[:, cols_of(q)] = dot(go[core_rows(1 - c), :], wj[:, cols_of(q)]).astype(BF)
            to_sibling[q].start()

    def pg_copy(d, q):
        to, rep, dev = ring_at(d)
        cols = cols_of(q)
        src, dst = pgs.at[tokens(to), cols], pgr.at[tokens(ring), cols]
        return remote(src, dst, pg_ss.at[d, q], pg_rs.at[ring, q], dev, rep)

    def gc_ring():
        for q in range(4):
            cols = cols_of(q)
            to_sibling[q].wait_recv()
            pgs[:, cols] = (dot(go[core_rows(c), :], wj[:, cols]) + pgb[:, cols].astype(F32)).astype(BF)
            for d in (1, 3, 2):
                pg_copy(d, q).start()
            pgr[tokens(ring), cols] = pgs[tokens(ring), cols]

    def gc_swap():
        for q in range(4):
            cols = cols_of(q)
            for d in (1, 3, 2):
                to, _, _ = ring_at(d)
                piece = pgr.at[tokens(to), cols]
                remote(piece, piece, pg_ss.at[d, q], pg_rs.at[to, q], me).wait_recv()
            gc = sum(pgr[n * 128 : (n + 1) * 128, cols].astype(F32) for n in range(4)).astype(BF)
            gc4[own_tokens, cols] = gc
            for n in range(3):
                swap_gc[q * 3 + n].start()

    def gc_dispatch():
        for q in range(4):
            for d in (1, 3, 2):
                g, _ = group_at(d)
                piece = gc4.at[rows_at(g * 128, 128), cols_of(q)]
                remote(piece, piece, bgc_ss.at[d, q], bgc_rs.at[g, q], me).wait_recv()
        dispatch(2, pg_send, gc4, s2, r2)

    def gather_back(which, src, dst):
        for ci in range(CHUNKS):
            arrived(which, ci, src, dst)

        for g in range(4):
            extra[g * EXTRA : g * EXTRA + EXTRA, :] = unpack(dst[g, :, 1024:1280])

    def part_copy(n, d, q):
        g, to = group_at(d)
        cols = cols_of(q)
        src, dst = part_s.at[n, g, :, cols], part_r.at[n, block, :, cols]
        return remote(src, dst, sw_ss.at[n, d, q], sw_rs.at[n, block, q], to)

    def part_sums(n, weights, src):
        for q in range(4):
            cols = cols_of(q)
            for g in range(4):
                both = dot(weights[g, :, 0:256], src[g, :, cols])
                both = both + dot(weights[g, :, 256:320], extra[g * EXTRA : g * EXTRA + EXTRA, cols])
                if weights.shape[1] == 256:
                    both = both[0:128] + both[128:256]
                part_f[g * 128 : g * 128 + 128, cols] = both
                part_s[n, g, :, cols] = both.astype(BF)
            for d in (1, 3, 2):
                part_copy(n, d, q).start()

    def part_total(n, q):
        cols = cols_of(q)
        total = part_f[own_tokens, cols]
        for d in (1, 3, 2):
            g, _ = group_at(d)
            piece = part_r.at[n, g, :, cols]
            remote(piece, piece, sw_ss.at[n, d, q], sw_rs.at[n, g, q], me).wait_recv()
        for d in (1, 3, 2):
            g, _ = group_at(d)
            total = total + part_r[n, g, :, cols].astype(F32)
        return total.astype(BF)

    def combine():
        gather_back(1, r1, b1)
        part_sums(0, pg_back, b1)

    def combine_back():
        gather_back(3, r2, b2)
        part_sums(1, p_back, b2)

    def cb_copy(m, q, ss, dev, rep):
        piece = cb.at[tokens(m), cols_of(q)]
        return remote(piece, piece, ss, cb_rs.at[m, q], dev, rep)

    def share_start():
        for q in range(4):
            cb[tokens(mine), cols_of(q)] = part_total(0, q)
            for d in (1, 3, 2):
                _, rep, dev = ring_at(d)
                cb_copy(mine, q, cb_ss.at[d, q], dev, rep).start()
            cb_copy(mine, q, cb_ss.at[0, q], sibling, dp).start()

    def share_pass():
        for q in range(4):
            for d in (1, 3, 2):
                m = c * 4 + (ring + d) % 4
                cb_copy(m, q, cb_ss.at[d, q], me, dp).wait_recv()
                cb_copy(m, q, cf_ss.at[d, q], sibling, dp).start()

    def gy(d, q):
        py, to = along_y(d)
        cols = cols_of(q)
        src, dst = gwp.at[tokens(py), cols], gwy.at[tokens(y), cols]
        return py, remote(src, dst, gy_ss.at[d, q], gy_rs.at[y, q], to)

    def far_cols(q):
        return pl.ds(q * 256 - 512, 256)

    def gb(py, q):
        to = index_of(y, z, far_source(py), c)
        src, dst = gwp.at[tokens(py), cols_of(q)], gwb.at[py // 2, tokens(x), far_cols(q)]
        return to, remote(src, dst, gb_ss.at[py, q - 2], gb_rs.at[py // 2, x, q - 2], to)

    def weight_grad():
        for q in range(4):
            for d in range(4):
                m = (1 - c) * 4 + (ring + d) % 4
                cb_copy(m, q, cb_ss.at[d, q], me, dp).wait_recv()
            cols = cols_of(q)
            gwp[:, cols] = dot(go[...], cb[:, cols], 0, 0).astype(BF)
            if q < 2:
                for d in (1, 3, 2):
                    gy(d, q)[1].start()
                gwy[tokens(y), cols] = gwp[tokens(y), cols]
            else:
                for py in range(4):
                    to, copy = gb(py, q)

                    @pl.when(to != me)
                    def _():
                        copy.start()

                    @pl.when(to == me)
                    def _():
                        gwb[py // 2, tokens(x), far_cols(q)] = gwp[tokens(py), cols]

    def mix_all():
        def mix(part, carry):
            cols = tokens(part)
            mps[:, cols] = dot(cb[...], wj[cols, :], 1, 1).astype(BF)
            for n, (dc, dz) in enumerate(others):
                m, rep, to = member(dc, dz)
                src, dst = mps.at[tokens(m), cols], mixed.at[:, feats(mine, part)]
                remote(src, dst, mx_ss.at[n], mx_rs.at[mine], to, rep).start()
            mixed[:, feats(mine, part)] = mps[tokens(mine), cols]
            return carry

        lax.fori_loop(0, 4, mix, 0)

    up_copy.wait()
    down_copy.wait()
    gc_sibling()
    gc_ring()
    forward(0)
    forward(1)
    forward(2)
    gc_swap()
    forward(3)
    gc_dispatch()
    combine()
    backward(0)
    share_start()
    backward(1)
    backward(2)
    backward(3)
    share_pass()
    weight_grad()
    mix_all()
    combine_back()

    for q in range(2):
        for d in (1, 3, 2):
            py, _ = along_y(d)
            piece = gwy.at[tokens(py), cols_of(q)]
            remote(piece, piece, gy_ss.at[d, q], gy_rs.at[py, q], me).wait_recv()
    gws[...] = sum(gwy[n * 128 : (n + 1) * 128, 0:512].astype(F32) for n in range(4)).astype(BF)
    x_slot = rows_at(x * 64, 64)

    def gx(cc):
        to = index_of(y, z, x_own, cc)
        return to, remote(gws.at[pl.ds(cc * 64, 64)], gwx.at[x_slot], gx_ss.at[cc], gx_rs.at[x], to)

    for cc in range(2):
        to, copy = gx(cc)

        @pl.when(to != me)
        def _():
            copy.start()

        @pl.when(to == me)
        def _():
            gwx[x_slot, :] = gws[cc * 64 : cc * 64 + 64, :]

    def gby(n, cc):
        to = index_of(own_y(n), z, x, cc)
        src = gwbs.at[n, pl.ds(cc * 64, 64)]
        return to, remote(src, gwby.at[rows_at(y * 64, 64)], gby_ss.at[n, cc], gby_rs.at[y], to)

    @pl.when(c == half)
    def _():
        for n in range(2):
            for px in range(4):

                @pl.when(x != px)
                def _():
                    for q in range(2):
                        piece = gwb.at[n, pl.ds(px * 128, 128), cols_of(q)]
                        remote(piece, piece, gb_ss.at[0, q], gb_rs.at[n, px, q], me).wait_recv()

            gwbs[n] = sum(gwb[n, px * 128 : px * 128 + 128, :].astype(F32) for px in range(4)).astype(BF)
            for cc in range(2):
                to, copy = gby(n, cc)

                @pl.when(to != me)
                def _():
                    copy.start()

                @pl.when(to == me)
                def _():
                    gwby[rows_at(y * 64, 64), :] = gwbs[n, cc * 64 : cc * 64 + 64, :]


    exchange = []
    for n, cols in enumerate((near_half, far_half)):
        src, dst = dps.at[:, cols], dpr.at[:, cols]
        exchange.append(remote(src, dst, dp_sem.at[n], dp_sem.at[2 + n], me, 1 - dp))

    @pl.when(sends_w)
    def _():
        for px in range(4):
            src = index_of(y, z, px, half)

            @pl.when(src != me)
            def _():
                rows = pl.ds(px * 64, 64)
                remote(gwx.at[rows], gwx.at[rows], gx_ss.at[0], gx_rs.at[px], me).wait_recv()

        dps[:, 0:512] = sum(gwx[n * 64 : (n + 1) * 64, :].astype(F32) for n in range(4)).astype(BF)
        exchange[0].start()
        for py in range(4):

            @pl.when(index_of(py, z, x, half) != me)
            def _():
                rows = pl.ds(py * 64, 64)
                remote(gwby.at[rows], gwby.at[rows], gby_ss.at[0, 0], gby_rs.at[py], me).wait_recv()

        dps[:, 512:1024] = sum(gwby[n * 64 : (n + 1) * 64, :].astype(F32) for n in range(4)).astype(BF)
        exchange[1].start()
        grad_w[...] = dps[...].astype(F32)

    for q in range(4):
        grad_latent[:, cols_of(q)] = part_total(1, q)

    @pl.when(sends_w)
    def _():
        for copy in exchange:
            copy.wait_send()

    @pl.when(jnp.logical_not(sends_w))
    def _():
        for copy in exchange:
            copy.wait_recv()
        grad_w[...] = dpr[...].astype(F32)

    for n, (dc, dz) in enumerate(others):
        m, _, _ = member(dc, dz)
        whole = remote(mps.at[tokens(m)], mps.at[tokens(m)], mx_ss.at[n], mx_rs.at[m], me)
        whole.wait_recv()
        whole.wait_send()
        remote(go.at[tokens(m)], go.at[tokens(m)], go_ss.at[n], go_rs.at[m], me).wait_send()
    for copy in swap + swap_gc + to_sibling:
        copy.wait_send()
    for d in range(4):
        for to, copy in (wx(d), wb(d)):

            @pl.when(jnp.logical_and(sends_w, to != me))
            def _():
                copy.wait_send()

        for q in range(2):
            to, copy = gb(d, q + 2)

            @pl.when(to != me)
            def _():
                copy.wait_send()

        for q in range(4):
            cb_copy(mine, q, cb_ss.at[d, q], me, dp).wait_send()
            if d:
                if q < 2:
                    gy(d, q)[1].wait_send()
                cb_copy(mine, q, cf_ss.at[d, q], me, dp).wait_send()
        if d:
            wy(d).wait_send()
            for q in range(4):
                pg_copy(d, q).wait_send()
                part_copy(0, d, q).wait_send()
                part_copy(1, d, q).wait_send()
    @pl.when(c == half)
    def _():
        for n in range(2):
            for d in (1, 2, 3):
                wbx(n, d).wait_send()
            for cc in range(2):
                to, copy = gby(n, cc)

                @pl.when(to != me)
                def _():
                    copy.wait_send()

    for cc in range(2):
        to, copy = gx(cc)

        @pl.when(to != me)
        def _():
            copy.wait_send()

    all_sent(0, s1, r1)
    all_sent(1, r1, b1)
    all_sent(2, s2, r2)
    all_sent(3, r2, b2)


def settle(mixed_in, latent_in, w_in, mixed, grad_latent, grad_w, sems):
    pairs = ((mixed_in, mixed), (latent_in, grad_latent), (w_in, grad_w))
    copies = [pltpu.make_async_copy(src, dst, sems.at[n]) for n, (src, dst) in enumerate(pairs)]
    for copy in copies:
        copy.start()
    for copy in copies:
        copy.wait()


def on_device(latent, routes, gates, grad_out, w_out_t, expert_up, expert_down):
    vm = pl.BlockSpec(memory_space=pltpu.VMEM)
    hbm = pl.BlockSpec(memory_space=pl.ANY)

    def dma(*shape):
        return pltpu.SemaphoreType.DMA(shape)

    def bf(*shape):
        return pltpu.VMEM(shape, BF)

    scratch = [bf(4, 256, 1280)] * 6 + [
        bf(1024, 2048), bf(2048, 1024), pltpu.VMEM((CHUNKS, ROWS, 2048), F32),
        bf(ROWS, 1024), pltpu.VMEM((ROWS, 1024), F32), bf(256, 1024),
        pltpu.VMEM((4, 8, 128), I32), pltpu.VMEM((4, 8, 128), F32), bf(512, 1024), bf(512, 1024),
        pltpu.VMEM((512, 1024), F32), bf(2, 4, 128, 1024), bf(2, 4, 128, 1024),
        bf(1024, 512), bf(512, 1024), bf(512, 1024), bf(512, 1024), bf(512, 1024), bf(512, 1024),
        bf(1024, 1024), bf(1024, 512), bf(512, 1024), bf(512, 512), bf(128, 512), bf(256, 512), bf(2, 512, 512), bf(2, 128, 512), bf(256, 512),
        bf(64, 1024), bf(64, 1024),
        pltpu.VMEM((4, 128, 128), F32), pltpu.VMEM((4, 128, 128), F32), bf(256, 256), bf(256, 256),
        bf(4, 320, 128), bf(4, 320, 256), bf(4, 128, 320), bf(4, 256, 320),
        dma(4), dma(4, 4), dma(3, 4), dma(3, 4), dma(2, 4, 4), dma(2, 4, 4), dma(4), dma(2), dma(4), dma(8), dma(2, 4), dma(4), dma(4), dma(4), dma(7), dma(8),
        dma(4), dma(4), dma(4, 4), dma(4, 4), dma(4, 4), dma(4, 4), dma(4, 4), dma(8, 4), dma(4, 4), dma(7), dma(8),
        dma(4, 4), dma(4, 4), dma(4, 2), dma(2, 4, 2), dma(2, 2), dma(4), dma(2), dma(4), dma(4), dma(6),
    ]
    shapes = (
        jax.ShapeDtypeStruct((128, 4096), BF),
        jax.ShapeDtypeStruct((128, 1024), BF),
        jax.ShapeDtypeStruct((64, 1024), F32),
    )
    results = pl.pallas_call(
        kernel,
        out_shape=shapes,
        in_specs=[vm, vm, vm, vm, hbm, hbm, hbm],
        out_specs=(vm, vm, vm),
        scratch_shapes=scratch,
        compiler_params=pltpu.CompilerParams(
            collective_id=0, has_side_effects=True, vmem_limit_bytes=63 * 1024 * 1024
        ),
        cost_estimate=pl.CostEstimate(flops=25_000_000_000, bytes_accessed=20_000_000, transcendentals=0),
        name="moe_layer",
    )(latent, routes.T, gates.T, w_out_t, grad_out, expert_up, expert_down)
    return pl.pallas_call(
        settle,
        out_shape=shapes,
        in_specs=[vm] * 3,
        out_specs=(hbm,) * 3,
        scratch_shapes=[dma(3)],
        name="settle",
    )(*results)


def solution(mesh):
    rows = P(("dp", "expert"), None)
    return jax.shard_map(
        on_device,
        mesh=mesh,
        in_specs=(rows, rows, rows, rows, P("expert", None), P("expert", None, None), P("expert", None, None)),
        out_specs=(rows, rows, P("expert", None)),
        check_vma=False,
    )
```
